256 devices in a mesh: seq: 64 (over z, y, core), head: 4 (over x).
Axes of the slice: x: 4, y: 4, z: 8, core: 2. Of those that a mesh axis runs over, the one named last changes fastest.
Arguments:
- queries: bfloat16 [32768, 1024], P('seq', 'head'), may hold values from -5 to 5
- keys: bfloat16 [32768, 1024], P('seq', 'head'), may hold values from -5 to 5
- values: bfloat16 [32768, 1024], P('seq', 'head'), may hold values from -6 to 6
- out_weight: bfloat16 [1024, 1024], P(None, 'head'), may hold values from -0.1875 to 0.1875
- grad_out: bfloat16 [32768, 1024], P('seq', 'head'), may hold values from -16 to 16
Outputs:
- output: bfloat16 [32768, 1024], P('seq', 'head')
- grad_queries: bfloat16 [32768, 1024], P('seq', 'head')
- grad_keys: bfloat16 [32768, 1024], P('seq', 'head')
- grad_values: bfloat16 [32768, 1024], P('seq', 'head')
- grad_weight: float32 [1024, 1024], P('seq', 'head')
The draws below stay inside these ranges and needn't reach their ends.
All inputs are finite; a program needn't handle non-finite values.
Results may differ from the reference program's by a relative error of at most 0.019.
Values may be sent and summed in bfloat16 or wider, within the bound.
No kernel may reach another device: no remote copies, remote signals or barrier semaphores. Data moves between devices by JAX's collectives and lax.ppermute only.
A program may use at most 64 MiB of HBM per device.

```python
import math
import jax
import jax.numpy as jnp
from jax import lax

HEAD_DIM = 128
BLOCK = 128
TOK_DEV = 512
D = 1024
TOKENS = 32768
N_SEQ = 64


def draw_queries(key, part):
    key = jax.random.fold_in(key, 5)
    base = jax.random.normal(key, (TOKENS, D), jnp.float32)
    return jnp.clip(base, -5.0, 5.0).astype(jnp.bfloat16)


def draw_keys(key, part):
    key = jax.random.fold_in(key, 6)
    base = jax.random.normal(key, (TOKENS, D), jnp.float32)
    return jnp.clip(base, -5.0, 5.0).astype(jnp.bfloat16)


def spiked(values, own_key, source, target, parts, factor):
    def block_of(axis_at):
        return (jnp.arange(values.shape[axis_at]) // (values.shape[axis_at] // parts)).reshape((-1,) + (1,) * (values.ndim - 1 - axis_at))

    near = jax.random.permutation(own_key, parts)[block_of(target)]
    other_side = (block_of(target) + parts // 2) % parts
    return jnp.where((block_of(source) == near) | (block_of(source) == other_side), factor * values, values)


def level_of(stream_key, extent, cuts, smallest, largest):
    level, own = 1.0, jax.random.fold_in(stream_key, 6)
    for dim, shards_of in cuts:
        steps = jnp.exp(jax.random.uniform(jax.random.fold_in(own, dim), (shards_of,), jnp.float32, smallest / len(cuts), largest / len(cuts)))
        level = level * jnp.repeat(steps, extent[dim] // shards_of).reshape([-1 if axis == dim else 1 for axis in range(len(extent))])
    return level


def noise(rng, dims, scale, bound, shards=(), kind=jnp.bfloat16):
    values = jax.random.normal(rng, dims, jnp.float32) * scale
    if len(shards) > 0:
        values = level_of(rng, dims, shards, -0.22, 0.18) * values
    return jnp.clip(values, min=-bound, max=bound).astype(kind)


def noise_with(key, extent, deviation, reach, shards, heavy, kind=jnp.bfloat16):
    entries = deviation * jax.random.normal(key, extent, jnp.float32)
    if shards:
        entries = entries * level_of(key, extent, shards, -0.22, 0.18)
    return jnp.clip(spiked(entries, jax.random.fold_in(key, 3), *heavy), -reach, reach).astype(kind)


def setup_inputs(seed: int = 0) -> dict:
    seeds = jax.random.split(jax.random.key(seed), 6)
    queries = draw_queries(jax.random.fold_in(seeds[5], 71), 0)
    keys = draw_keys(jax.random.fold_in(seeds[5], 71), 0)
    values = noise(seeds[2], (TOKENS, D), 1.0, 6.0, ((0, 64), (1, 4)))
    out_weight = noise(seeds[3], (D, D), D ** -0.5, 0.1875, ((1, 4),))
    grad_out = noise_with(seeds[4], (TOKENS, D), 1.0, 16.0, ((0, 64), (1, 4)), (0, 1, 64, 4.0))
    return dict(queries=queries, keys=keys, values=values, out_weight=out_weight, grad_out=grad_out)


def key_sets(levels, nblocks):
    first_level, second_level, third_level = levels
    stacked = []
    for index in range(nblocks):
        half = index // 2
        quarter = index // 4
        stacked.append(jnp.concatenate([
            first_level[BLOCK * index:BLOCK * index + 3 * BLOCK],
            second_level[BLOCK * half:BLOCK * half + BLOCK],
            second_level[BLOCK * half + 2 * BLOCK:BLOCK * half + 3 * BLOCK],
            third_level[BLOCK * quarter:BLOCK * quarter + BLOCK],
            third_level[BLOCK * quarter + 2 * BLOCK:BLOCK * quarter + 3 * BLOCK]], axis=0))
    return jnp.stack(stacked)


def set_masks(first, total, nblocks):
    flags = []
    biases = []
    for index in range(nblocks):
        half = index // 2
        quarter = index // 4
        starts = [(first - BLOCK + BLOCK * index, 0, 3), (first // 2 - BLOCK + BLOCK * half, 1, 1),
                  (first // 2 + BLOCK + BLOCK * half, 1, 1), (first // 4 - BLOCK + BLOCK * quarter, 2, 1),
                  (first // 4 + BLOCK + BLOCK * quarter, 2, 1)]
        row_flags = []
        row_bias = []
        for begin, level, blocks in starts:
            where = begin + jnp.arange(blocks * BLOCK, dtype=jnp.int32)
            row_flags.append((where >= 0) & (where < total // (2 ** level)))
            row_bias.append(jnp.full((blocks * BLOCK,), level * math.log(2.0), jnp.float32))
        flags.append(jnp.concatenate(row_flags))
        biases.append(jnp.concatenate(row_bias))
    return jnp.stack(flags), jnp.stack(biases)


def weights_of(queries, key_set, flags, biases):
    nblocks = queries.shape[0] // BLOCK
    nheads = queries.shape[1] // HEAD_DIM
    query_blocks = queries.reshape(nblocks, BLOCK, nheads, HEAD_DIM).astype(jnp.float32)
    key_blocks = key_set.reshape(nblocks, -1, nheads, HEAD_DIM).astype(jnp.float32)
    scores = jnp.einsum('jqhe,jkhe->jhqk', query_blocks, key_blocks) * (HEAD_DIM ** -0.5)
    scores = scores + biases[:, None, None, :]
    scores = jnp.where(flags[:, None, None, :], scores, jnp.float32(-1e30))
    top = jnp.max(scores, axis=-1, keepdims=True)
    expd = jnp.exp(scores - top)
    return expd / jnp.sum(expd, axis=-1, keepdims=True)


def attend(queries, key_set, value_set, flags, biases):
    nblocks = queries.shape[0] // BLOCK
    nheads = queries.shape[1] // HEAD_DIM
    weight = weights_of(queries, key_set, flags, biases).astype(jnp.bfloat16)
    value_blocks = value_set.reshape(nblocks, -1, nheads, HEAD_DIM).astype(jnp.float32)
    result = jnp.einsum('jhqk,jkhe->jqhe', weight.astype(jnp.float32), value_blocks)
    return result.reshape(queries.shape).astype(jnp.bfloat16)


def attend_back(queries, key_set, value_set, flags, biases, grad_attn):
    nblocks = queries.shape[0] // BLOCK
    nheads = queries.shape[1] // HEAD_DIM
    weight = weights_of(queries, key_set, flags, biases)
    rounded = weight.astype(jnp.bfloat16).astype(jnp.float32)
    query_blocks = queries.reshape(nblocks, BLOCK, nheads, HEAD_DIM).astype(jnp.float32)
    key_blocks = key_set.reshape(nblocks, -1, nheads, HEAD_DIM).astype(jnp.float32)
    value_blocks = value_set.reshape(nblocks, -1, nheads, HEAD_DIM).astype(jnp.float32)
    grad_blocks = grad_attn.reshape(nblocks, BLOCK, nheads, HEAD_DIM).astype(jnp.float32)
    dprob = jnp.einsum('jqhe,jkhe->jhqk', grad_blocks, value_blocks)
    delta = jnp.sum(weight * dprob, axis=-1, keepdims=True)
    dscore = (weight * (dprob - delta)).astype(jnp.bfloat16).astype(jnp.float32)
    grad_q = jnp.einsum('jhqk,jkhe->jqhe', dscore, key_blocks) * (HEAD_DIM ** -0.5)
    grad_k = jnp.einsum('jhqk,jqhe->jkhe', dscore, query_blocks) * (HEAD_DIM ** -0.5)
    grad_v = jnp.einsum('jhqk,jqhe->jkhe', rounded, grad_blocks)
    members = jnp.concatenate([grad_k.reshape(nblocks, -1, nheads * HEAD_DIM),
                               grad_v.reshape(nblocks, -1, nheads * HEAD_DIM)], axis=-1)
    return grad_q.reshape(queries.shape).astype(jnp.bfloat16), members


def shifted(blocks, before, after):
    return jnp.pad(blocks, ((before, after), (0, 0), (0, 0)))


def spread(members, rows):
    nblocks = members.shape[0]
    width = members.shape[2]
    pieces = [members[:, number * BLOCK:(number + 1) * BLOCK] for number in range(7)]
    first_level = shifted(pieces[0], 0, 2) + shifted(pieces[1], 1, 1) + shifted(pieces[2], 2, 0)
    lower_two = jnp.sum(pieces[3].reshape(nblocks // 2, 2, BLOCK, width), axis=1)
    upper_two = jnp.sum(pieces[4].reshape(nblocks // 2, 2, BLOCK, width), axis=1)
    second_level = shifted(lower_two, 0, 2) + shifted(upper_two, 2, 0)
    lower_four = jnp.sum(pieces[5].reshape(nblocks // 4, 4, BLOCK, width), axis=1)
    upper_four = jnp.sum(pieces[6].reshape(nblocks // 4, 4, BLOCK, width), axis=1)
    third_level = shifted(lower_four, 0, 2) + shifted(upper_four, 2, 0)
    return first_level.reshape(-1, width), second_level.reshape(-1, width), third_level.reshape(-1, width)


def pooled(array, factor):
    rows, width = array.shape
    return jnp.mean(array.reshape(rows // factor, factor, width).astype(jnp.float32), axis=1).astype(jnp.bfloat16)


def padded(array):
    return jnp.pad(array, ((BLOCK, BLOCK), (0, 0)))


def stitch(stacked):
    middle = stacked[:, BLOCK:-BLOCK]
    tails = jnp.concatenate([jnp.zeros_like(stacked[:1, -BLOCK:]), stacked[:-1, -BLOCK:]], axis=0)
    heads_part = jnp.concatenate([stacked[1:, :BLOCK], jnp.zeros_like(stacked[:1, :BLOCK])], axis=0)
    middle = middle.at[:, :BLOCK].add(tails)
    middle = middle.at[:, -BLOCK:].add(heads_part)
    return middle.reshape(-1, stacked.shape[2])


def reference(queries, keys, values, out_weight, grad_out):
    rows = TOK_DEV
    nblocks = rows // BLOCK
    key_levels = [padded(keys), padded(pooled(keys, 2)), padded(pooled(keys, 4))]
    value_levels = [padded(values), padded(pooled(values, 2)), padded(pooled(values, 4))]

    def local_sets(group):
        first = group * rows
        key_ext = [lax.dynamic_slice_in_dim(key_levels[level], (group * (rows // 2 ** level)).astype(jnp.int32), rows // 2 ** level + 2 * BLOCK, 0) for level in range(3)]
        value_ext = [lax.dynamic_slice_in_dim(value_levels[level], (group * (rows // 2 ** level)).astype(jnp.int32), rows // 2 ** level + 2 * BLOCK, 0) for level in range(3)]
        flags, biases = set_masks(first, TOKENS, nblocks)
        local_q = lax.dynamic_slice_in_dim(queries, (group * rows).astype(jnp.int32), rows, 0)
        return local_q, key_sets(key_ext, nblocks), key_sets(value_ext, nblocks), flags, biases

    def forward_group(group):
        local_q, key_set, value_set, flags, biases = local_sets(group)
        return attend(local_q, key_set, value_set, flags, biases)

    groups = jnp.arange(N_SEQ, dtype=jnp.int32)
    attention = lax.map(forward_group, groups).reshape(TOKENS, D)
    output = lax.dot_general(attention, out_weight, (((1,), (1,)), ((), ())), preferred_element_type=jnp.float32).astype(jnp.bfloat16)
    grad_attention = jnp.dot(grad_out, out_weight, preferred_element_type=jnp.float32).astype(jnp.bfloat16)
    grad_weight = lax.dot_general(grad_out, attention, (((0,), (0,)), ((), ())), preferred_element_type=jnp.float32)

    def backward_group(group):
        local_q, key_set, value_set, flags, biases = local_sets(group)
        local_g = lax.dynamic_slice_in_dim(grad_attention, (group * rows).astype(jnp.int32), rows, 0)
        grad_q, members = attend_back(local_q, key_set, value_set, flags, biases, local_g)
        first_level, second_level, third_level = spread(members, rows)
        return grad_q, first_level, second_level, third_level

    grad_q, first_level, second_level, third_level = lax.map(backward_group, groups)
    summed = stitch(first_level) + jnp.repeat(stitch(second_level) * 0.5, 2, axis=0) + jnp.repeat(stitch(third_level) * 0.25, 4, axis=0)
    grad_keys = summed[:, :D].astype(jnp.bfloat16)
    grad_values = summed[:, D:].astype(jnp.bfloat16)
    return output, grad_q.reshape(TOKENS, D), grad_keys, grad_values, grad_weight
```

```python
import math

import jax
import jax.numpy as jnp
from jax import lax
from jax.experimental import pallas as pl
from jax.experimental.pallas import tpu as pltpu
from jax.sharding import PartitionSpec as P

HEAD_DIM = 128
BLOCK = 128
SCALE = HEAD_DIM ** -0.5
LOG2 = SCALE / math.log(2.0)
NEG = -1e30
VMEM = pl.BlockSpec(memory_space=pltpu.VMEM)
FAR = pl.BlockSpec(memory_space=pl.ANY)
PIECES = 4
NT = (((1,), (1,)), ((), ()))
TN = (((0,), (0,)), ((), ()))
NN = (((1,), (0,)), ((), ()))


def mm(a, b, dims):
    return lax.dot_general(a, b, dims, preferred_element_type=jnp.float32)


def run(body, args, outs, scratch=(), flops=0, moved=0, far_args=(), far_outs=(), room=24):
    return pl.pallas_call(
        body,
        in_specs=[FAR if number in far_args else VMEM for number in range(len(args))],
        out_shape=[jax.ShapeDtypeStruct(shape, kind) for shape, kind in outs],
        out_specs=[FAR if number in far_outs else VMEM for number in range(len(outs))],
        scratch_shapes=list(scratch),
        cost_estimate=pl.CostEstimate(flops=flops, bytes_accessed=moved, transcendentals=0),
        compiler_params=pltpu.CompilerParams(vmem_limit_bytes=room * 1024 * 1024),
    )(*args)


def pool_matrix(rows, factor):
    row = lax.broadcasted_iota(jnp.int32, (rows, rows * factor), 0)
    col = lax.broadcasted_iota(jnp.int32, (rows, rows * factor), 1)
    inside = (col >= row * factor) & (col < row * factor + factor)
    return jnp.where(inside, 1.0 / factor, 0.0).astype(jnp.bfloat16)


def repeat_matrix(rows, factor):
    row = lax.broadcasted_iota(jnp.int32, (rows * factor, rows), 0)
    col = lax.broadcasted_iota(jnp.int32, (rows * factor, rows), 1)
    inside = (row >= col * factor) & (row < col * factor + factor)
    return jnp.where(inside, 1.0, 0.0).astype(jnp.bfloat16)


def repeated(part, factor):
    matrix = repeat_matrix(part.shape[0], factor)
    high = part.astype(jnp.bfloat16)
    low = (part - high.astype(jnp.float32)).astype(jnp.bfloat16)
    return mm(matrix, high, NN) + mm(matrix, low, NN)


def in_pieces(source, target, sems):
    count = sems.shape[0]
    size = source.shape[0] // count
    return [pltpu.make_async_copy(source.at[pl.ds(number * size, size)], target.at[pl.ds(number * size, size)],
                                  sems.at[number]) for number in range(count)]


def on_even():
    return lax.rem(lax.axis_index("seq"), 2) == 0


def prepare(keys, values, mine, to_next, to_prev):
    width = keys.shape[1]
    two = pool_matrix(256, 2)
    four = pool_matrix(64, 4)
    for number, source in enumerate((keys, values)):
        cols = slice(number * width, (number + 1) * width)
        mine[:, cols] = source[...]
        first = mm(two, source[...], NN).astype(jnp.bfloat16)
        to_next[0:128, cols] = source[384:512]
        to_next[128:192, cols] = first[128:192]
        to_next[192:256, cols] = mm(four, source[0:256], NN).astype(jnp.bfloat16)
        to_prev[0:128, cols] = source[0:128]
        to_prev[128:192, cols] = first[64:128]
        to_prev[192:256, cols] = mm(four, source[256:512], NN).astype(jnp.bfloat16)


def fetch(queries, weight, _, queries_here, weight_here):
    queries_here[...] = queries[...]
    weight_here[...] = weight[...]


def widen(before, after, edge):
    half = pool_matrix(64, 2)
    both = pool_matrix(32, 2)
    quarter = pool_matrix(32, 4)
    edge[0:128] = before[0:128]
    edge[128:256] = after[0:128]
    edge[256:320] = before[128:192]
    edge[320:384] = mm(half, before[0:128], NN).astype(jnp.bfloat16)
    edge[384:448] = mm(half, after[0:128], NN).astype(jnp.bfloat16)
    edge[448:512] = after[128:192]
    edge[512:576] = before[192:256]
    edge[576:608] = mm(both, before[128:192], NN).astype(jnp.bfloat16)
    edge[608:640] = mm(quarter, before[0:128], NN).astype(jnp.bfloat16)
    edge[640:672] = mm(quarter, after[0:128], NN).astype(jnp.bfloat16)
    edge[672:704] = mm(both, after[128:192], NN).astype(jnp.bfloat16)
    edge[704:768] = after[192:256]


def own_set(half, mine, pooled):
    both = (0, 256)
    if half == 0:
        return [(mine, 0, 128, 0, both), (mine, 128, 256, 0, both), (mine, 256, 384, 0, (128, 256)), (pooled, 128, 1024, 1, both)]
    return [(mine, 128, 256, 0, (0, 128)), (mine, 256, 384, 0, both), (mine, 384, 512, 0, both), (pooled, 0, 896, 1, both)]


def edge_set(half, edge):
    place = lax.axis_index("seq")
    has_prev = place > 0
    has_next = place < lax.axis_size("seq") - 1
    both = (0, 256)
    far = [(edge, 512, 1280, 2, both, has_prev), (edge, 640, 1408, 2, both, has_next)]
    if half == 0:
        return [(edge, 0, 0, 0, (0, 128), has_prev), (edge, 256, 768, 1, both, has_prev)] + far
    return [(edge, 128, 640, 0, (128, 256), has_next), (edge, 384, 1152, 1, both, has_next)] + far


def logits_of(blocks, mine_q, cols):
    scores = []
    for source, row, _, level, seen, *there in blocks:
        score = mm(source[row:row + 128, cols], mine_q, NT) * LOG2
        if there:
            score = score + jnp.where(there[0], float(level), NEG)
        elif level:
            score = score + float(level)
        empty = jnp.full((128, 128), NEG, jnp.float32)
        if seen == (0, 128):
            score = jnp.concatenate([score[:, :128], empty], axis=1)
        if seen == (128, 256):
            score = jnp.concatenate([empty, score[:, 128:]], axis=1)
        scores.append(score)
    return scores


def gather(blocks, scores, top, value_cols):
    total = jnp.zeros((128, 256), jnp.float32)
    summed = jnp.zeros((128, 256), jnp.float32)
    for (source, row, *_), score in zip(blocks, scores):
        expd = jnp.exp2(score - top)
        total = total + expd
        summed = summed + mm(source[row:row + 128, value_cols], expd.astype(jnp.bfloat16), TN)
    return jnp.sum(total, axis=0, keepdims=True), summed


def top_of(scores):
    top = scores[0]
    for score in scores[1:]:
        top = jnp.maximum(top, score)
    return jnp.max(top, axis=0, keepdims=True)


def forward_own(queries, mine, _, tops, totals, sums, pooled):
    pooled[...] = mm(pool_matrix(256, 2), mine[...], NN).astype(jnp.bfloat16)
    width = queries.shape[1]
    for head in range(2):
        cols = slice(head * 128, head * 128 + 128)
        value_cols = slice(width + head * 128, width + head * 128 + 128)
        for half in range(2):
            span = slice(256 * half, 256 * half + 256)
            blocks = own_set(half, mine, pooled)
            scores = logits_of(blocks, queries[span, cols], cols)
            top = top_of(scores)
            tops[head:head + 1, span] = top
            totals[head:head + 1, span], sums[head * 128:head * 128 + 128, span] = gather(blocks, scores, top, value_cols)


def forward(queries, before, after, weight, tops, totals, sums,
            attention, lse, own, first_up, second_up, first_down, edge):
    widen(before, after, edge)
    width = queries.shape[1]
    for head in range(2):
        cols = slice(head * 128, head * 128 + 128)
        value_cols = slice(width + head * 128, width + head * 128 + 128)
        for half in range(2):
            span = slice(256 * half, 256 * half + 256)
            blocks = edge_set(half, edge)
            scores = logits_of(blocks, queries[span, cols], cols)
            before_top = tops[head:head + 1, span]
            top = jnp.maximum(before_top, top_of(scores))
            total, summed = gather(blocks, scores, top, value_cols)
            scale = jnp.exp2(before_top - top)
            total = total + scale * totals[head:head + 1, span]
            lse[head:head + 1, span] = top + jnp.log2(total)
            result = ((summed + scale * sums[head * 128:head * 128 + 128, span]) / total).T
            attention[span, cols] = result.astype(jnp.bfloat16)
    heads = lax.axis_size("head")
    here = lax.axis_index("head")

    def partial_to(target):
        start = pl.multiple_of(lax.rem(target, heads) * width, width)
        return mm(attention[...], weight[pl.ds(start, width), :], NT)

    own[...] = partial_to(here).astype(jnp.bfloat16)
    first_up[...] = partial_to(here + 2).astype(jnp.bfloat16)
    second_up[...] = partial_to(here + 1).astype(jnp.bfloat16)
    first_down[...] = partial_to(here + 3).astype(jnp.bfloat16)


def products(mine, below, above, opposite, attention, weight, keep, send, grad_attention, deltas):
    heads = lax.axis_size("head")
    here = lax.axis_index("head")
    even = on_even()
    groups, rows, width = keep.shape
    each = groups // heads
    total = jnp.zeros(grad_attention.shape, jnp.float32)
    for shift, cot in ((0, mine), (heads - 1, below), (1, above), (2, opposite)):
        owner = lax.rem(here + shift, heads)
        chunks = mm(cot[...], attention[...], TN).reshape(each, 2, rows, width)
        first, second = chunks[:, 0], chunks[:, 1]
        start = owner * each
        keep[pl.ds(start, each)] = jnp.where(even, first, second)
        send[pl.ds(start, each)] = jnp.where(even, second, first).astype(jnp.bfloat16)
        total = total + mm(cot[...], weight[pl.ds(pl.multiple_of(owner * width, width), width), :], NN)
    rounded = total.astype(jnp.bfloat16)
    grad_attention[...] = rounded
    terms = rounded.astype(jnp.float32) * attention[...].astype(jnp.float32)
    high = terms.astype(jnp.bfloat16)
    low = (terms - high.astype(jnp.float32)).astype(jnp.bfloat16)
    ones = jnp.ones((16, HEAD_DIM), jnp.bfloat16)
    for head in range(2):
        cols = slice(head * HEAD_DIM, head * HEAD_DIM + HEAD_DIM)
        deltas[head:head + 1] = (mm(ones, high[:, cols], NT) + mm(ones, low[:, cols], NT))[0:1]


def pair_sum(keep, sibling, pairs):
    pairs[...] = (keep[...] + sibling[...].astype(jnp.float32)).astype(jnp.bfloat16)


def score_grads(blocks, scores, norm, delta, cot, value_cols):
    pairs = []
    for (source, row, *_), score in zip(blocks, scores):
        prob = jnp.exp2(score - norm)
        dprob = mm(source[row:row + 128, value_cols], cot, NT)
        pairs.append((prob.astype(jnp.bfloat16), (prob * (dprob - delta)).astype(jnp.bfloat16)))
    return pairs


def backward(queries, before, after, lse, grad_attention, deltas, second_up, from_below,
             dscores, to_next, to_prev, edge, send_up, total):
    send_up[...] = (second_up[...].astype(jnp.float32) + from_below[...].astype(jnp.float32)).astype(jnp.bfloat16)
    widen(before, after, edge)
    width = queries.shape[1]
    for half in range(2):
        span = slice(256 * half, 256 * half + 256)
        blocks = edge_set(half, edge)
        for head in range(2):
            cols = slice(head * 128, head * 128 + 128)
            value_cols = slice(width + head * 128, width + head * 128 + 128)
            mine_q = queries[span, cols]
            cot = grad_attention[span, cols]
            pairs = score_grads(blocks, logits_of(blocks, mine_q, cols), lse[head:head + 1, span],
                                deltas[head:head + 1, span], cot, value_cols)
            for number, ((_, _, at, *_), (prob, dscore)) in enumerate(zip(blocks, pairs)):
                dscores[2 * half + head, 128 * number:128 * number + 128] = dscore
                grad_k = mm(dscore, mine_q, NN) * SCALE
                grad_v = mm(prob, cot, NN)
                if half == 1 and at >= 1280:
                    total[at:at + 128, cols] += grad_k
                    total[at:at + 128, value_cols] += grad_v
                else:
                    total[at:at + 128, cols] = grad_k
                    total[at:at + 128, value_cols] = grad_v
    to_prev[0:128] = (total[0:128] + repeated(total[832:896] * 0.5, 2)
                      + repeated(total[1376:1408] * 0.25, 4)).astype(jnp.bfloat16)
    to_prev[128:192] = (total[768:832] * 0.5 + repeated(total[1344:1376] * 0.25, 2)).astype(jnp.bfloat16)
    to_prev[192:256] = (total[1280:1344] * 0.25).astype(jnp.bfloat16)
    to_next[0:128] = (total[640:768] + repeated(total[1152:1216] * 0.5, 2)
                      + repeated(total[1408:1440] * 0.25, 4)).astype(jnp.bfloat16)
    to_next[128:192] = (total[1216:1280] * 0.5 + repeated(total[1440:1472] * 0.25, 2)).astype(jnp.bfloat16)
    to_next[192:256] = (total[1472:1536] * 0.25).astype(jnp.bfloat16)


def own_grads(queries, mine, edge, lse, grad_attention, deltas, dscores,
              grad_queries, own, total, pooled, grad_q_here, sems):
    pooled[...] = mm(pool_matrix(256, 2), mine[...], NN).astype(jnp.bfloat16)
    stores = []
    width = queries.shape[1]
    for half in range(2):
        span = slice(256 * half, 256 * half + 256)
        blocks = own_set(half, mine, pooled)
        for head in range(2):
            cols = slice(head * 128, head * 128 + 128)
            value_cols = slice(width + head * 128, width + head * 128 + 128)
            mine_q = queries[span, cols]
            cot = grad_attention[span, cols]
            pairs = score_grads(blocks, logits_of(blocks, mine_q, cols), lse[head:head + 1, span],
                                deltas[head:head + 1, span], cot, value_cols)
            grad_q = jnp.zeros((128, 256), jnp.float32)
            for number, (source, row, *_) in enumerate(edge_set(half, edge)):
                grad_q = grad_q + mm(source[row:row + 128, cols], dscores[2 * half + head, 128 * number:128 * number + 128], TN)
            for (source, row, at, *_), (prob, dscore) in zip(blocks, pairs):
                grad_q = grad_q + mm(source[row:row + 128, cols], dscore, TN)
                grad_k = mm(dscore, mine_q, NN) * SCALE
                grad_v = mm(prob, cot, NN)
                if half == 1 and 256 <= at < 512:
                    total[at:at + 128, cols] += grad_k
                    total[at:at + 128, value_cols] += grad_v
                else:
                    total[at:at + 128, cols] = grad_k
                    total[at:at + 128, value_cols] = grad_v
            grad_q_here[span, cols] = (grad_q * SCALE).T.astype(jnp.bfloat16)
        store = pltpu.make_async_copy(grad_q_here.at[span], grad_queries.at[span], sems.at[half])
        store.start()
        stores.append(store)
    own[...] = (total[128:640] + repeated(total[896:1152] * 0.5, 2)).astype(jnp.bfloat16)
    for store in stores:
        store.wait()


def finish(own_out, from_above, last_below, own, from_prev, from_next, spread,
           output, grad_keys, grad_values, grad_weight,
           output_here, grad_keys_here, grad_values_here, grad_weight_here, spread_here, load_sems, sems):
    loads = in_pieces(spread, spread_here, load_sems)
    for copy in loads:
        copy.start()
    width = grad_keys.shape[1]
    stores = []

    def store(source, target):
        copy = pltpu.make_async_copy(source, target, sems.at[len(stores)])
        copy.start()
        stores.append(copy)

    top, bottom = pl.ds(0, 256), pl.ds(256, 256)
    output_here[top] = (own_out[top].astype(jnp.float32) + last_below[top].astype(jnp.float32)
                        + from_above[top].astype(jnp.float32)).astype(jnp.bfloat16)
    store(output_here.at[top], output.at[top])
    output_here[bottom] = (own_out[bottom].astype(jnp.float32) + last_below[bottom].astype(jnp.float32)
                           + from_above[bottom].astype(jnp.float32)).astype(jnp.bfloat16)
    store(output_here.at[bottom], output.at[bottom])
    twice = repeat_matrix(64, 2)
    four = repeat_matrix(64, 4)
    coarse = mm(four, from_next[192:256], NN)
    low = mm(four, from_prev[192:256], NN)
    first = own[0:128].astype(jnp.float32) + coarse[0:128] + from_prev[0:128].astype(jnp.float32)
    second = own[128:256].astype(jnp.float32) + coarse[128:256] + mm(twice, from_prev[128:192], NN)
    third = own[256:384].astype(jnp.float32) + low[0:128] + mm(twice, from_next[128:192], NN)
    fourth = own[384:512].astype(jnp.float32) + low[128:256] + from_next[0:128].astype(jnp.float32)
    for number, part in enumerate((first, second, third, fourth)):
        span = pl.ds(128 * number, 128)
        part = part.astype(jnp.bfloat16)
        grad_keys_here[span] = part[:, :width]
        grad_values_here[span] = part[:, width:]
        if number % 2:
            half = pl.ds(128 * (number - 1), 256)
            store(grad_keys_here.at[half], grad_keys.at[half])
            store(grad_values_here.at[half], grad_values.at[half])
    for copy in loads:
        copy.wait()
    grad_weight_here[...] = jnp.sum(spread_here[...].astype(jnp.float32), axis=0)
    store(grad_weight_here, grad_weight)
    for copy in stores:
        copy.wait()


def local(queries, keys, values, out_weight, grad_out):
    bf16, f32 = jnp.bfloat16, jnp.float32
    rows, width = queries.shape
    shards = lax.axis_size("seq")
    heads = lax.axis_size("head")
    features = out_weight.shape[0]
    up = [(i, (i + 1) % heads) for i in range(heads)]
    down = [(target, source) for source, target in up]
    swap = [(i, i ^ 1) for i in range(shards)]
    onward = [(i, (i + 1) % shards) for i in range(shards)]
    back = [(target, source) for source, target in onward]
    dma = pltpu.SemaphoreType.DMA

    below = lax.ppermute(grad_out, "head", up)
    above = lax.ppermute(grad_out, "head", down)

    mine, to_next, to_prev = run(
        prepare, (keys, values),
        [((512, 2 * width), bf16), ((256, 2 * width), bf16), ((256, 2 * width), bf16)],
        flops=2 * 384 * 512 * 512, moved=1 << 20)
    before = lax.ppermute(to_next, "seq", onward)
    after = lax.ppermute(to_prev, "seq", back)
    queries, out_weight = run(
        fetch, (queries, out_weight, to_next), [((rows, width), bf16), ((features, width), bf16)],
        moved=2 << 20, far_args=(2,))
    tops, totals, sums = run(
        forward_own, (queries, mine, to_next),
        [((2, rows), f32), ((2, rows), f32), ((2 * HEAD_DIM, rows), f32)],
        [pltpu.VMEM((256, 2 * width), bf16)], flops=10 ** 9, moved=2 << 20, far_args=(2,))
    opposite = lax.ppermute(below, "head", up)

    attention, lse, own_out, first_up, second_up, first_down = run(
        forward, (queries, before, after, out_weight, tops, totals, sums),
        [((rows, width), bf16), ((2, rows), f32), ((rows, width), bf16), ((rows, width), bf16),
         ((rows, width), bf16), ((rows, width), bf16)],
        [pltpu.VMEM((768, 2 * width), bf16)], flops=10 ** 9, moved=3 << 20)
    from_below = lax.ppermute(first_up, "head", up)
    from_above = lax.ppermute(first_down, "head", down)

    chunk = features // shards
    keep, send, grad_attention, deltas = run(
        products, (grad_out, below, above, opposite, attention, out_weight),
        [((shards // 2, chunk, width), f32), ((shards // 2, chunk, width), bf16), ((rows, width), bf16), ((2, rows), f32)],
        flops=6 * 10 ** 8, moved=2 << 20)
    half_sum = lax.ppermute(send, "seq", swap)
    pairs, = run(pair_sum, (keep, half_sum), [((shards // 2, chunk, width), bf16)], moved=1 << 20)
    groups = [list(range(core, shards, 2)) for core in range(2)]
    spread = lax.all_to_all(pairs, "seq", 0, 0, axis_index_groups=groups)

    dscores, to_next, to_prev, edge, send_up = run(
        backward, (queries, before, after, lse, grad_attention, deltas, second_up, from_below),
        [((4, 512, 256), bf16), ((256, 2 * width), bf16), ((256, 2 * width), bf16), ((768, 2 * width), bf16),
         ((rows, width), bf16)],
        [pltpu.VMEM((1536, 2 * width), f32)], flops=2 * 10 ** 9, moved=4 << 20)
    last_below = lax.ppermute(send_up, "head", up)
    grad_before = lax.ppermute(to_next, "seq", onward)
    grad_after = lax.ppermute(to_prev, "seq", back)
    grad_queries, own_grad = run(
        own_grads, (queries, mine, edge, lse, grad_attention, deltas, dscores),
        [((rows, width), bf16), ((rows, 2 * width), bf16)],
        [pltpu.VMEM((1536, 2 * width), f32), pltpu.VMEM((256, 2 * width), bf16), pltpu.VMEM((rows, width), bf16), dma((2,))],
        flops=3 * 10 ** 9, moved=6 << 20, far_outs=(0,))

    output, grad_keys, grad_values, grad_weight = run(
        finish,
        (own_out, from_above, last_below, own_grad, grad_before, grad_after, spread),
        [((rows, width), bf16)] * 3 + [((chunk, width), f32)],
        [pltpu.VMEM((rows, width), bf16)] * 3 + [pltpu.VMEM((chunk, width), f32)]
        + [pltpu.VMEM((shards // 2, chunk, width), bf16), dma((PIECES,)), dma((7,))],
        moved=4 << 20, far_args=(6,), far_outs=(0, 1, 2, 3))
    return output, grad_queries, grad_keys, grad_values, grad_weight


def solution(mesh):
    split = P("seq", "head")
    return jax.shard_map(
        local, mesh=mesh, in_specs=(split, split, split, P(None, "head"), split),
        out_specs=(split,) * 5, check_vma=False)
```

```python
import math

import jax
import jax.numpy as jnp
from jax import lax
from jax.experimental import pallas as pl
from jax.experimental.pallas import tpu as pltpu
from jax.sharding import PartitionSpec as P

HEAD_DIM = 128
BLOCK = 128
SCALE = HEAD_DIM ** -0.5
LOG2 = SCALE / math.log(2.0)
NEG = -1e30
VMEM = pl.BlockSpec(memory_space=pltpu.VMEM)
FAR = pl.BlockSpec(memory_space=pl.ANY)
PIECES = 4
NT = (((1,), (1,)), ((), ()))
TN = (((0,), (0,)), ((), ()))
NN = (((1,), (0,)), ((), ()))


def mm(a, b, dims):
    return lax.dot_general(a, b, dims, preferred_element_type=jnp.float32)


def run(body, args, outs, scratch=(), flops=0, moved=0, far_args=(), far_outs=(), room=24):
    return pl.pallas_call(
        body,
        in_specs=[FAR if number in far_args else VMEM for number in range(len(args))],
        out_shape=[jax.ShapeDtypeStruct(shape, kind) for shape, kind in outs],
        out_specs=[FAR if number in far_outs else VMEM for number in range(len(outs))],
        scratch_shapes=list(scratch),
        cost_estimate=pl.CostEstimate(flops=flops, bytes_accessed=moved, transcendentals=0),
        compiler_params=pltpu.CompilerParams(vmem_limit_bytes=room * 1024 * 1024),
    )(*args)


def pool_matrix(rows, factor):
    row = lax.broadcasted_iota(jnp.int32, (rows, rows * factor), 0)
    col = lax.broadcasted_iota(jnp.int32, (rows, rows * factor), 1)
    inside = (col >= row * factor) & (col < row * factor + factor)
    return jnp.where(inside, 1.0 / factor, 0.0).astype(jnp.bfloat16)


def repeat_matrix(rows, factor):
    row = lax.broadcasted_iota(jnp.int32, (rows * factor, rows), 0)
    col = lax.broadcasted_iota(jnp.int32, (rows * factor, rows), 1)
    inside = (row >= col * factor) & (row < col * factor + factor)
    return jnp.where(inside, 1.0, 0.0).astype(jnp.bfloat16)


def repeated(part, factor):
    matrix = repeat_matrix(part.shape[0], factor)
    high = part.astype(jnp.bfloat16)
    low = (part - high.astype(jnp.float32)).astype(jnp.bfloat16)
    return mm(matrix, high, NN) + mm(matrix, low, NN)


def in_pieces(source, target, sems):
    count = sems.shape[0]
    size = source.shape[0] // count
    return [pltpu.make_async_copy(source.at[pl.ds(number * size, size)], target.at[pl.ds(number * size, size)],
                                  sems.at[number]) for number in range(count)]


def on_even():
    return lax.rem(lax.axis_index("seq"), 2) == 0


def prepare(keys, values, mine, to_next, to_prev):
    width = keys.shape[1]
    two = pool_matrix(256, 2)
    four = pool_matrix(64, 4)
    for number, source in enumerate((keys, values)):
        cols = slice(number * width, (number + 1) * width)
        mine[:, cols] = source[...]
        first = mm(two, source[...], NN).astype(jnp.bfloat16)
        to_next[0:128, cols] = source[384:512]
        to_next[128:192, cols] = first[128:192]
        to_next[192:256, cols] = mm(four, source[0:256], NN).astype(jnp.bfloat16)
        to_prev[0:128, cols] = source[0:128]
        to_prev[128:192, cols] = first[64:128]
        to_prev[192:256, cols] = mm(four, source[256:512], NN).astype(jnp.bfloat16)


def fetch(queries, weight, _, queries_here, weight_here):
    queries_here[...] = queries[...]
    weight_here[...] = weight[...]


def widen(before, after, edge):
    half = pool_matrix(64, 2)
    both = pool_matrix(32, 2)
    quarter = pool_matrix(32, 4)
    edge[0:128] = before[0:128]
    edge[128:256] = after[0:128]
    edge[256:320] = before[128:192]
    edge[320:384] = mm(half, before[0:128], NN).astype(jnp.bfloat16)
    edge[384:448] = mm(half, after[0:128], NN).astype(jnp.bfloat16)
    edge[448:512] = after[128:192]
    edge[512:576] = before[192:256]
    edge[576:608] = mm(both, before[128:192], NN).astype(jnp.bfloat16)
    edge[608:640] = mm(quarter, before[0:128], NN).astype(jnp.bfloat16)
    edge[640:672] = mm(quarter, after[0:128], NN).astype(jnp.bfloat16)
    edge[672:704] = mm(both, after[128:192], NN).astype(jnp.bfloat16)
    edge[704:768] = after[192:256]


def own_set(half, mine, pooled):
    both = (0, 256)
    if half == 0:
        return [(mine, 0, 128, 0, both), (mine, 128, 256, 0, both), (mine, 256, 384, 0, (128, 256)), (pooled, 128, 1024, 1, both)]
    return [(mine, 128, 256, 0, (0, 128)), (mine, 256, 384, 0, both), (mine, 384, 512, 0, both), (pooled, 0, 896, 1, both)]


def edge_set(half, edge):
    place = lax.axis_index("seq")
    has_prev = place > 0
    has_next = place < lax.axis_size("seq") - 1
    both = (0, 256)
    far = [(edge, 512, 1280, 2, both, has_prev), (edge, 640, 1408, 2, both, has_next)]
    if half == 0:
        return [(edge, 0, 0, 0, (0, 128), has_prev), (edge, 256, 768, 1, both, has_prev)] + far
    return [(edge, 128, 640, 0, (128, 256), has_next), (edge, 384, 1152, 1, both, has_next)] + far


def logits_of(blocks, mine_q, cols):
    scores = []
    for source, row, _, level, seen, *there in blocks:
        score = mm(source[row:row + 128, cols], mine_q, NT) * LOG2
        if there:
            score = score + jnp.where(there[0], float(level), NEG)
        elif level:
            score = score + float(level)
        empty = jnp.full((128, 128), NEG, jnp.float32)
        if seen == (0, 128):
            score = jnp.concatenate([score[:, :128], empty], axis=1)
        if seen == (128, 256):
            score = jnp.concatenate([empty, score[:, 128:]], axis=1)
        scores.append(score)
    return scores


def gather(blocks, scores, top, value_cols):
    total = jnp.zeros((128, 256), jnp.float32)
    summed = jnp.zeros((128, 256), jnp.float32)
    for (source, row, *_), score in zip(blocks, scores):
        expd = jnp.exp2(score - top)
        total = total + expd
        summed = summed + mm(source[row:row + 128, value_cols], expd.astype(jnp.bfloat16), TN)
    return jnp.sum(total, axis=0, keepdims=True), summed


def top_of(scores):
    top = scores[0]
    for score in scores[1:]:
        top = jnp.maximum(top, score)
    return jnp.max(top, axis=0, keepdims=True)


def forward_own(queries, mine, _, tops, totals, sums, pooled):
    pooled[...] = mm(pool_matrix(256, 2), mine[...], NN).astype(jnp.bfloat16)
    width = queries.shape[1]
    for head in range(2):
        cols = slice(head * 128, head * 128 + 128)
        value_cols = slice(width + head * 128, width + head * 128 + 128)
        for half in range(2):
            span = slice(256 * half, 256 * half + 256)
            blocks = own_set(half, mine, pooled)
            scores = logits_of(blocks, queries[span, cols], cols)
            top = top_of(scores)
            tops[head:head + 1, span] = top
            totals[head:head + 1, span], sums[head * 128:head * 128 + 128, span] = gather(blocks, scores, top, value_cols)


def forward(queries, before, after, weight, tops, totals, sums,
            attention, lse, own, first_up, second_up, first_down, edge):
    widen(before, after, edge)
    width = queries.shape[1]
    for head in range(2):
        cols = slice(head * 128, head * 128 + 128)
        value_cols = slice(width + head * 128, width + head * 128 + 128)
        for half in range(2):
            span = slice(256 * half, 256 * half + 256)
            blocks = edge_set(half, edge)
            scores = logits_of(blocks, queries[span, cols], cols)
            before_top = tops[head:head + 1, span]
            top = jnp.maximum(before_top, top_of(scores))
            total, summed = gather(blocks, scores, top, value_cols)
            scale = jnp.exp2(before_top - top)
            total = total + scale * totals[head:head + 1, span]
            lse[head:head + 1, span] = top + jnp.log2(total)
            result = ((summed + scale * sums[head * 128:head * 128 + 128, span]) / total).T
            attention[span, cols] = result.astype(jnp.bfloat16)
    heads = lax.axis_size("head")
    here = lax.axis_index("head")

    def partial_to(target):
        start = pl.multiple_of(lax.rem(target, heads) * width, width)
        return mm(attention[...], weight[pl.ds(start, width), :], NT)

    own[...] = partial_to(here).astype(jnp.bfloat16)
    first_up[...] = partial_to(here + 2).astype(jnp.bfloat16)
    second_up[...] = partial_to(here + 1).astype(jnp.bfloat16)
    first_down[...] = partial_to(here + 3).astype(jnp.bfloat16)


def product_of(shift, cot, attention, weight, keep, send):
    heads = lax.axis_size("head")
    owner = lax.rem(lax.axis_index("head") + shift, heads)
    even = on_even()
    groups, rows, width = keep.shape
    each = groups // heads
    chunks = mm(cot[...], attention[...], TN).reshape(each, 2, rows, width)
    first, second = chunks[:, 0], chunks[:, 1]
    start = owner * each
    keep[pl.ds(start, each)] = jnp.where(even, first, second)
    send[pl.ds(start, each)] = jnp.where(even, second, first).astype(jnp.bfloat16)
    return mm(cot[...], weight[pl.ds(pl.multiple_of(owner * width, width), width), :], NN)


def near_products(mine, below, above, attention, weight, keep, send, part):
    heads = lax.axis_size("head")
    part[...] = (product_of(0, mine, attention, weight, keep, send)
                 + product_of(heads - 1, below, attention, weight, keep, send)
                 + product_of(1, above, attention, weight, keep, send))


def far_products(opposite, attention, weight, near_keep, near_send, part, keep, send, grad_attention, deltas):
    keep[...] = near_keep[...]
    send[...] = near_send[...]
    rounded = (part[...] + product_of(2, opposite, attention, weight, keep, send)).astype(jnp.bfloat16)
    grad_attention[...] = rounded
    terms = rounded.astype(jnp.float32) * attention[...].astype(jnp.float32)
    high = terms.astype(jnp.bfloat16)
    low = (terms - high.astype(jnp.float32)).astype(jnp.bfloat16)
    ones = jnp.ones((16, HEAD_DIM), jnp.bfloat16)
    for head in range(2):
        cols = slice(head * HEAD_DIM, head * HEAD_DIM + HEAD_DIM)
        deltas[head:head + 1] = (mm(ones, high[:, cols], NT) + mm(ones, low[:, cols], NT))[0:1]


def pair_sum(keep, sibling, pairs, pairs_here, sems):
    stores = in_pieces(pairs_here, pairs, sems)
    size = pairs.shape[0] // len(stores)
    for number, store in enumerate(stores):
        span = pl.ds(number * size, size)
        pairs_here[span] = (keep[span] + sibling[span].astype(jnp.float32)).astype(jnp.bfloat16)
        store.start()
    for store in stores:
        store.wait()


def score_grads(blocks, scores, norm, delta, cot, value_cols):
    pairs = []
    for (source, row, *_), score in zip(blocks, scores):
        prob = jnp.exp2(score - norm)
        dprob = mm(source[row:row + 128, value_cols], cot, NT)
        pairs.append((prob.astype(jnp.bfloat16), (prob * (dprob - delta)).astype(jnp.bfloat16)))
    return pairs


def backward(queries, before, after, lse, grad_attention, deltas, second_up, from_below, own, from_above,
             dscores, to_next, to_prev, edge, send_up, near, total):
    send_up[...] = (second_up[...].astype(jnp.float32) + from_below[...].astype(jnp.float32)).astype(jnp.bfloat16)
    near[...] = own[...].astype(jnp.float32) + from_above[...].astype(jnp.float32)
    widen(before, after, edge)
    width = queries.shape[1]
    for half in range(2):
        span = slice(256 * half, 256 * half + 256)
        blocks = edge_set(half, edge)
        for head in range(2):
            cols = slice(head * 128, head * 128 + 128)
            value_cols = slice(width + head * 128, width + head * 128 + 128)
            mine_q = queries[span, cols]
            cot = grad_attention[span, cols]
            pairs = score_grads(blocks, logits_of(blocks, mine_q, cols), lse[head:head + 1, span],
                                deltas[head:head + 1, span], cot, value_cols)
            for number, ((_, _, at, *_), (prob, dscore)) in enumerate(zip(blocks, pairs)):
                dscores[2 * half + head, 128 * number:128 * number + 128] = dscore
                grad_k = mm(dscore, mine_q, NN) * SCALE
                grad_v = mm(prob, cot, NN)
                if half == 1 and at >= 1280:
                    total[at:at + 128, cols] += grad_k
                    total[at:at + 128, value_cols] += grad_v
                else:
                    total[at:at + 128, cols] = grad_k
                    total[at:at + 128, value_cols] = grad_v
    to_prev[0:128] = (total[0:128] + repeated(total[832:896] * 0.5, 2)
                      + repeated(total[1376:1408] * 0.25, 4)).astype(jnp.bfloat16)
    to_prev[128:192] = (total[768:832] * 0.5 + repeated(total[1344:1376] * 0.25, 2)).astype(jnp.bfloat16)
    to_prev[192:256] = (total[1280:1344] * 0.25).astype(jnp.bfloat16)
    to_next[0:128] = (total[640:768] + repeated(total[1152:1216] * 0.5, 2)
                      + repeated(total[1408:1440] * 0.25, 4)).astype(jnp.bfloat16)
    to_next[128:192] = (total[1216:1280] * 0.5 + repeated(total[1440:1472] * 0.25, 2)).astype(jnp.bfloat16)
    to_next[192:256] = (total[1472:1536] * 0.25).astype(jnp.bfloat16)


def own_grads(queries, mine, edge, lse, grad_attention, deltas, dscores,
              grad_queries, own, total, pooled, grad_q_here, sems):
    pooled[...] = mm(pool_matrix(256, 2), mine[...], NN).astype(jnp.bfloat16)
    stores = []
    width = queries.shape[1]
    for half in range(2):
        span = slice(256 * half, 256 * half + 256)
        blocks = own_set(half, mine, pooled)
        for head in range(2):
            cols = slice(head * 128, head * 128 + 128)
            value_cols = slice(width + head * 128, width + head * 128 + 128)
            mine_q = queries[span, cols]
            cot = grad_attention[span, cols]
            pairs = score_grads(blocks, logits_of(blocks, mine_q, cols), lse[head:head + 1, span],
                                deltas[head:head + 1, span], cot, value_cols)
            grad_q = jnp.zeros((128, 256), jnp.float32)
            for number, (source, row, *_) in enumerate(edge_set(half, edge)):
                grad_q = grad_q + mm(source[row:row + 128, cols], dscores[2 * half + head, 128 * number:128 * number + 128], TN)
            for (source, row, at, *_), (prob, dscore) in zip(blocks, pairs):
                grad_q = grad_q + mm(source[row:row + 128, cols], dscore, TN)
                grad_k = mm(dscore, mine_q, NN) * SCALE
                grad_v = mm(prob, cot, NN)
                if half == 1 and 256 <= at < 512:
                    total[at:at + 128, cols] += grad_k
                    total[at:at + 128, value_cols] += grad_v
                else:
                    total[at:at + 128, cols] = grad_k
                    total[at:at + 128, value_cols] = grad_v
            grad_q_here[span, cols] = (grad_q * SCALE).T.astype(jnp.bfloat16)
        store = pltpu.make_async_copy(grad_q_here.at[span], grad_queries.at[span], sems.at[half])
        store.start()
        stores.append(store)
    own[...] = (total[128:640] + repeated(total[896:1152] * 0.5, 2)).astype(jnp.bfloat16)
    for store in stores:
        store.wait()


def finish(near_out, last_below, own, from_prev, from_next, spread,
           output, grad_keys, grad_values, grad_weight,
           output_here, grad_keys_here, grad_values_here, grad_weight_here, spread_here, load_sems, sems):
    loads = in_pieces(spread, spread_here, load_sems)
    for copy in loads:
        copy.start()
    width = grad_keys.shape[1]
    stores = []

    def store(source, target):
        copy = pltpu.make_async_copy(source, target, sems.at[len(stores)])
        copy.start()
        stores.append(copy)

    top, bottom = pl.ds(0, 256), pl.ds(256, 256)
    output_here[top] = (near_out[top] + last_below[top].astype(jnp.float32)).astype(jnp.bfloat16)
    store(output_here.at[top], output.at[top])
    output_here[bottom] = (near_out[bottom] + last_below[bottom].astype(jnp.float32)).astype(jnp.bfloat16)
    store(output_here.at[bottom], output.at[bottom])
    twice = repeat_matrix(64, 2)
    four = repeat_matrix(64, 4)
    coarse = mm(four, from_next[192:256], NN)
    low = mm(four, from_prev[192:256], NN)
    first = own[0:128].astype(jnp.float32) + coarse[0:128] + from_prev[0:128].astype(jnp.float32)
    second = own[128:256].astype(jnp.float32) + coarse[128:256] + mm(twice, from_prev[128:192], NN)
    third = own[256:384].astype(jnp.float32) + low[0:128] + mm(twice, from_next[128:192], NN)
    fourth = own[384:512].astype(jnp.float32) + low[128:256] + from_next[0:128].astype(jnp.float32)
    for number, part in enumerate((first, second, third, fourth)):
        span = pl.ds(128 * number, 128)
        part = part.astype(jnp.bfloat16)
        grad_keys_here[span] = part[:, :width]
        grad_values_here[span] = part[:, width:]
        if number % 2:
            half = pl.ds(128 * (number - 1), 256)
            store(grad_keys_here.at[half], grad_keys.at[half])
            store(grad_values_here.at[half], grad_values.at[half])
    for copy in loads:
        copy.wait()
    grad_weight_here[...] = jnp.sum(spread_here[...].astype(jnp.float32), axis=0)
    store(grad_weight_here, grad_weight)
    for copy in stores:
        copy.wait()


def local(queries, keys, values, out_weight, grad_out):
    bf16, f32 = jnp.bfloat16, jnp.float32
    rows, width = queries.shape
    shards = lax.axis_size("seq")
    heads = lax.axis_size("head")
    features = out_weight.shape[0]
    up = [(i, (i + 1) % heads) for i in range(heads)]
    down = [(target, source) for source, target in up]
    swap = [(i, i ^ 1) for i in range(shards)]
    onward = [(i, (i + 1) % shards) for i in range(shards)]
    back = [(target, source) for source, target in onward]
    dma = pltpu.SemaphoreType.DMA

    below = lax.ppermute(grad_out, "head", up)
    above = lax.ppermute(grad_out, "head", down)

    mine, to_next, to_prev = run(
        prepare, (keys, values),
        [((512, 2 * width), bf16), ((256, 2 * width), bf16), ((256, 2 * width), bf16)],
        flops=2 * 384 * 512 * 512, moved=1 << 20)
    before = lax.ppermute(to_next, "seq", onward)
    after = lax.ppermute(to_prev, "seq", back)
    queries, out_weight = run(
        fetch, (queries, out_weight, to_next), [((rows, width), bf16), ((features, width), bf16)],
        moved=2 << 20, far_args=(2,))
    tops, totals, sums = run(
        forward_own, (queries, mine, to_next),
        [((2, rows), f32), ((2, rows), f32), ((2 * HEAD_DIM, rows), f32)],
        [pltpu.VMEM((256, 2 * width), bf16)], flops=10 ** 9, moved=2 << 20, far_args=(2,))
    opposite = lax.ppermute(below, "head", up)

    attention, lse, own_out, first_up, second_up, first_down = run(
        forward, (queries, before, after, out_weight, tops, totals, sums),
        [((rows, width), bf16), ((2, rows), f32), ((rows, width), bf16), ((rows, width), bf16),
         ((rows, width), bf16), ((rows, width), bf16)],
        [pltpu.VMEM((768, 2 * width), bf16)], flops=10 ** 9, moved=3 << 20)
    from_below = lax.ppermute(first_up, "head", up)
    from_above = lax.ppermute(first_down, "head", down)

    chunk = features // shards
    shapes = [((shards // 2, chunk, width), f32), ((shards // 2, chunk, width), bf16)]
    keep, send, part = run(
        near_products, (grad_out, below, above, attention, out_weight), shapes + [((rows, width), f32)],
        flops=4 * 10 ** 8, moved=1 << 20)
    keep, send, grad_attention, deltas = run(
        far_products, (opposite, attention, out_weight, keep, send, part),
        shapes + [((rows, width), bf16), ((2, rows), f32)])
    half_sum = lax.ppermute(send, "seq", swap)
    pairs, = run(pair_sum, (keep, half_sum), [((shards // 2, chunk, width), bf16)],
                 [pltpu.VMEM((shards // 2, chunk, width), bf16), dma((PIECES,))], far_outs=(0,))
    groups = [list(range(core, shards, 2)) for core in range(2)]
    spread = lax.all_to_all(pairs, "seq", 0, 0, axis_index_groups=groups)

    dscores, to_next, to_prev, edge, send_up, near_out = run(
        backward,
        (queries, before, after, lse, grad_attention, deltas, second_up, from_below, own_out, from_above),
        [((4, 512, 256), bf16), ((256, 2 * width), bf16), ((256, 2 * width), bf16), ((768, 2 * width), bf16),
         ((rows, width), bf16), ((rows, width), f32)],
        [pltpu.VMEM((1536, 2 * width), f32)], flops=2 * 10 ** 9, moved=4 << 20)
    last_below = lax.ppermute(send_up, "head", up)
    grad_before = lax.ppermute(to_next, "seq", onward)
    grad_after = lax.ppermute(to_prev, "seq", back)
    grad_queries, own_grad = run(
        own_grads, (queries, mine, edge, lse, grad_attention, deltas, dscores),
        [((rows, width), bf16), ((rows, 2 * width), bf16)],
        [pltpu.VMEM((1536, 2 * width), f32), pltpu.VMEM((256, 2 * width), bf16), pltpu.VMEM((rows, width), bf16), dma((2,))],
        flops=3 * 10 ** 9, moved=6 << 20, far_outs=(0,))

    output, grad_keys, grad_values, grad_weight = run(
        finish,
        (near_out, last_below, own_grad, grad_before, grad_after, spread),
        [((rows, width), bf16)] * 3 + [((chunk, width), f32)],
        [pltpu.VMEM((rows, width), bf16)] * 3 + [pltpu.VMEM((chunk, width), f32)]
        + [pltpu.VMEM((shards // 2, chunk, width), bf16), dma((PIECES,)), dma((7,))],
        moved=4 << 20, far_args=(5,), far_outs=(0, 1, 2, 3))
    return output, grad_queries, grad_keys, grad_values, grad_weight


def solution(mesh):
    split = P("seq", "head")
    return jax.shard_map(
        local, mesh=mesh, in_specs=(split, split, split, P(None, "head"), split),
        out_specs=(split,) * 5, check_vma=False)
```

```python
import math

import jax
import jax.numpy as jnp
from jax import lax
from jax.experimental import pallas as pl
from jax.experimental.pallas import tpu as pltpu
from jax.sharding import PartitionSpec as P

HEAD_DIM = 128
BLOCK = 128
SCALE = HEAD_DIM ** -0.5
LOG2 = SCALE / math.log(2.0)
NEG = -1e30
VMEM = pl.BlockSpec(memory_space=pltpu.VMEM)
FAR = pl.BlockSpec(memory_space=pl.ANY)
PIECES = 4
NT = (((1,), (1,)), ((), ()))
TN = (((0,), (0,)), ((), ()))
NN = (((1,), (0,)), ((), ()))


def mm(a, b, dims):
    return lax.dot_general(a, b, dims, preferred_element_type=jnp.float32)


def run(body, args, outs, scratch=(), flops=0, moved=0, far_args=(), far_outs=(), room=24):
    return pl.pallas_call(
        body,
        in_specs=[FAR if number in far_args else VMEM for number in range(len(args))],
        out_shape=[jax.ShapeDtypeStruct(shape, kind) for shape, kind in outs],
        out_specs=[FAR if number in far_outs else VMEM for number in range(len(outs))],
        scratch_shapes=list(scratch),
        cost_estimate=pl.CostEstimate(flops=flops, bytes_accessed=moved, transcendentals=0),
        compiler_params=pltpu.CompilerParams(vmem_limit_bytes=room * 1024 * 1024),
    )(*args)


def pool_matrix(rows, factor):
    row = lax.broadcasted_iota(jnp.int32, (rows, rows * factor), 0)
    col = lax.broadcasted_iota(jnp.int32, (rows, rows * factor), 1)
    inside = (col >= row * factor) & (col < row * factor + factor)
    return jnp.where(inside, 1.0 / factor, 0.0).astype(jnp.bfloat16)


def repeat_matrix(rows, factor):
    row = lax.broadcasted_iota(jnp.int32, (rows * factor, rows), 0)
    col = lax.broadcasted_iota(jnp.int32, (rows * factor, rows), 1)
    inside = (row >= col * factor) & (row < col * factor + factor)
    return jnp.where(inside, 1.0, 0.0).astype(jnp.bfloat16)


def repeated(part, factor):
    matrix = repeat_matrix(part.shape[0], factor)
    high = part.astype(jnp.bfloat16)
    low = (part - high.astype(jnp.float32)).astype(jnp.bfloat16)
    return mm(matrix, high, NN) + mm(matrix, low, NN)


def in_pieces(source, target, sems):
    count = sems.shape[0]
    size = source.shape[0] // count
    return [pltpu.make_async_copy(source.at[pl.ds(number * size, size)], target.at[pl.ds(number * size, size)],
                                  sems.at[number]) for number in range(count)]


def on_even():
    return lax.rem(lax.axis_index("seq"), 2) == 0


def prepare(keys, values, mine, to_next, to_prev):
    width = keys.shape[1]
    two = pool_matrix(256, 2)
    four = pool_matrix(64, 4)
    for number, source in enumerate((keys, values)):
        cols = slice(number * width, (number + 1) * width)
        mine[:, cols] = source[...]
        first = mm(two, source[...], NN).astype(jnp.bfloat16)
        to_next[0:128, cols] = source[384:512]
        to_next[128:192, cols] = first[128:192]
        to_next[192:256, cols] = mm(four, source[0:256], NN).astype(jnp.bfloat16)
        to_prev[0:128, cols] = source[0:128]
        to_prev[128:192, cols] = first[64:128]
        to_prev[192:256, cols] = mm(four, source[256:512], NN).astype(jnp.bfloat16)


def fetch(queries, weight, _, queries_here, weight_here):
    queries_here[...] = queries[...]
    weight_here[...] = weight[...]


def widen(before, after, edge):
    half = pool_matrix(64, 2)
    both = pool_matrix(32, 2)
    quarter = pool_matrix(32, 4)
    edge[0:128] = before[0:128]
    edge[128:256] = after[0:128]
    edge[256:320] = before[128:192]
    edge[320:384] = mm(half, before[0:128], NN).astype(jnp.bfloat16)
    edge[384:448] = mm(half, after[0:128], NN).astype(jnp.bfloat16)
    edge[448:512] = after[128:192]
    edge[512:576] = before[192:256]
    edge[576:608] = mm(both, before[128:192], NN).astype(jnp.bfloat16)
    edge[608:640] = mm(quarter, before[0:128], NN).astype(jnp.bfloat16)
    edge[640:672] = mm(quarter, after[0:128], NN).astype(jnp.bfloat16)
    edge[672:704] = mm(both, after[128:192], NN).astype(jnp.bfloat16)
    edge[704:768] = after[192:256]


def own_set(half, mine, pooled):
    both = (0, 256)
    if half == 0:
        return [(mine, 0, 128, 0, both), (mine, 128, 256, 0, both), (mine, 256, 384, 0, (128, 256)), (pooled, 128, 1024, 1, both)]
    return [(mine, 128, 256, 0, (0, 128)), (mine, 256, 384, 0, both), (mine, 384, 512, 0, both), (pooled, 0, 896, 1, both)]


def edge_set(half, edge):
    place = lax.axis_index("seq")
    has_prev = place > 0
    has_next = place < lax.axis_size("seq") - 1
    both = (0, 256)
    far = [(edge, 512, 1280, 2, both, has_prev), (edge, 640, 1408, 2, both, has_next)]
    if half == 0:
        return [(edge, 0, 0, 0, (0, 128), has_prev), (edge, 256, 768, 1, both, has_prev)] + far
    return [(edge, 128, 640, 0, (128, 256), has_next), (edge, 384, 1152, 1, both, has_next)] + far


def logits_of(blocks, mine_q, cols):
    scores = []
    for source, row, _, level, seen, *there in blocks:
        score = mm(source[row:row + 128, cols], mine_q, NT) * LOG2
        if there:
            score = score + jnp.where(there[0], float(level), NEG)
        elif level:
            score = score + float(level)
        empty = jnp.full((128, 128), NEG, jnp.float32)
        if seen == (0, 128):
            score = jnp.concatenate([score[:, :128], empty], axis=1)
        if seen == (128, 256):
            score = jnp.concatenate([empty, score[:, 128:]], axis=1)
        scores.append(score)
    return scores


def gather(blocks, scores, top, value_cols):
    total = jnp.zeros((128, 256), jnp.float32)
    summed = jnp.zeros((128, 256), jnp.float32)
    for (source, row, *_), score in zip(blocks, scores):
        expd = jnp.exp2(score - top)
        total = total + expd
        summed = summed + mm(source[row:row + 128, value_cols], expd.astype(jnp.bfloat16), TN)
    return jnp.sum(total, axis=0, keepdims=True), summed


def top_of(scores):
    top = scores[0]
    for score in scores[1:]:
        top = jnp.maximum(top, score)
    return jnp.max(top, axis=0, keepdims=True)


def forward_own(queries, mine, _, tops, totals, sums, pooled):
    pooled[...] = mm(pool_matrix(256, 2), mine[...], NN).astype(jnp.bfloat16)
    width = queries.shape[1]
    for head in range(2):
        cols = slice(head * 128, head * 128 + 128)
        value_cols = slice(width + head * 128, width + head * 128 + 128)
        for half in range(2):
            span = slice(256 * half, 256 * half + 256)
            blocks = own_set(half, mine, pooled)
            scores = logits_of(blocks, queries[span, cols], cols)
            top = top_of(scores)
            tops[head:head + 1, span] = top
            totals[head:head + 1, span], sums[head * 128:head * 128 + 128, span] = gather(blocks, scores, top, value_cols)


def forward(queries, before, after, weight, tops, totals, sums,
            attention, lse, own, first_ahead, second_ahead, first_behind, edge):
    widen(before, after, edge)
    width = queries.shape[1]
    for head in range(2):
        cols = slice(head * 128, head * 128 + 128)
        value_cols = slice(width + head * 128, width + head * 128 + 128)
        for half in range(2):
            span = slice(256 * half, 256 * half + 256)
            blocks = edge_set(half, edge)
            scores = logits_of(blocks, queries[span, cols], cols)
            before_top = tops[head:head + 1, span]
            top = jnp.maximum(before_top, top_of(scores))
            total, summed = gather(blocks, scores, top, value_cols)
            scale = jnp.exp2(before_top - top)
            total = total + scale * totals[head:head + 1, span]
            lse[head:head + 1, span] = top + jnp.log2(total)
            result = ((summed + scale * sums[head * 128:head * 128 + 128, span]) / total).T
            attention[span, cols] = result.astype(jnp.bfloat16)
    heads = lax.axis_size("head")
    here = lax.axis_index("head")

    def partial_to(target):
        start = pl.multiple_of(lax.rem(target, heads) * width, width)
        return mm(attention[...], weight[pl.ds(start, width), :], NT)

    own[...] = partial_to(here).astype(jnp.bfloat16)
    step = step_ahead()
    first_ahead[...] = partial_to(here + 2).astype(jnp.bfloat16)
    second_ahead[...] = partial_to(here + step).astype(jnp.bfloat16)
    first_behind[...] = partial_to(here + heads - step).astype(jnp.bfloat16)


def step_ahead():
    return jnp.where(on_even(), 1, lax.axis_size("head") - 1)


def product_of(shift, cot, attention, weight, keep, send):
    heads = lax.axis_size("head")
    owner = lax.rem(lax.axis_index("head") + shift, heads)
    even = on_even()
    groups, rows, width = keep.shape
    each = groups // heads
    chunks = mm(cot[...], attention[...], TN).reshape(each, 2, rows, width)
    first, second = chunks[:, 0], chunks[:, 1]
    start = owner * each
    keep[pl.ds(start, each)] = jnp.where(even, first, second)
    send[pl.ds(start, each)] = jnp.where(even, second, first).astype(jnp.bfloat16)
    return mm(cot[...], weight[pl.ds(pl.multiple_of(owner * width, width), width), :], NN)


def near_products(mine, behind_cot, ahead_cot, attention, weight, keep, send, part):
    heads = lax.axis_size("head")
    step = step_ahead()
    part[...] = (product_of(0, mine, attention, weight, keep, send)
                 + product_of(heads - step, behind_cot, attention, weight, keep, send)
                 + product_of(step, ahead_cot, attention, weight, keep, send))


def far_products(opposite, attention, weight, near_keep, near_send, part, keep, send, grad_attention, deltas):
    keep[...] = near_keep[...]
    send[...] = near_send[...]
    rounded = (part[...] + product_of(2, opposite, attention, weight, keep, send)).astype(jnp.bfloat16)
    grad_attention[...] = rounded
    terms = rounded.astype(jnp.float32) * attention[...].astype(jnp.float32)
    high = terms.astype(jnp.bfloat16)
    low = (terms - high.astype(jnp.float32)).astype(jnp.bfloat16)
    ones = jnp.ones((16, HEAD_DIM), jnp.bfloat16)
    for head in range(2):
        cols = slice(head * HEAD_DIM, head * HEAD_DIM + HEAD_DIM)
        deltas[head:head + 1] = (mm(ones, high[:, cols], NT) + mm(ones, low[:, cols], NT))[0:1]


def pair_sum(keep, sibling, pairs, pairs_here, sems):
    stores = in_pieces(pairs_here, pairs, sems)
    size = pairs.shape[0] // len(stores)
    for number, store in enumerate(stores):
        span = pl.ds(number * size, size)
        pairs_here[span] = (keep[span] + sibling[span].astype(jnp.float32)).astype(jnp.bfloat16)
        store.start()
    for store in stores:
        store.wait()


def score_grads(blocks, scores, norm, delta, cot, value_cols):
    pairs = []
    for (source, row, *_), score in zip(blocks, scores):
        prob = jnp.exp2(score - norm)
        dprob = mm(source[row:row + 128, value_cols], cot, NT)
        pairs.append((prob.astype(jnp.bfloat16), (prob * (dprob - delta)).astype(jnp.bfloat16)))
    return pairs


def backward(queries, before, after, lse, grad_attention, deltas, second_ahead, from_behind, own, from_ahead,
             dscores, to_next, to_prev, edge, send_ahead, near, total):
    send_ahead[...] = (second_ahead[...].astype(jnp.float32) + from_behind[...].astype(jnp.float32)).astype(jnp.bfloat16)
    near[...] = own[...].astype(jnp.float32) + from_ahead[...].astype(jnp.float32)
    widen(before, after, edge)
    width = queries.shape[1]
    for half in range(2):
        span = slice(256 * half, 256 * half + 256)
        blocks = edge_set(half, edge)
        for head in range(2):
            cols = slice(head * 128, head * 128 + 128)
            value_cols = slice(width + head * 128, width + head * 128 + 128)
            mine_q = queries[span, cols]
            cot = grad_attention[span, cols]
            pairs = score_grads(blocks, logits_of(blocks, mine_q, cols), lse[head:head + 1, span],
                                deltas[head:head + 1, span], cot, value_cols)
            for number, ((_, _, at, *_), (prob, dscore)) in enumerate(zip(blocks, pairs)):
                dscores[2 * half + head, 128 * number:128 * number + 128] = dscore
                grad_k = mm(dscore, mine_q, NN) * SCALE
                grad_v = mm(prob, cot, NN)
                if half == 1 and at >= 1280:
                    total[at:at + 128, cols] += grad_k
                    total[at:at + 128, value_cols] += grad_v
                else:
                    total[at:at + 128, cols] = grad_k
                    total[at:at + 128, value_cols] = grad_v
    to_prev[0:128] = (total[0:128] + repeated(total[832:896] * 0.5, 2)
                      + repeated(total[1376:1408] * 0.25, 4)).astype(jnp.bfloat16)
    to_prev[128:192] = (total[768:832] * 0.5 + repeated(total[1344:1376] * 0.25, 2)).astype(jnp.bfloat16)
    to_prev[192:256] = (total[1280:1344] * 0.25).astype(jnp.bfloat16)
    to_next[0:128] = (total[640:768] + repeated(total[1152:1216] * 0.5, 2)
                      + repeated(total[1408:1440] * 0.25, 4)).astype(jnp.bfloat16)
    to_next[128:192] = (total[1216:1280] * 0.5 + repeated(total[1440:1472] * 0.25, 2)).astype(jnp.bfloat16)
    to_next[192:256] = (total[1472:1536] * 0.25).astype(jnp.bfloat16)


def own_grads(queries, mine, edge, lse, grad_attention, deltas, dscores,
              grad_queries, own, total, pooled, grad_q_here, sems):
    pooled[...] = mm(pool_matrix(256, 2), mine[...], NN).astype(jnp.bfloat16)
    stores = []
    width = queries.shape[1]
    for half in range(2):
        span = slice(256 * half, 256 * half + 256)
        blocks = own_set(half, mine, pooled)
        for head in range(2):
            cols = slice(head * 128, head * 128 + 128)
            value_cols = slice(width + head * 128, width + head * 128 + 128)
            mine_q = queries[span, cols]
            cot = grad_attention[span, cols]
            pairs = score_grads(blocks, logits_of(blocks, mine_q, cols), lse[head:head + 1, span],
                                deltas[head:head + 1, span], cot, value_cols)
            grad_q = jnp.zeros((128, 256), jnp.float32)
            for number, (source, row, *_) in enumerate(edge_set(half, edge)):
                grad_q = grad_q + mm(source[row:row + 128, cols], dscores[2 * half + head, 128 * number:128 * number + 128], TN)
            for (source, row, at, *_), (prob, dscore) in zip(blocks, pairs):
                grad_q = grad_q + mm(source[row:row + 128, cols], dscore, TN)
                grad_k = mm(dscore, mine_q, NN) * SCALE
                grad_v = mm(prob, cot, NN)
                if half == 1 and 256 <= at < 512:
                    total[at:at + 128, cols] += grad_k
                    total[at:at + 128, value_cols] += grad_v
                else:
                    total[at:at + 128, cols] = grad_k
                    total[at:at + 128, value_cols] = grad_v
            grad_q_here[span, cols] = (grad_q * SCALE).T.astype(jnp.bfloat16)
        store = pltpu.make_async_copy(grad_q_here.at[span], grad_queries.at[span], sems.at[half])
        store.start()
        stores.append(store)
    own[...] = (total[128:640] + repeated(total[896:1152] * 0.5, 2)).astype(jnp.bfloat16)
    for store in stores:
        store.wait()


def finish(near_out, last_behind, own, from_prev, from_next, spread,
           output, grad_keys, grad_values, grad_weight,
           output_here, grad_keys_here, grad_values_here, grad_weight_here, spread_here, load_sems, sems):
    loads = in_pieces(spread, spread_here, load_sems)
    for copy in loads:
        copy.start()
    width = grad_keys.shape[1]
    stores = []

    def store(source, target):
        copy = pltpu.make_async_copy(source, target, sems.at[len(stores)])
        copy.start()
        stores.append(copy)

    top, bottom = pl.ds(0, 256), pl.ds(256, 256)
    output_here[top] = (near_out[top] + last_behind[top].astype(jnp.float32)).astype(jnp.bfloat16)
    store(output_here.at[top], output.at[top])
    output_here[bottom] = (near_out[bottom] + last_behind[bottom].astype(jnp.float32)).astype(jnp.bfloat16)
    store(output_here.at[bottom], output.at[bottom])
    twice = repeat_matrix(64, 2)
    four = repeat_matrix(64, 4)
    coarse = mm(four, from_next[192:256], NN)
    low = mm(four, from_prev[192:256], NN)
    first = own[0:128].astype(jnp.float32) + coarse[0:128] + from_prev[0:128].astype(jnp.float32)
    second = own[128:256].astype(jnp.float32) + coarse[128:256] + mm(twice, from_prev[128:192], NN)
    third = own[256:384].astype(jnp.float32) + low[0:128] + mm(twice, from_next[128:192], NN)
    fourth = own[384:512].astype(jnp.float32) + low[128:256] + from_next[0:128].astype(jnp.float32)
    for number, part in enumerate((first, second, third, fourth)):
        span = pl.ds(128 * number, 128)
        part = part.astype(jnp.bfloat16)
        grad_keys_here[span] = part[:, :width]
        grad_values_here[span] = part[:, width:]
        if number % 2:
            half = pl.ds(128 * (number - 1), 256)
            store(grad_keys_here.at[half], grad_keys.at[half])
            store(grad_values_here.at[half], grad_values.at[half])
    for copy in loads:
        copy.wait()
    grad_weight_here[...] = jnp.sum(spread_here[...].astype(jnp.float32), axis=0)
    store(grad_weight_here, grad_weight)
    for copy in stores:
        copy.wait()


def local(queries, keys, values, out_weight, grad_out):
    bf16, f32 = jnp.bfloat16, jnp.float32
    rows, width = queries.shape
    shards = lax.axis_size("seq")
    heads = lax.axis_size("head")
    features = out_weight.shape[0]
    ahead = [(place * heads + head, place * heads + (head + (1 if place % 2 == 0 else heads - 1)) % heads)
             for place in range(shards) for head in range(heads)]
    behind = [(target, source) for source, target in ahead]
    swap = [(i, i ^ 1) for i in range(shards)]
    onward = [(i, (i + 1) % shards) for i in range(shards)]
    back = [(target, source) for source, target in onward]
    dma = pltpu.SemaphoreType.DMA

    behind_cot = lax.ppermute(grad_out, ("seq", "head"), ahead)
    ahead_cot = lax.ppermute(grad_out, ("seq", "head"), behind)

    mine, to_next, to_prev = run(
        prepare, (keys, values),
        [((512, 2 * width), bf16), ((256, 2 * width), bf16), ((256, 2 * width), bf16)],
        flops=2 * 384 * 512 * 512, moved=1 << 20)
    before = lax.ppermute(to_next, "seq", onward)
    after = lax.ppermute(to_prev, "seq", back)
    queries, out_weight = run(
        fetch, (queries, out_weight, to_next), [((rows, width), bf16), ((features, width), bf16)],
        moved=2 << 20, far_args=(2,))
    tops, totals, sums = run(
        forward_own, (queries, mine, to_next),
        [((2, rows), f32), ((2, rows), f32), ((2 * HEAD_DIM, rows), f32)],
        [pltpu.VMEM((256, 2 * width), bf16)], flops=10 ** 9, moved=2 << 20, far_args=(2,))
    opposite = lax.ppermute(behind_cot, ("seq", "head"), ahead)

    attention, lse, own_out, first_ahead, second_ahead, first_behind = run(
        forward, (queries, before, after, out_weight, tops, totals, sums),
        [((rows, width), bf16), ((2, rows), f32), ((rows, width), bf16), ((rows, width), bf16),
         ((rows, width), bf16), ((rows, width), bf16)],
        [pltpu.VMEM((768, 2 * width), bf16)], flops=10 ** 9, moved=3 << 20)
    from_behind = lax.ppermute(first_ahead, ("seq", "head"), ahead)
    from_ahead = lax.ppermute(first_behind, ("seq", "head"), behind)

    chunk = features // shards
    shapes = [((shards // 2, chunk, width), f32), ((shards // 2, chunk, width), bf16)]
    keep, send, part = run(
        near_products, (grad_out, behind_cot, ahead_cot, attention, out_weight), shapes + [((rows, width), f32)],
        flops=4 * 10 ** 8, moved=1 << 20)
    keep, send, grad_attention, deltas = run(
        far_products, (opposite, attention, out_weight, keep, send, part),
        shapes + [((rows, width), bf16), ((2, rows), f32)])
    half_sum = lax.ppermute(send, "seq", swap)
    pairs, = run(pair_sum, (keep, half_sum), [((shards // 2, chunk, width), bf16)],
                 [pltpu.VMEM((shards // 2, chunk, width), bf16), dma((PIECES,))], far_outs=(0,))
    groups = [list(range(core, shards, 2)) for core in range(2)]
    spread = lax.all_to_all(pairs, "seq", 0, 0, axis_index_groups=groups)

    dscores, to_next, to_prev, edge, send_ahead, near_out = run(
        backward,
        (queries, before, after, lse, grad_attention, deltas, second_ahead, from_behind, own_out, from_ahead),
        [((4, 512, 256), bf16), ((256, 2 * width), bf16), ((256, 2 * width), bf16), ((768, 2 * width), bf16),
         ((rows, width), bf16), ((rows, width), f32)],
        [pltpu.VMEM((1536, 2 * width), f32)], flops=2 * 10 ** 9, moved=4 << 20)
    last_behind = lax.ppermute(send_ahead, ("seq", "head"), ahead)
    grad_before = lax.ppermute(to_next, "seq", onward)
    grad_after = lax.ppermute(to_prev, "seq", back)
    grad_queries, own_grad = run(
        own_grads, (queries, mine, edge, lse, grad_attention, deltas, dscores),
        [((rows, width), bf16), ((rows, 2 * width), bf16)],
        [pltpu.VMEM((1536, 2 * width), f32), pltpu.VMEM((256, 2 * width), bf16), pltpu.VMEM((rows, width), bf16), dma((2,))],
        flops=3 * 10 ** 9, moved=6 << 20, far_outs=(0,))

    output, grad_keys, grad_values, grad_weight = run(
        finish,
        (near_out, last_behind, own_grad, grad_before, grad_after, spread),
        [((rows, width), bf16)] * 3 + [((chunk, width), f32)],
        [pltpu.VMEM((rows, width), bf16)] * 3 + [pltpu.VMEM((chunk, width), f32)]
        + [pltpu.VMEM((shards // 2, chunk, width), bf16), dma((PIECES,)), dma((7,))],
        moved=4 << 20, far_args=(5,), far_outs=(0, 1, 2, 3))
    return output, grad_queries, grad_keys, grad_values, grad_weight


def solution(mesh):
    split = P("seq", "head")
    return jax.shard_map(
        local, mesh=mesh, in_specs=(split, split, split, P(None, "head"), split),
        out_specs=(split,) * 5, check_vma=False)
```

```python
import math

import jax
import jax.numpy as jnp
from jax import lax
from jax.experimental import pallas as pl
from jax.experimental.pallas import tpu as pltpu
from jax.sharding import PartitionSpec as P

HEAD_DIM = 128
BLOCK = 128
SCALE = HEAD_DIM ** -0.5
LOG2 = SCALE / math.log(2.0)
NEG = -1e30
VMEM = pl.BlockSpec(memory_space=pltpu.VMEM)
FAR = pl.BlockSpec(memory_space=pl.ANY)
PIECES = 4
NT = (((1,), (1,)), ((), ()))
TN = (((0,), (0,)), ((), ()))
NN = (((1,), (0,)), ((), ()))


def mm(a, b, dims):
    return lax.dot_general(a, b, dims, preferred_element_type=jnp.float32)


def run(body, args, outs, scratch=(), flops=0, moved=0, far_args=(), far_outs=(), room=24):
    return pl.pallas_call(
        body,
        in_specs=[FAR if number in far_args else VMEM for number in range(len(args))],
        out_shape=[jax.ShapeDtypeStruct(shape, kind) for shape, kind in outs],
        out_specs=[FAR if number in far_outs else VMEM for number in range(len(outs))],
        scratch_shapes=list(scratch),
        cost_estimate=pl.CostEstimate(flops=flops, bytes_accessed=moved, transcendentals=0),
        compiler_params=pltpu.CompilerParams(vmem_limit_bytes=room * 1024 * 1024),
    )(*args)


def pool_matrix(rows, factor):
    row = lax.broadcasted_iota(jnp.int32, (rows, rows * factor), 0)
    col = lax.broadcasted_iota(jnp.int32, (rows, rows * factor), 1)
    inside = (col >= row * factor) & (col < row * factor + factor)
    return jnp.where(inside, 1.0 / factor, 0.0).astype(jnp.bfloat16)


def repeat_matrix(rows, factor):
    row = lax.broadcasted_iota(jnp.int32, (rows * factor, rows), 0)
    col = lax.broadcasted_iota(jnp.int32, (rows * factor, rows), 1)
    inside = (row >= col * factor) & (row < col * factor + factor)
    return jnp.where(inside, 1.0, 0.0).astype(jnp.bfloat16)


def repeated(part, factor):
    matrix = repeat_matrix(part.shape[0], factor)
    high = part.astype(jnp.bfloat16)
    low = (part - high.astype(jnp.float32)).astype(jnp.bfloat16)
    return mm(matrix, high, NN) + mm(matrix, low, NN)


def in_pieces(source, target, sems):
    count = sems.shape[0]
    size = source.shape[0] // count
    return [pltpu.make_async_copy(source.at[pl.ds(number * size, size)], target.at[pl.ds(number * size, size)],
                                  sems.at[number]) for number in range(count)]


def on_even():
    return lax.rem(lax.axis_index("seq"), 2) == 0


def prepare(keys, values, mine, to_next, to_prev):
    width = keys.shape[1]
    two = pool_matrix(256, 2)
    four = pool_matrix(64, 4)
    for number, source in enumerate((keys, values)):
        cols = slice(number * width, (number + 1) * width)
        mine[:, cols] = source[...]
        first = mm(two, source[...], NN).astype(jnp.bfloat16)
        to_next[0:128, cols] = source[384:512]
        to_next[128:192, cols] = first[128:192]
        to_next[192:256, cols] = mm(four, source[0:256], NN).astype(jnp.bfloat16)
        to_prev[0:128, cols] = source[0:128]
        to_prev[128:192, cols] = first[64:128]
        to_prev[192:256, cols] = mm(four, source[256:512], NN).astype(jnp.bfloat16)


def fetch(queries, weight, _, queries_here, weight_here):
    queries_here[...] = queries[...]
    weight_here[...] = weight[...]


def widen(before, after, edge):
    half = pool_matrix(64, 2)
    both = pool_matrix(32, 2)
    quarter = pool_matrix(32, 4)
    edge[0:128] = before[0:128]
    edge[128:256] = after[0:128]
    edge[256:320] = before[128:192]
    edge[320:384] = mm(half, before[0:128], NN).astype(jnp.bfloat16)
    edge[384:448] = mm(half, after[0:128], NN).astype(jnp.bfloat16)
    edge[448:512] = after[128:192]
    edge[512:576] = before[192:256]
    edge[576:608] = mm(both, before[128:192], NN).astype(jnp.bfloat16)
    edge[608:640] = mm(quarter, before[0:128], NN).astype(jnp.bfloat16)
    edge[640:672] = mm(quarter, after[0:128], NN).astype(jnp.bfloat16)
    edge[672:704] = mm(both, after[128:192], NN).astype(jnp.bfloat16)
    edge[704:768] = after[192:256]


def own_set(half, mine, pooled):
    both = (0, 256)
    if half == 0:
        return [(mine, 0, 128, 0, both), (mine, 128, 256, 0, both), (mine, 256, 384, 0, (128, 256)), (pooled, 128, 1024, 1, both)]
    return [(mine, 128, 256, 0, (0, 128)), (mine, 256, 384, 0, both), (mine, 384, 512, 0, both), (pooled, 0, 896, 1, both)]


def edge_set(half, edge):
    place = lax.axis_index("seq")
    has_prev = place > 0
    has_next = place < lax.axis_size("seq") - 1
    both = (0, 256)
    far = [(edge, 512, 1280, 2, both, has_prev), (edge, 640, 1408, 2, both, has_next)]
    if half == 0:
        return [(edge, 0, 0, 0, (0, 128), has_prev), (edge, 256, 768, 1, both, has_prev)] + far
    return [(edge, 128, 640, 0, (128, 256), has_next), (edge, 384, 1152, 1, both, has_next)] + far


def logits_of(blocks, mine_q, cols):
    scores = []
    for source, row, _, level, seen, *there in blocks:
        score = mm(source[row:row + 128, cols], mine_q, NT) * LOG2
        if there:
            score = score + jnp.where(there[0], float(level), NEG)
        elif level:
            score = score + float(level)
        empty = jnp.full((128, 128), NEG, jnp.float32)
        if seen == (0, 128):
            score = jnp.concatenate([score[:, :128], empty], axis=1)
        if seen == (128, 256):
            score = jnp.concatenate([empty, score[:, 128:]], axis=1)
        scores.append(score)
    return scores


def gather(blocks, scores, top, value_cols):
    total = jnp.zeros((128, 256), jnp.float32)
    summed = jnp.zeros((128, 256), jnp.float32)
    for (source, row, *_), score in zip(blocks, scores):
        expd = jnp.exp2(score - top)
        total = total + expd
        summed = summed + mm(source[row:row + 128, value_cols], expd.astype(jnp.bfloat16), TN)
    return jnp.sum(total, axis=0, keepdims=True), summed


def top_of(scores):
    top = scores[0]
    for score in scores[1:]:
        top = jnp.maximum(top, score)
    return jnp.max(top, axis=0, keepdims=True)


def forward_own(queries, mine, _, tops, totals, sums, pooled):
    pooled[...] = mm(pool_matrix(256, 2), mine[...], NN).astype(jnp.bfloat16)
    width = queries.shape[1]
    for head in range(2):
        cols = slice(head * 128, head * 128 + 128)
        value_cols = slice(width + head * 128, width + head * 128 + 128)
        for half in range(2):
            span = slice(256 * half, 256 * half + 256)
            blocks = own_set(half, mine, pooled)
            scores = logits_of(blocks, queries[span, cols], cols)
            top = top_of(scores)
            tops[head:head + 1, span] = top
            totals[head:head + 1, span], sums[head * 128:head * 128 + 128, span] = gather(blocks, scores, top, value_cols)


def forward(queries, before, after, weight, tops, totals, sums,
            attention, lse, own, first_up, second_up, first_down, edge):
    widen(before, after, edge)
    width = queries.shape[1]
    for head in range(2):
        cols = slice(head * 128, head * 128 + 128)
        value_cols = slice(width + head * 128, width + head * 128 + 128)
        for half in range(2):
            span = slice(256 * half, 256 * half + 256)
            blocks = edge_set(half, edge)
            scores = logits_of(blocks, queries[span, cols], cols)
            before_top = tops[head:head + 1, span]
            top = jnp.maximum(before_top, top_of(scores))
            total, summed = gather(blocks, scores, top, value_cols)
            scale = jnp.exp2(before_top - top)
            total = total + scale * totals[head:head + 1, span]
            lse[head:head + 1, span] = top + jnp.log2(total)
            result = ((summed + scale * sums[head * 128:head * 128 + 128, span]) / total).T
            attention[span, cols] = result.astype(jnp.bfloat16)
    heads = lax.axis_size("head")
    here = lax.axis_index("head")

    def partial_to(target):
        start = pl.multiple_of(lax.rem(target, heads) * width, width)
        return mm(attention[...], weight[pl.ds(start, width), :], NT)

    own[...] = partial_to(here).astype(jnp.bfloat16)
    first_up[...] = partial_to(here + 2).astype(jnp.bfloat16)
    second_up[...] = partial_to(here + 1).astype(jnp.bfloat16)
    first_down[...] = partial_to(here + 3).astype(jnp.bfloat16)


def owner_of(shift):
    return lax.rem(lax.axis_index("head") + shift, lax.axis_size("head"))


def product_of(shift, place, cot, attention, weight, keep, send):
    even = on_even()
    rows, width = keep.shape[1:]
    each = cot.shape[1] // (2 * rows)
    chunks = mm(cot[...], attention[...], TN).reshape(each, 2, rows, width)
    first, second = chunks[:, 0], chunks[:, 1]
    span = slice(place * each, place * each + each)
    keep[span] = jnp.where(even, first, second)
    send[span] = jnp.where(even, second, first).astype(jnp.bfloat16)
    return mm(cot[...], weight[pl.ds(pl.multiple_of(owner_of(shift) * width, width), width), :], NN)


def near_products(mine, below, above, attention, weight, keep, send, part):
    heads = lax.axis_size("head")
    part[...] = (product_of(0, 0, mine, attention, weight, keep, send)
                 + product_of(heads - 1, 1, below, attention, weight, keep, send)
                 + product_of(1, 2, above, attention, weight, keep, send))


def far_products(opposite, attention, weight, part, keep, send, grad_attention, deltas):
    rounded = (part[...] + product_of(2, 0, opposite, attention, weight, keep, send)).astype(jnp.bfloat16)
    grad_attention[...] = rounded
    terms = rounded.astype(jnp.float32) * attention[...].astype(jnp.float32)
    high = terms.astype(jnp.bfloat16)
    low = (terms - high.astype(jnp.float32)).astype(jnp.bfloat16)
    ones = jnp.ones((16, HEAD_DIM), jnp.bfloat16)
    for head in range(2):
        cols = slice(head * HEAD_DIM, head * HEAD_DIM + HEAD_DIM)
        deltas[head:head + 1] = (mm(ones, high[:, cols], NT) + mm(ones, low[:, cols], NT))[0:1]


def pair_sum(near_keep, near_sibling, far_keep, far_sibling, pairs, pairs_here, sems):
    heads = lax.axis_size("head")
    each = far_keep.shape[0]
    stores = []
    for place, shift in enumerate((0, heads - 1, 1, 2)):
        keep, sibling = (near_keep, near_sibling) if place < 3 else (far_keep, far_sibling)
        source = pl.ds(place * each if place < 3 else 0, each)
        target = pl.ds(owner_of(shift) * each, each)
        pairs_here[target] = (keep[source] + sibling[source].astype(jnp.float32)).astype(jnp.bfloat16)
        stores.append(pltpu.make_async_copy(pairs_here.at[target], pairs.at[target], sems.at[place]))
        stores[-1].start()
    for store in stores:
        store.wait()


def score_grads(blocks, scores, norm, delta, cot, value_cols):
    pairs = []
    for (source, row, *_), score in zip(blocks, scores):
        prob = jnp.exp2(score - norm)
        dprob = mm(source[row:row + 128, value_cols], cot, NT)
        pairs.append((prob.astype(jnp.bfloat16), (prob * (dprob - delta)).astype(jnp.bfloat16)))
    return pairs


def backward(queries, before, after, lse, grad_attention, deltas, second_up, from_below, own, from_above,
             dscores, to_next, to_prev, edge, send_up, near, total):
    send_up[...] = (second_up[...].astype(jnp.float32) + from_below[...].astype(jnp.float32)).astype(jnp.bfloat16)
    near[...] = own[...].astype(jnp.float32) + from_above[...].astype(jnp.float32)
    widen(before, after, edge)
    width = queries.shape[1]
    for half in range(2):
        span = slice(256 * half, 256 * half + 256)
        blocks = edge_set(half, edge)
        for head in range(2):
            cols = slice(head * 128, head * 128 + 128)
            value_cols = slice(width + head * 128, width + head * 128 + 128)
            mine_q = queries[span, cols]
            cot = grad_attention[span, cols]
            pairs = score_grads(blocks, logits_of(blocks, mine_q, cols), lse[head:head + 1, span],
                                deltas[head:head + 1, span], cot, value_cols)
            for number, ((_, _, at, *_), (prob, dscore)) in enumerate(zip(blocks, pairs)):
                dscores[2 * half + head, 128 * number:128 * number + 128] = dscore
                grad_k = mm(dscore, mine_q, NN) * SCALE
                grad_v = mm(prob, cot, NN)
                if half == 1 and at >= 1280:
                    total[at:at + 128, cols] += grad_k
                    total[at:at + 128, value_cols] += grad_v
                else:
                    total[at:at + 128, cols] = grad_k
                    total[at:at + 128, value_cols] = grad_v
    to_prev[0:128] = (total[0:128] + repeated(total[832:896] * 0.5, 2)
                      + repeated(total[1376:1408] * 0.25, 4)).astype(jnp.bfloat16)
    to_prev[128:192] = (total[768:832] * 0.5 + repeated(total[1344:1376] * 0.25, 2)).astype(jnp.bfloat16)
    to_prev[192:256] = (total[1280:1344] * 0.25).astype(jnp.bfloat16)
    to_next[0:128] = (total[640:768] + repeated(total[1152:1216] * 0.5, 2)
                      + repeated(total[1408:1440] * 0.25, 4)).astype(jnp.bfloat16)
    to_next[128:192] = (total[1216:1280] * 0.5 + repeated(total[1440:1472] * 0.25, 2)).astype(jnp.bfloat16)
    to_next[192:256] = (total[1472:1536] * 0.25).astype(jnp.bfloat16)


def own_grads(queries, mine, edge, lse, grad_attention, deltas, dscores,
              grad_queries, own, total, pooled, grad_q_here, sems):
    pooled[...] = mm(pool_matrix(256, 2), mine[...], NN).astype(jnp.bfloat16)
    stores = []
    width = queries.shape[1]
    for half in range(2):
        span = slice(256 * half, 256 * half + 256)
        blocks = own_set(half, mine, pooled)
        for head in range(2):
            cols = slice(head * 128, head * 128 + 128)
            value_cols = slice(width + head * 128, width + head * 128 + 128)
            mine_q = queries[span, cols]
            cot = grad_attention[span, cols]
            pairs = score_grads(blocks, logits_of(blocks, mine_q, cols), lse[head:head + 1, span],
                                deltas[head:head + 1, span], cot, value_cols)
            grad_q = jnp.zeros((128, 256), jnp.float32)
            for number, (source, row, *_) in enumerate(edge_set(half, edge)):
                grad_q = grad_q + mm(source[row:row + 128, cols], dscores[2 * half + head, 128 * number:128 * number + 128], TN)
            for (source, row, at, *_), (prob, dscore) in zip(blocks, pairs):
                grad_q = grad_q + mm(source[row:row + 128, cols], dscore, TN)
                grad_k = mm(dscore, mine_q, NN) * SCALE
                grad_v = mm(prob, cot, NN)
                if half == 1 and 256 <= at < 512:
                    total[at:at + 128, cols] += grad_k
                    total[at:at + 128, value_cols] += grad_v
                else:
                    total[at:at + 128, cols] = grad_k
                    total[at:at + 128, value_cols] = grad_v
            grad_q_here[span, cols] = (grad_q * SCALE).T.astype(jnp.bfloat16)
        store = pltpu.make_async_copy(grad_q_here.at[span], grad_queries.at[span], sems.at[half])
        store.start()
        stores.append(store)
    own[...] = (total[128:640] + repeated(total[896:1152] * 0.5, 2)).astype(jnp.bfloat16)
    for store in stores:
        store.wait()


def finish(near_out, last_below, own, from_prev, from_next, spread,
           output, grad_keys, grad_values, grad_weight,
           output_here, grad_keys_here, grad_values_here, grad_weight_here, spread_here, load_sems, sems):
    loads = in_pieces(spread, spread_here, load_sems)
    for copy in loads:
        copy.start()
    width = grad_keys.shape[1]
    stores = []

    def store(source, target):
        copy = pltpu.make_async_copy(source, target, sems.at[len(stores)])
        copy.start()
        stores.append(copy)

    top, bottom = pl.ds(0, 256), pl.ds(256, 256)
    output_here[top] = (near_out[top] + last_below[top].astype(jnp.float32)).astype(jnp.bfloat16)
    store(output_here.at[top], output.at[top])
    output_here[bottom] = (near_out[bottom] + last_below[bottom].astype(jnp.float32)).astype(jnp.bfloat16)
    store(output_here.at[bottom], output.at[bottom])
    twice = repeat_matrix(64, 2)
    four = repeat_matrix(64, 4)
    coarse = mm(four, from_next[192:256], NN)
    low = mm(four, from_prev[192:256], NN)
    first = own[0:128].astype(jnp.float32) + coarse[0:128] + from_prev[0:128].astype(jnp.float32)
    second = own[128:256].astype(jnp.float32) + coarse[128:256] + mm(twice, from_prev[128:192], NN)
    third = own[256:384].astype(jnp.float32) + low[0:128] + mm(twice, from_next[128:192], NN)
    fourth = own[384:512].astype(jnp.float32) + low[128:256] + from_next[0:128].astype(jnp.float32)
    for number, part in enumerate((first, second, third, fourth)):
        span = pl.ds(128 * number, 128)
        part = part.astype(jnp.bfloat16)
        grad_keys_here[span] = part[:, :width]
        grad_values_here[span] = part[:, width:]
        if number % 2:
            half = pl.ds(128 * (number - 1), 256)
            store(grad_keys_here.at[half], grad_keys.at[half])
            store(grad_values_here.at[half], grad_values.at[half])
    for copy in loads:
        copy.wait()
    grad_weight_here[...] = jnp.sum(spread_here[...].astype(jnp.float32), axis=0)
    store(grad_weight_here, grad_weight)
    for copy in stores:
        copy.wait()


def local(queries, keys, values, out_weight, grad_out):
    bf16, f32 = jnp.bfloat16, jnp.float32
    rows, width = queries.shape
    shards = lax.axis_size("seq")
    heads = lax.axis_size("head")
    features = out_weight.shape[0]
    up = [(i, (i + 1) % heads) for i in range(heads)]
    down = [(target, source) for source, target in up]
    swap = [(i, i ^ 1) for i in range(shards)]
    onward = [(i, (i + 1) % shards) for i in range(shards)]
    back = [(target, source) for source, target in onward]
    dma = pltpu.SemaphoreType.DMA

    below = lax.ppermute(grad_out, "head", up)
    above = lax.ppermute(grad_out, "head", down)

    mine, to_next, to_prev = run(
        prepare, (keys, values),
        [((512, 2 * width), bf16), ((256, 2 * width), bf16), ((256, 2 * width), bf16)],
        flops=2 * 384 * 512 * 512, moved=1 << 20)
    before = lax.ppermute(to_next, "seq", onward)
    after = lax.ppermute(to_prev, "seq", back)
    queries, out_weight = run(
        fetch, (queries, out_weight, to_next), [((rows, width), bf16), ((features, width), bf16)],
        moved=2 << 20, far_args=(2,))
    tops, totals, sums = run(
        forward_own, (queries, mine, to_next),
        [((2, rows), f32), ((2, rows), f32), ((2 * HEAD_DIM, rows), f32)],
        [pltpu.VMEM((256, 2 * width), bf16)], flops=10 ** 9, moved=2 << 20, far_args=(2,))
    opposite = lax.ppermute(below, "head", up)

    attention, lse, own_out, first_up, second_up, first_down = run(
        forward, (queries, before, after, out_weight, tops, totals, sums),
        [((rows, width), bf16), ((2, rows), f32), ((rows, width), bf16), ((rows, width), bf16),
         ((rows, width), bf16), ((rows, width), bf16)],
        [pltpu.VMEM((768, 2 * width), bf16)], flops=10 ** 9, moved=3 << 20)
    from_below = lax.ppermute(first_up, "head", up)
    from_above = lax.ppermute(first_down, "head", down)

    chunk = features // shards
    each = shards // 2 // heads
    near_keep, near_send, part = run(
        near_products, (grad_out, below, above, attention, out_weight),
        [((3 * each, chunk, width), f32), ((3 * each, chunk, width), bf16), ((rows, width), f32)],
        flops=4 * 10 ** 8, moved=1 << 20)
    near_sum = lax.ppermute(near_send, "seq", swap)
    far_keep, far_send, grad_attention, deltas = run(
        far_products, (opposite, attention, out_weight, part),
        [((each, chunk, width), f32), ((each, chunk, width), bf16), ((rows, width), bf16), ((2, rows), f32)])
    far_sum = lax.ppermute(far_send, "seq", swap)
    pairs, = run(pair_sum, (near_keep, near_sum, far_keep, far_sum), [((shards // 2, chunk, width), bf16)],
                 [pltpu.VMEM((shards // 2, chunk, width), bf16), dma((4,))], far_outs=(0,))
    groups = [list(range(core, shards, 2)) for core in range(2)]
    spread = lax.all_to_all(pairs, "seq", 0, 0, axis_index_groups=groups)

    dscores, to_next, to_prev, edge, send_up, near_out = run(
        backward,
        (queries, before, after, lse, grad_attention, deltas, second_up, from_below, own_out, from_above),
        [((4, 512, 256), bf16), ((256, 2 * width), bf16), ((256, 2 * width), bf16), ((768, 2 * width), bf16),
         ((rows, width), bf16), ((rows, width), f32)],
        [pltpu.VMEM((1536, 2 * width), f32)], flops=2 * 10 ** 9, moved=4 << 20)
    last_below = lax.ppermute(send_up, "head", up)
    grad_before = lax.ppermute(to_next, "seq", onward)
    grad_after = lax.ppermute(to_prev, "seq", back)
    grad_queries, own_grad = run(
        own_grads, (queries, mine, edge, lse, grad_attention, deltas, dscores),
        [((rows, width), bf16), ((rows, 2 * width), bf16)],
        [pltpu.VMEM((1536, 2 * width), f32), pltpu.VMEM((256, 2 * width), bf16), pltpu.VMEM((rows, width), bf16), dma((2,))],
        flops=3 * 10 ** 9, moved=6 << 20, far_outs=(0,))

    output, grad_keys, grad_values, grad_weight = run(
        finish,
        (near_out, last_below, own_grad, grad_before, grad_after, spread),
        [((rows, width), bf16)] * 3 + [((chunk, width), f32)],
        [pltpu.VMEM((rows, width), bf16)] * 3 + [pltpu.VMEM((chunk, width), f32)]
        + [pltpu.VMEM((shards // 2, chunk, width), bf16), dma((PIECES,)), dma((7,))],
        moved=4 << 20, far_args=(5,), far_outs=(0, 1, 2, 3))
    return output, grad_queries, grad_keys, grad_values, grad_weight


def solution(mesh):
    split = P("seq", "head")
    return jax.shard_map(
        local, mesh=mesh, in_specs=(split, split, split, P(None, "head"), split),
        out_specs=(split,) * 5, check_vma=False)
```

```python
import math

import jax
import jax.numpy as jnp
from jax import lax
from jax.experimental import pallas as pl
from jax.experimental.pallas import tpu as pltpu
from jax.sharding import PartitionSpec as P

HEAD_DIM = 128
BLOCK = 128
SCALE = HEAD_DIM ** -0.5
LOG2 = SCALE / math.log(2.0)
NEG = -1e30
VMEM = pl.BlockSpec(memory_space=pltpu.VMEM)
FAR = pl.BlockSpec(memory_space=pl.ANY)
PIECES = 4
NT = (((1,), (1,)), ((), ()))
TN = (((0,), (0,)), ((), ()))
NN = (((1,), (0,)), ((), ()))


def mm(a, b, dims):
    return lax.dot_general(a, b, dims, preferred_element_type=jnp.float32)


def run(body, args, outs, scratch=(), flops=0, moved=0, far_args=(), far_outs=(), room=24):
    return pl.pallas_call(
        body,
        in_specs=[FAR if number in far_args else VMEM for number in range(len(args))],
        out_shape=[jax.ShapeDtypeStruct(shape, kind) for shape, kind in outs],
        out_specs=[FAR if number in far_outs else VMEM for number in range(len(outs))],
        scratch_shapes=list(scratch),
        cost_estimate=pl.CostEstimate(flops=flops, bytes_accessed=moved, transcendentals=0),
        compiler_params=pltpu.CompilerParams(vmem_limit_bytes=room * 1024 * 1024),
    )(*args)


def pool_matrix(rows, factor):
    row = lax.broadcasted_iota(jnp.int32, (rows, rows * factor), 0)
    col = lax.broadcasted_iota(jnp.int32, (rows, rows * factor), 1)
    inside = (col >= row * factor) & (col < row * factor + factor)
    return jnp.where(inside, 1.0 / factor, 0.0).astype(jnp.bfloat16)


def repeat_matrix(rows, factor):
    row = lax.broadcasted_iota(jnp.int32, (rows * factor, rows), 0)
    col = lax.broadcasted_iota(jnp.int32, (rows * factor, rows), 1)
    inside = (row >= col * factor) & (row < col * factor + factor)
    return jnp.where(inside, 1.0, 0.0).astype(jnp.bfloat16)


def repeated(part, factor):
    matrix = repeat_matrix(part.shape[0], factor)
    high = part.astype(jnp.bfloat16)
    low = (part - high.astype(jnp.float32)).astype(jnp.bfloat16)
    return mm(matrix, high, NN) + mm(matrix, low, NN)


def in_pieces(source, target, sems):
    count = sems.shape[0]
    size = source.shape[0] // count
    return [pltpu.make_async_copy(source.at[pl.ds(number * size, size)], target.at[pl.ds(number * size, size)],
                                  sems.at[number]) for number in range(count)]


def on_even():
    return lax.rem(lax.axis_index("seq"), 2) == 0


def prepare(keys, values, mine, to_next, to_prev):
    width = keys.shape[1]
    two = pool_matrix(256, 2)
    four = pool_matrix(64, 4)
    for number, source in enumerate((keys, values)):
        cols = slice(number * width, (number + 1) * width)
        mine[:, cols] = source[...]
        first = mm(two, source[...], NN).astype(jnp.bfloat16)
        to_next[0:128, cols] = source[384:512]
        to_next[128:192, cols] = first[128:192]
        to_next[192:256, cols] = mm(four, source[0:256], NN).astype(jnp.bfloat16)
        to_prev[0:128, cols] = source[0:128]
        to_prev[128:192, cols] = first[64:128]
        to_prev[192:256, cols] = mm(four, source[256:512], NN).astype(jnp.bfloat16)


def fetch(queries, weight, _, queries_here, weight_here):
    queries_here[...] = queries[...]
    weight_here[...] = weight[...]


def widen(before, after, edge):
    half = pool_matrix(64, 2)
    both = pool_matrix(32, 2)
    quarter = pool_matrix(32, 4)
    edge[0:128] = before[0:128]
    edge[128:256] = after[0:128]
    edge[256:320] = before[128:192]
    edge[320:384] = mm(half, before[0:128], NN).astype(jnp.bfloat16)
    edge[384:448] = mm(half, after[0:128], NN).astype(jnp.bfloat16)
    edge[448:512] = after[128:192]
    edge[512:576] = before[192:256]
    edge[576:608] = mm(both, before[128:192], NN).astype(jnp.bfloat16)
    edge[608:640] = mm(quarter, before[0:128], NN).astype(jnp.bfloat16)
    edge[640:672] = mm(quarter, after[0:128], NN).astype(jnp.bfloat16)
    edge[672:704] = mm(both, after[128:192], NN).astype(jnp.bfloat16)
    edge[704:768] = after[192:256]


def own_set(half, mine, pooled):
    both = (0, 256)
    if half == 0:
        return [(mine, 0, 128, 0, both), (mine, 128, 256, 0, both), (mine, 256, 384, 0, (128, 256)), (pooled, 128, 1024, 1, both)]
    return [(mine, 128, 256, 0, (0, 128)), (mine, 256, 384, 0, both), (mine, 384, 512, 0, both), (pooled, 0, 896, 1, both)]


def edge_set(half, edge):
    place = lax.axis_index("seq")
    has_prev = place > 0
    has_next = place < lax.axis_size("seq") - 1
    both = (0, 256)
    far = [(edge, 512, 1280, 2, both, has_prev), (edge, 640, 1408, 2, both, has_next)]
    if half == 0:
        return [(edge, 0, 0, 0, (0, 128), has_prev), (edge, 256, 768, 1, both, has_prev)] + far
    return [(edge, 128, 640, 0, (128, 256), has_next), (edge, 384, 1152, 1, both, has_next)] + far


def logits_of(blocks, mine_q, cols):
    scores = []
    for source, row, _, level, seen, *there in blocks:
        score = mm(source[row:row + 128, cols], mine_q, NT) * LOG2
        if there:
            score = score + jnp.where(there[0], float(level), NEG)
        elif level:
            score = score + float(level)
        empty = jnp.full((128, 128), NEG, jnp.float32)
        if seen == (0, 128):
            score = jnp.concatenate([score[:, :128], empty], axis=1)
        if seen == (128, 256):
            score = jnp.concatenate([empty, score[:, 128:]], axis=1)
        scores.append(score)
    return scores


def gather(blocks, scores, top, value_cols):
    total = jnp.zeros((128, 256), jnp.float32)
    summed = jnp.zeros((128, 256), jnp.float32)
    for (source, row, *_), score in zip(blocks, scores):
        expd = jnp.exp2(score - top)
        total = total + expd
        summed = summed + mm(source[row:row + 128, value_cols], expd.astype(jnp.bfloat16), TN)
    return jnp.sum(total, axis=0, keepdims=True), summed


def top_of(scores):
    top = scores[0]
    for score in scores[1:]:
        top = jnp.maximum(top, score)
    return jnp.max(top, axis=0, keepdims=True)


def forward_own(queries, mine, _, tops, totals, sums, pooled):
    pooled[...] = mm(pool_matrix(256, 2), mine[...], NN).astype(jnp.bfloat16)
    width = queries.shape[1]
    for head in range(2):
        cols = slice(head * 128, head * 128 + 128)
        value_cols = slice(width + head * 128, width + head * 128 + 128)
        for half in range(2):
            span = slice(256 * half, 256 * half + 256)
            blocks = own_set(half, mine, pooled)
            scores = logits_of(blocks, queries[span, cols], cols)
            top = top_of(scores)
            tops[head:head + 1, span] = top
            totals[head:head + 1, span], sums[head * 128:head * 128 + 128, span] = gather(blocks, scores, top, value_cols)


def forward(queries, before, after, weight, tops, totals, sums,
            attention, lse, own, first_ahead, second_ahead, first_behind, edge):
    widen(before, after, edge)
    width = queries.shape[1]
    for head in range(2):
        cols = slice(head * 128, head * 128 + 128)
        value_cols = slice(width + head * 128, width + head * 128 + 128)
        for half in range(2):
            span = slice(256 * half, 256 * half + 256)
            blocks = edge_set(half, edge)
            scores = logits_of(blocks, queries[span, cols], cols)
            before_top = tops[head:head + 1, span]
            top = jnp.maximum(before_top, top_of(scores))
            total, summed = gather(blocks, scores, top, value_cols)
            scale = jnp.exp2(before_top - top)
            total = total + scale * totals[head:head + 1, span]
            lse[head:head + 1, span] = top + jnp.log2(total)
            result = ((summed + scale * sums[head * 128:head * 128 + 128, span]) / total).T
            attention[span, cols] = result.astype(jnp.bfloat16)
    heads = lax.axis_size("head")
    here = lax.axis_index("head")

    def partial_to(target):
        start = pl.multiple_of(lax.rem(target, heads) * width, width)
        return mm(attention[...], weight[pl.ds(start, width), :], NT)

    own[...] = partial_to(here).astype(jnp.bfloat16)
    first_ahead[...] = partial_to(here + 2).astype(jnp.bfloat16)
    second_ahead[...] = partial_to(here + heads - 1).astype(jnp.bfloat16)
    first_behind[...] = partial_to(here + 1).astype(jnp.bfloat16)


def product_of(shift, cot, attention, weight, keep, send):
    heads = lax.axis_size("head")
    owner = lax.rem(lax.axis_index("head") + shift, heads)
    even = on_even()
    groups, rows, width = keep.shape
    each = groups // heads
    chunks = mm(cot[...], attention[...], TN).reshape(each, 2, rows, width)
    first, second = chunks[:, 0], chunks[:, 1]
    start = owner * each
    keep[pl.ds(start, each)] = jnp.where(even, first, second)
    send[pl.ds(start, each)] = jnp.where(even, second, first).astype(jnp.bfloat16)
    return mm(cot[...], weight[pl.ds(pl.multiple_of(owner * width, width), width), :], NN)


def near_products(mine, behind_cot, ahead_cot, attention, weight, keep, send, part):
    heads = lax.axis_size("head")
    part[...] = (product_of(0, mine, attention, weight, keep, send)
                 + product_of(1, behind_cot, attention, weight, keep, send)
                 + product_of(heads - 1, ahead_cot, attention, weight, keep, send))


def far_products(opposite, attention, weight, near_keep, near_send, part, keep, send, grad_attention, deltas):
    keep[...] = near_keep[...]
    send[...] = near_send[...]
    rounded = (part[...] + product_of(2, opposite, attention, weight, keep, send)).astype(jnp.bfloat16)
    grad_attention[...] = rounded
    terms = rounded.astype(jnp.float32) * attention[...].astype(jnp.float32)
    high = terms.astype(jnp.bfloat16)
    low = (terms - high.astype(jnp.float32)).astype(jnp.bfloat16)
    ones = jnp.ones((16, HEAD_DIM), jnp.bfloat16)
    for head in range(2):
        cols = slice(head * HEAD_DIM, head * HEAD_DIM + HEAD_DIM)
        deltas[head:head + 1] = (mm(ones, high[:, cols], NT) + mm(ones, low[:, cols], NT))[0:1]


def pair_sum(keep, sibling, pairs, pairs_here, sems):
    stores = in_pieces(pairs_here, pairs, sems)
    size = pairs.shape[0] // len(stores)
    for number, store in enumerate(stores):
        span = pl.ds(number * size, size)
        pairs_here[span] = (keep[span] + sibling[span].astype(jnp.float32)).astype(jnp.bfloat16)
        store.start()
    for store in stores:
        store.wait()


def score_grads(blocks, scores, norm, delta, cot, value_cols):
    pairs = []
    for (source, row, *_), score in zip(blocks, scores):
        prob = jnp.exp2(score - norm)
        dprob = mm(source[row:row + 128, value_cols], cot, NT)
        pairs.append((prob.astype(jnp.bfloat16), (prob * (dprob - delta)).astype(jnp.bfloat16)))
    return pairs


def backward(queries, before, after, lse, grad_attention, deltas, second_ahead, from_behind, own, from_ahead,
             dscores, to_next, to_prev, edge, send_ahead, near, total):
    send_ahead[...] = (second_ahead[...].astype(jnp.float32) + from_behind[...].astype(jnp.float32)).astype(jnp.bfloat16)
    near[...] = own[...].astype(jnp.float32) + from_ahead[...].astype(jnp.float32)
    widen(before, after, edge)
    width = queries.shape[1]
    for half in range(2):
        span = slice(256 * half, 256 * half + 256)
        blocks = edge_set(half, edge)
        for head in range(2):
            cols = slice(head * 128, head * 128 + 128)
            value_cols = slice(width + head * 128, width + head * 128 + 128)
            mine_q = queries[span, cols]
            cot = grad_attention[span, cols]
            pairs = score_grads(blocks, logits_of(blocks, mine_q, cols), lse[head:head + 1, span],
                                deltas[head:head + 1, span], cot, value_cols)
            for number, ((_, _, at, *_), (prob, dscore)) in enumerate(zip(blocks, pairs)):
                dscores[2 * half + head, 128 * number:128 * number + 128] = dscore
                grad_k = mm(dscore, mine_q, NN) * SCALE
                grad_v = mm(prob, cot, NN)
                if half == 1 and at >= 1280:
                    total[at:at + 128, cols] += grad_k
                    total[at:at + 128, value_cols] += grad_v
                else:
                    total[at:at + 128, cols] = grad_k
                    total[at:at + 128, value_cols] = grad_v
    to_prev[0:128] = (total[0:128] + repeated(total[832:896] * 0.5, 2)
                      + repeated(total[1376:1408] * 0.25, 4)).astype(jnp.bfloat16)
    to_prev[128:192] = (total[768:832] * 0.5 + repeated(total[1344:1376] * 0.25, 2)).astype(jnp.bfloat16)
    to_prev[192:256] = (total[1280:1344] * 0.25).astype(jnp.bfloat16)
    to_next[0:128] = (total[640:768] + repeated(total[1152:1216] * 0.5, 2)
                      + repeated(total[1408:1440] * 0.25, 4)).astype(jnp.bfloat16)
    to_next[128:192] = (total[1216:1280] * 0.5 + repeated(total[1440:1472] * 0.25, 2)).astype(jnp.bfloat16)
    to_next[192:256] = (total[1472:1536] * 0.25).astype(jnp.bfloat16)


def own_grads(queries, mine, edge, lse, grad_attention, deltas, dscores,
              grad_queries, own, total, pooled, grad_q_here, sems):
    pooled[...] = mm(pool_matrix(256, 2), mine[...], NN).astype(jnp.bfloat16)
    stores = []
    width = queries.shape[1]
    for half in range(2):
        span = slice(256 * half, 256 * half + 256)
        blocks = own_set(half, mine, pooled)
        for head in range(2):
            cols = slice(head * 128, head * 128 + 128)
            value_cols = slice(width + head * 128, width + head * 128 + 128)
            mine_q = queries[span, cols]
            cot = grad_attention[span, cols]
            pairs = score_grads(blocks, logits_of(blocks, mine_q, cols), lse[head:head + 1, span],
                                deltas[head:head + 1, span], cot, value_cols)
            grad_q = jnp.zeros((128, 256), jnp.float32)
            for number, (source, row, *_) in enumerate(edge_set(half, edge)):
                grad_q = grad_q + mm(source[row:row + 128, cols], dscores[2 * half + head, 128 * number:128 * number + 128], TN)
            for (source, row, at, *_), (prob, dscore) in zip(blocks, pairs):
                grad_q = grad_q + mm(source[row:row + 128, cols], dscore, TN)
                grad_k = mm(dscore, mine_q, NN) * SCALE
                grad_v = mm(prob, cot, NN)
                if half == 1 and 256 <= at < 512:
                    total[at:at + 128, cols] += grad_k
                    total[at:at + 128, value_cols] += grad_v
                else:
                    total[at:at + 128, cols] = grad_k
                    total[at:at + 128, value_cols] = grad_v
            grad_q_here[span, cols] = (grad_q * SCALE).T.astype(jnp.bfloat16)
        store = pltpu.make_async_copy(grad_q_here.at[span], grad_queries.at[span], sems.at[half])
        store.start()
        stores.append(store)
    own[...] = (total[128:640] + repeated(total[896:1152] * 0.5, 2)).astype(jnp.bfloat16)
    for store in stores:
        store.wait()


def finish(near_out, last_behind, own, from_prev, from_next, spread,
           output, grad_keys, grad_values, grad_weight,
           output_here, grad_keys_here, grad_values_here, grad_weight_here, spread_here, load_sems, sems):
    loads = in_pieces(spread, spread_here, load_sems)
    for copy in loads:
        copy.start()
    width = grad_keys.shape[1]
    stores = []

    def store(source, target):
        copy = pltpu.make_async_copy(source, target, sems.at[len(stores)])
        copy.start()
        stores.append(copy)

    top, bottom = pl.ds(0, 256), pl.ds(256, 256)
    output_here[top] = (near_out[top] + last_behind[top].astype(jnp.float32)).astype(jnp.bfloat16)
    store(output_here.at[top], output.at[top])
    output_here[bottom] = (near_out[bottom] + last_behind[bottom].astype(jnp.float32)).astype(jnp.bfloat16)
    store(output_here.at[bottom], output.at[bottom])
    twice = repeat_matrix(64, 2)
    four = repeat_matrix(64, 4)
    coarse = mm(four, from_next[192:256], NN)
    low = mm(four, from_prev[192:256], NN)
    first = own[0:128].astype(jnp.float32) + coarse[0:128] + from_prev[0:128].astype(jnp.float32)
    second = own[128:256].astype(jnp.float32) + coarse[128:256] + mm(twice, from_prev[128:192], NN)
    third = own[256:384].astype(jnp.float32) + low[0:128] + mm(twice, from_next[128:192], NN)
    fourth = own[384:512].astype(jnp.float32) + low[128:256] + from_next[0:128].astype(jnp.float32)
    for number, part in enumerate((first, second, third, fourth)):
        span = pl.ds(128 * number, 128)
        part = part.astype(jnp.bfloat16)
        grad_keys_here[span] = part[:, :width]
        grad_values_here[span] = part[:, width:]
        if number % 2:
            half = pl.ds(128 * (number - 1), 256)
            store(grad_keys_here.at[half], grad_keys.at[half])
            store(grad_values_here.at[half], grad_values.at[half])
    for copy in loads:
        copy.wait()
    grad_weight_here[...] = jnp.sum(spread_here[...].astype(jnp.float32), axis=0)
    store(grad_weight_here, grad_weight)
    for copy in stores:
        copy.wait()


def local(queries, keys, values, out_weight, grad_out):
    bf16, f32 = jnp.bfloat16, jnp.float32
    rows, width = queries.shape
    shards = lax.axis_size("seq")
    heads = lax.axis_size("head")
    features = out_weight.shape[0]
    ahead = [(i, (i - 1) % heads) for i in range(heads)]
    behind = [(target, source) for source, target in ahead]
    swap = [(i, i ^ 1) for i in range(shards)]
    onward = [(i, (i + 1) % shards) for i in range(shards)]
    back = [(target, source) for source, target in onward]
    dma = pltpu.SemaphoreType.DMA

    behind_cot = lax.ppermute(grad_out, "head", ahead)
    ahead_cot = lax.ppermute(grad_out, "head", behind)

    mine, to_next, to_prev = run(
        prepare, (keys, values),
        [((512, 2 * width), bf16), ((256, 2 * width), bf16), ((256, 2 * width), bf16)],
        flops=2 * 384 * 512 * 512, moved=1 << 20)
    before = lax.ppermute(to_next, "seq", onward)
    after = lax.ppermute(to_prev, "seq", back)
    queries, out_weight = run(
        fetch, (queries, out_weight, to_next), [((rows, width), bf16), ((features, width), bf16)],
        moved=2 << 20, far_args=(2,))
    tops, totals, sums = run(
        forward_own, (queries, mine, to_next),
        [((2, rows), f32), ((2, rows), f32), ((2 * HEAD_DIM, rows), f32)],
        [pltpu.VMEM((256, 2 * width), bf16)], flops=10 ** 9, moved=2 << 20, far_args=(2,))
    opposite = lax.ppermute(behind_cot, "head", ahead)

    attention, lse, own_out, first_ahead, second_ahead, first_behind = run(
        forward, (queries, before, after, out_weight, tops, totals, sums),
        [((rows, width), bf16), ((2, rows), f32), ((rows, width), bf16), ((rows, width), bf16),
         ((rows, width), bf16), ((rows, width), bf16)],
        [pltpu.VMEM((768, 2 * width), bf16)], flops=10 ** 9, moved=3 << 20)
    from_behind = lax.ppermute(first_ahead, "head", ahead)
    from_ahead = lax.ppermute(first_behind, "head", behind)

    chunk = features // shards
    shapes = [((shards // 2, chunk, width), f32), ((shards // 2, chunk, width), bf16)]
    keep, send, part = run(
        near_products, (grad_out, behind_cot, ahead_cot, attention, out_weight), shapes + [((rows, width), f32)],
        flops=4 * 10 ** 8, moved=1 << 20)
    keep, send, grad_attention, deltas = run(
        far_products, (opposite, attention, out_weight, keep, send, part),
        shapes + [((rows, width), bf16), ((2, rows), f32)])
    half_sum = lax.ppermute(send, "seq", swap)
    pairs, = run(pair_sum, (keep, half_sum), [((shards // 2, chunk, width), bf16)],
                 [pltpu.VMEM((shards // 2, chunk, width), bf16), dma((PIECES,))], far_outs=(0,))
    groups = [list(range(core, shards, 2)) for core in range(2)]
    spread = lax.all_to_all(pairs, "seq", 0, 0, axis_index_groups=groups)

    dscores, to_next, to_prev, edge, send_ahead, near_out = run(
        backward,
        (queries, before, after, lse, grad_attention, deltas, second_ahead, from_behind, own_out, from_ahead),
        [((4, 512, 256), bf16), ((256, 2 * width), bf16), ((256, 2 * width), bf16), ((768, 2 * width), bf16),
         ((rows, width), bf16), ((rows, width), f32)],
        [pltpu.VMEM((1536, 2 * width), f32)], flops=2 * 10 ** 9, moved=4 << 20)
    last_behind = lax.ppermute(send_ahead, "head", ahead)
    grad_before = lax.ppermute(to_next, "seq", onward)
    grad_after = lax.ppermute(to_prev, "seq", back)
    grad_queries, own_grad = run(
        own_grads, (queries, mine, edge, lse, grad_attention, deltas, dscores),
        [((rows, width), bf16), ((rows, 2 * width), bf16)],
        [pltpu.VMEM((1536, 2 * width), f32), pltpu.VMEM((256, 2 * width), bf16), pltpu.VMEM((rows, width), bf16), dma((2,))],
        flops=3 * 10 ** 9, moved=6 << 20, far_outs=(0,))

    output, grad_keys, grad_values, grad_weight = run(
        finish,
        (near_out, last_behind, own_grad, grad_before, grad_after, spread),
        [((rows, width), bf16)] * 3 + [((chunk, width), f32)],
        [pltpu.VMEM((rows, width), bf16)] * 3 + [pltpu.VMEM((chunk, width), f32)]
        + [pltpu.VMEM((shards // 2, chunk, width), bf16), dma((PIECES,)), dma((7,))],
        moved=4 << 20, far_args=(5,), far_outs=(0, 1, 2, 3))
    return output, grad_queries, grad_keys, grad_values, grad_weight


def solution(mesh):
    split = P("seq", "head")
    return jax.shard_map(
        local, mesh=mesh, in_specs=(split, split, split, P(None, "head"), split),
        out_specs=(split,) * 5, check_vma=False)
```

```python
import math

import jax
import jax.numpy as jnp
from jax import lax
from jax.experimental import pallas as pl
from jax.experimental.pallas import tpu as pltpu
from jax.sharding import PartitionSpec as P

HEAD_DIM = 128
BLOCK = 128
SCALE = HEAD_DIM ** -0.5
LOG2 = SCALE / math.log(2.0)
NEG = -1e30
VMEM = pl.BlockSpec(memory_space=pltpu.VMEM)
FAR = pl.BlockSpec(memory_space=pl.ANY)
PIECES = 4
NT = (((1,), (1,)), ((), ()))
TN = (((0,), (0,)), ((), ()))
NN = (((1,), (0,)), ((), ()))


def mm(a, b, dims):
    return lax.dot_general(a, b, dims, preferred_element_type=jnp.float32)


def run(body, args, outs, scratch=(), flops=0, moved=0, far_args=(), far_outs=(), room=24):
    return pl.pallas_call(
        body,
        in_specs=[FAR if number in far_args else VMEM for number in range(len(args))],
        out_shape=[jax.ShapeDtypeStruct(shape, kind) for shape, kind in outs],
        out_specs=[FAR if number in far_outs else VMEM for number in range(len(outs))],
        scratch_shapes=list(scratch),
        cost_estimate=pl.CostEstimate(flops=flops, bytes_accessed=moved, transcendentals=0),
        compiler_params=pltpu.CompilerParams(vmem_limit_bytes=room * 1024 * 1024),
    )(*args)


def pool_matrix(rows, factor):
    row = lax.broadcasted_iota(jnp.int32, (rows, rows * factor), 0)
    col = lax.broadcasted_iota(jnp.int32, (rows, rows * factor), 1)
    inside = (col >= row * factor) & (col < row * factor + factor)
    return jnp.where(inside, 1.0 / factor, 0.0).astype(jnp.bfloat16)


def repeat_matrix(rows, factor):
    row = lax.broadcasted_iota(jnp.int32, (rows * factor, rows), 0)
    col = lax.broadcasted_iota(jnp.int32, (rows * factor, rows), 1)
    inside = (row >= col * factor) & (row < col * factor + factor)
    return jnp.where(inside, 1.0, 0.0).astype(jnp.bfloat16)


def repeated(part, factor):
    matrix = repeat_matrix(part.shape[0], factor)
    high = part.astype(jnp.bfloat16)
    low = (part - high.astype(jnp.float32)).astype(jnp.bfloat16)
    return mm(matrix, high, NN) + mm(matrix, low, NN)


def in_pieces(source, target, sems):
    count = sems.shape[0]
    size = source.shape[0] // count
    return [pltpu.make_async_copy(source.at[pl.ds(number * size, size)], target.at[pl.ds(number * size, size)],
                                  sems.at[number]) for number in range(count)]


def on_even():
    return lax.rem(lax.axis_index("seq"), 2) == 0


def prepare(keys, values, mine, to_next, to_prev):
    width = keys.shape[1]
    two = pool_matrix(256, 2)
    four = pool_matrix(64, 4)
    for number, source in enumerate((keys, values)):
        cols = slice(number * width, (number + 1) * width)
        mine[:, cols] = source[...]
        first = mm(two, source[...], NN).astype(jnp.bfloat16)
        to_next[0:128, cols] = source[384:512]
        to_next[128:192, cols] = first[128:192]
        to_next[192:256, cols] = mm(four, source[0:256], NN).astype(jnp.bfloat16)
        to_prev[0:128, cols] = source[0:128]
        to_prev[128:192, cols] = first[64:128]
        to_prev[192:256, cols] = mm(four, source[256:512], NN).astype(jnp.bfloat16)


def fetch(queries, weight, _, queries_here, weight_here):
    queries_here[...] = queries[...]
    weight_here[...] = weight[...]


def widen(before, after, edge):
    half = pool_matrix(64, 2)
    both = pool_matrix(32, 2)
    quarter = pool_matrix(32, 4)
    edge[0:128] = before[0:128]
    edge[128:256] = after[0:128]
    edge[256:320] = before[128:192]
    edge[320:384] = mm(half, before[0:128], NN).astype(jnp.bfloat16)
    edge[384:448] = mm(half, after[0:128], NN).astype(jnp.bfloat16)
    edge[448:512] = after[128:192]
    edge[512:576] = before[192:256]
    edge[576:608] = mm(both, before[128:192], NN).astype(jnp.bfloat16)
    edge[608:640] = mm(quarter, before[0:128], NN).astype(jnp.bfloat16)
    edge[640:672] = mm(quarter, after[0:128], NN).astype(jnp.bfloat16)
    edge[672:704] = mm(both, after[128:192], NN).astype(jnp.bfloat16)
    edge[704:768] = after[192:256]


def own_set(half, mine, pooled):
    both = (0, 256)
    if half == 0:
        return [(mine, 0, 128, 0, both), (mine, 128, 256, 0, both), (mine, 256, 384, 0, (128, 256)), (pooled, 128, 1024, 1, both)]
    return [(mine, 128, 256, 0, (0, 128)), (mine, 256, 384, 0, both), (mine, 384, 512, 0, both), (pooled, 0, 896, 1, both)]


def edge_set(half, edge):
    place = lax.axis_index("seq")
    has_prev = place > 0
    has_next = place < lax.axis_size("seq") - 1
    both = (0, 256)
    far = [(edge, 512, 1280, 2, both, has_prev), (edge, 640, 1408, 2, both, has_next)]
    if half == 0:
        return [(edge, 0, 0, 0, (0, 128), has_prev), (edge, 256, 768, 1, both, has_prev)] + far
    return [(edge, 128, 640, 0, (128, 256), has_next), (edge, 384, 1152, 1, both, has_next)] + far


def logits_of(blocks, mine_q, cols):
    scores = []
    for source, row, _, level, seen, *there in blocks:
        score = mm(source[row:row + 128, cols], mine_q, NT) * LOG2
        if there:
            score = score + jnp.where(there[0], float(level), NEG)
        elif level:
            score = score + float(level)
        empty = jnp.full((128, 128), NEG, jnp.float32)
        if seen == (0, 128):
            score = jnp.concatenate([score[:, :128], empty], axis=1)
        if seen == (128, 256):
            score = jnp.concatenate([empty, score[:, 128:]], axis=1)
        scores.append(score)
    return scores


def gather(blocks, scores, top, value_cols):
    total = jnp.zeros((128, 256), jnp.float32)
    summed = jnp.zeros((128, 256), jnp.float32)
    for (source, row, *_), score in zip(blocks, scores):
        expd = jnp.exp2(score - top)
        total = total + expd
        summed = summed + mm(source[row:row + 128, value_cols], expd.astype(jnp.bfloat16), TN)
    return jnp.sum(total, axis=0, keepdims=True), summed


def top_of(scores):
    top = scores[0]
    for score in scores[1:]:
        top = jnp.maximum(top, score)
    return jnp.max(top, axis=0, keepdims=True)


def forward_own(queries, mine, _, tops, totals, sums, pooled):
    pooled[...] = mm(pool_matrix(256, 2), mine[...], NN).astype(jnp.bfloat16)
    width = queries.shape[1]
    for head in range(2):
        cols = slice(head * 128, head * 128 + 128)
        value_cols = slice(width + head * 128, width + head * 128 + 128)
        for half in range(2):
            span = slice(256 * half, 256 * half + 256)
            blocks = own_set(half, mine, pooled)
            scores = logits_of(blocks, queries[span, cols], cols)
            top = top_of(scores)
            tops[head:head + 1, span] = top
            totals[head:head + 1, span], sums[head * 128:head * 128 + 128, span] = gather(blocks, scores, top, value_cols)


def forward(queries, before, after, weight, tops, totals, sums,
            attention, lse, own, first_up, second_up, first_down, edge):
    widen(before, after, edge)
    width = queries.shape[1]
    for head in range(2):
        cols = slice(head * 128, head * 128 + 128)
        value_cols = slice(width + head * 128, width + head * 128 + 128)
        for half in range(2):
            span = slice(256 * half, 256 * half + 256)
            blocks = edge_set(half, edge)
            scores = logits_of(blocks, queries[span, cols], cols)
            before_top = tops[head:head + 1, span]
            top = jnp.maximum(before_top, top_of(scores))
            total, summed = gather(blocks, scores, top, value_cols)
            scale = jnp.exp2(before_top - top)
            total = total + scale * totals[head:head + 1, span]
            lse[head:head + 1, span] = top + jnp.log2(total)
            result = ((summed + scale * sums[head * 128:head * 128 + 128, span]) / total).T
            attention[span, cols] = result.astype(jnp.bfloat16)
    heads = lax.axis_size("head")
    here = lax.axis_index("head")

    def partial_to(target):
        start = pl.multiple_of(lax.rem(target, heads) * width, width)
        return mm(attention[...], weight[pl.ds(start, width), :], NT)

    own[...] = partial_to(here).astype(jnp.bfloat16)
    first_up[...] = partial_to(here + 2).astype(jnp.bfloat16)
    second_up[...] = partial_to(here + 1).astype(jnp.bfloat16)
    first_down[...] = partial_to(here + 3).astype(jnp.bfloat16)


def product_of(shift, cot, attention, weight, keep, send):
    heads = lax.axis_size("head")
    owner = lax.rem(lax.axis_index("head") + shift, heads)
    even = on_even()
    groups, rows, width = keep.shape
    each = groups // heads
    chunks = mm(cot[...], attention[...], TN).reshape(each, 2, rows, width)
    first, second = chunks[:, 0], chunks[:, 1]
    start = owner * each
    keep[pl.ds(start, each)] = jnp.where(even, first, second)
    send[pl.ds(start, each)] = jnp.where(even, second, first).astype(jnp.bfloat16)
    return mm(cot[...], weight[pl.ds(pl.multiple_of(owner * width, width), width), :], NN)


def near_products(mine, first_cot, second_cot, attention, weight, keep, send, part):
    heads = lax.axis_size("head")
    part[...] = (product_of(0, mine, attention, weight, keep, send)
                 + product_of(1, first_cot, attention, weight, keep, send)
                 + product_of(heads - 1, second_cot, attention, weight, keep, send))


def far_products(opposite, attention, weight, near_keep, near_send, part, keep, send, grad_attention, deltas):
    keep[...] = near_keep[...]
    send[...] = near_send[...]
    rounded = (part[...] + product_of(2, opposite, attention, weight, keep, send)).astype(jnp.bfloat16)
    grad_attention[...] = rounded
    terms = rounded.astype(jnp.float32) * attention[...].astype(jnp.float32)
    high = terms.astype(jnp.bfloat16)
    low = (terms - high.astype(jnp.float32)).astype(jnp.bfloat16)
    ones = jnp.ones((16, HEAD_DIM), jnp.bfloat16)
    for head in range(2):
        cols = slice(head * HEAD_DIM, head * HEAD_DIM + HEAD_DIM)
        deltas[head:head + 1] = (mm(ones, high[:, cols], NT) + mm(ones, low[:, cols], NT))[0:1]


def pair_sum(keep, sibling, pairs, pairs_here, sems):
    stores = in_pieces(pairs_here, pairs, sems)
    size = pairs.shape[0] // len(stores)
    for number, store in enumerate(stores):
        span = pl.ds(number * size, size)
        pairs_here[span] = (keep[span] + sibling[span].astype(jnp.float32)).astype(jnp.bfloat16)
        store.start()
    for store in stores:
        store.wait()


def score_grads(blocks, scores, norm, delta, cot, value_cols):
    pairs = []
    for (source, row, *_), score in zip(blocks, scores):
        prob = jnp.exp2(score - norm)
        dprob = mm(source[row:row + 128, value_cols], cot, NT)
        pairs.append((prob.astype(jnp.bfloat16), (prob * (dprob - delta)).astype(jnp.bfloat16)))
    return pairs


def backward(queries, before, after, lse, grad_attention, deltas, second_up, from_below, own, from_above,
             dscores, to_next, to_prev, edge, send_up, near, total):
    send_up[...] = (second_up[...].astype(jnp.float32) + from_below[...].astype(jnp.float32)).astype(jnp.bfloat16)
    near[...] = own[...].astype(jnp.float32) + from_above[...].astype(jnp.float32)
    widen(before, after, edge)
    width = queries.shape[1]
    for half in range(2):
        span = slice(256 * half, 256 * half + 256)
        blocks = edge_set(half, edge)
        for head in range(2):
            cols = slice(head * 128, head * 128 + 128)
            value_cols = slice(width + head * 128, width + head * 128 + 128)
            mine_q = queries[span, cols]
            cot = grad_attention[span, cols]
            pairs = score_grads(blocks, logits_of(blocks, mine_q, cols), lse[head:head + 1, span],
                                deltas[head:head + 1, span], cot, value_cols)
            for number, ((_, _, at, *_), (prob, dscore)) in enumerate(zip(blocks, pairs)):
                dscores[2 * half + head, 128 * number:128 * number + 128] = dscore
                grad_k = mm(dscore, mine_q, NN) * SCALE
                grad_v = mm(prob, cot, NN)
                if half == 1 and at >= 1280:
                    total[at:at + 128, cols] += grad_k
                    total[at:at + 128, value_cols] += grad_v
                else:
                    total[at:at + 128, cols] = grad_k
                    total[at:at + 128, value_cols] = grad_v
    to_prev[0:128] = (total[0:128] + repeated(total[832:896] * 0.5, 2)
                      + repeated(total[1376:1408] * 0.25, 4)).astype(jnp.bfloat16)
    to_prev[128:192] = (total[768:832] * 0.5 + repeated(total[1344:1376] * 0.25, 2)).astype(jnp.bfloat16)
    to_prev[192:256] = (total[1280:1344] * 0.25).astype(jnp.bfloat16)
    to_next[0:128] = (total[640:768] + repeated(total[1152:1216] * 0.5, 2)
                      + repeated(total[1408:1440] * 0.25, 4)).astype(jnp.bfloat16)
    to_next[128:192] = (total[1216:1280] * 0.5 + repeated(total[1440:1472] * 0.25, 2)).astype(jnp.bfloat16)
    to_next[192:256] = (total[1472:1536] * 0.25).astype(jnp.bfloat16)


def own_grads(queries, mine, edge, lse, grad_attention, deltas, dscores,
              grad_queries, own, total, pooled, grad_q_here, sems):
    pooled[...] = mm(pool_matrix(256, 2), mine[...], NN).astype(jnp.bfloat16)
    stores = []
    width = queries.shape[1]
    for half in range(2):
        span = slice(256 * half, 256 * half + 256)
        blocks = own_set(half, mine, pooled)
        for head in range(2):
            cols = slice(head * 128, head * 128 + 128)
            value_cols = slice(width + head * 128, width + head * 128 + 128)
            mine_q = queries[span, cols]
            cot = grad_attention[span, cols]
            pairs = score_grads(blocks, logits_of(blocks, mine_q, cols), lse[head:head + 1, span],
                                deltas[head:head + 1, span], cot, value_cols)
            grad_q = jnp.zeros((128, 256), jnp.float32)
            for number, (source, row, *_) in enumerate(edge_set(half, edge)):
                grad_q = grad_q + mm(source[row:row + 128, cols], dscores[2 * half + head, 128 * number:128 * number + 128], TN)
            for (source, row, at, *_), (prob, dscore) in zip(blocks, pairs):
                grad_q = grad_q + mm(source[row:row + 128, cols], dscore, TN)
                grad_k = mm(dscore, mine_q, NN) * SCALE
                grad_v = mm(prob, cot, NN)
                if half == 1 and 256 <= at < 512:
                    total[at:at + 128, cols] += grad_k
                    total[at:at + 128, value_cols] += grad_v
                else:
                    total[at:at + 128, cols] = grad_k
                    total[at:at + 128, value_cols] = grad_v
            grad_q_here[span, cols] = (grad_q * SCALE).T.astype(jnp.bfloat16)
        store = pltpu.make_async_copy(grad_q_here.at[span], grad_queries.at[span], sems.at[half])
        store.start()
        stores.append(store)
    own[...] = (total[128:640] + repeated(total[896:1152] * 0.5, 2)).astype(jnp.bfloat16)
    for store in stores:
        store.wait()


def finish(near_out, last_below, own, from_prev, from_next, spread,
           output, grad_keys, grad_values, grad_weight,
           output_here, grad_keys_here, grad_values_here, grad_weight_here, spread_here, load_sems, sems):
    loads = in_pieces(spread, spread_here, load_sems)
    for copy in loads:
        copy.start()
    width = grad_keys.shape[1]
    stores = []

    def store(source, target):
        copy = pltpu.make_async_copy(source, target, sems.at[len(stores)])
        copy.start()
        stores.append(copy)

    top, bottom = pl.ds(0, 256), pl.ds(256, 256)
    output_here[top] = (near_out[top] + last_below[top].astype(jnp.float32)).astype(jnp.bfloat16)
    store(output_here.at[top], output.at[top])
    output_here[bottom] = (near_out[bottom] + last_below[bottom].astype(jnp.float32)).astype(jnp.bfloat16)
    store(output_here.at[bottom], output.at[bottom])
    twice = repeat_matrix(64, 2)
    four = repeat_matrix(64, 4)
    coarse = mm(four, from_next[192:256], NN)
    low = mm(four, from_prev[192:256], NN)
    first = own[0:128].astype(jnp.float32) + coarse[0:128] + from_prev[0:128].astype(jnp.float32)
    second = own[128:256].astype(jnp.float32) + coarse[128:256] + mm(twice, from_prev[128:192], NN)
    third = own[256:384].astype(jnp.float32) + low[0:128] + mm(twice, from_next[128:192], NN)
    fourth = own[384:512].astype(jnp.float32) + low[128:256] + from_next[0:128].astype(jnp.float32)
    for number, part in enumerate((first, second, third, fourth)):
        span = pl.ds(128 * number, 128)
        part = part.astype(jnp.bfloat16)
        grad_keys_here[span] = part[:, :width]
        grad_values_here[span] = part[:, width:]
        if number % 2:
            half = pl.ds(128 * (number - 1), 256)
            store(grad_keys_here.at[half], grad_keys.at[half])
            store(grad_values_here.at[half], grad_values.at[half])
    for copy in loads:
        copy.wait()
    grad_weight_here[...] = jnp.sum(spread_here[...].astype(jnp.float32), axis=0)
    store(grad_weight_here, grad_weight)
    for copy in stores:
        copy.wait()


def local(queries, keys, values, out_weight, grad_out):
    bf16, f32 = jnp.bfloat16, jnp.float32
    rows, width = queries.shape
    shards = lax.axis_size("seq")
    heads = lax.axis_size("head")
    features = out_weight.shape[0]
    up = [(i, (i + 1) % heads) for i in range(heads)]
    down = [(target, source) for source, target in up]
    swap = [(i, i ^ 1) for i in range(shards)]
    onward = [(i, (i + 1) % shards) for i in range(shards)]
    back = [(target, source) for source, target in onward]
    dma = pltpu.SemaphoreType.DMA

    first_cot = lax.ppermute(grad_out, "head", down)
    second_cot = lax.ppermute(grad_out, "head", up)

    mine, to_next, to_prev = run(
        prepare, (keys, values),
        [((512, 2 * width), bf16), ((256, 2 * width), bf16), ((256, 2 * width), bf16)],
        flops=2 * 384 * 512 * 512, moved=1 << 20)
    before = lax.ppermute(to_next, "seq", onward)
    after = lax.ppermute(to_prev, "seq", back)
    queries, out_weight = run(
        fetch, (queries, out_weight, to_next), [((rows, width), bf16), ((features, width), bf16)],
        moved=2 << 20, far_args=(2,))
    tops, totals, sums = run(
        forward_own, (queries, mine, to_next),
        [((2, rows), f32), ((2, rows), f32), ((2 * HEAD_DIM, rows), f32)],
        [pltpu.VMEM((256, 2 * width), bf16)], flops=10 ** 9, moved=2 << 20, far_args=(2,))
    opposite = lax.ppermute(first_cot, "head", down)

    attention, lse, own_out, first_up, second_up, first_down = run(
        forward, (queries, before, after, out_weight, tops, totals, sums),
        [((rows, width), bf16), ((2, rows), f32), ((rows, width), bf16), ((rows, width), bf16),
         ((rows, width), bf16), ((rows, width), bf16)],
        [pltpu.VMEM((768, 2 * width), bf16)], flops=10 ** 9, moved=3 << 20)
    from_below = lax.ppermute(first_up, "head", up)
    from_above = lax.ppermute(first_down, "head", down)

    chunk = features // shards
    shapes = [((shards // 2, chunk, width), f32), ((shards // 2, chunk, width), bf16)]
    keep, send, part = run(
        near_products, (grad_out, first_cot, second_cot, attention, out_weight), shapes + [((rows, width), f32)],
        flops=4 * 10 ** 8, moved=1 << 20)
    keep, send, grad_attention, deltas = run(
        far_products, (opposite, attention, out_weight, keep, send, part),
        shapes + [((rows, width), bf16), ((2, rows), f32)])
    half_sum = lax.ppermute(send, "seq", swap)
    pairs, = run(pair_sum, (keep, half_sum), [((shards // 2, chunk, width), bf16)],
                 [pltpu.VMEM((shards // 2, chunk, width), bf16), dma((PIECES,))], far_outs=(0,))
    groups = [list(range(core, shards, 2)) for core in range(2)]
    spread = lax.all_to_all(pairs, "seq", 0, 0, axis_index_groups=groups)

    dscores, to_next, to_prev, edge, send_up, near_out = run(
        backward,
        (queries, before, after, lse, grad_attention, deltas, second_up, from_below, own_out, from_above),
        [((4, 512, 256), bf16), ((256, 2 * width), bf16), ((256, 2 * width), bf16), ((768, 2 * width), bf16),
         ((rows, width), bf16), ((rows, width), f32)],
        [pltpu.VMEM((1536, 2 * width), f32)], flops=2 * 10 ** 9, moved=4 << 20)
    last_below = lax.ppermute(send_up, "head", up)
    grad_before = lax.ppermute(to_next, "seq", onward)
    grad_after = lax.ppermute(to_prev, "seq", back)
    grad_queries, own_grad = run(
        own_grads, (queries, mine, edge, lse, grad_attention, deltas, dscores),
        [((rows, width), bf16), ((rows, 2 * width), bf16)],
        [pltpu.VMEM((1536, 2 * width), f32), pltpu.VMEM((256, 2 * width), bf16), pltpu.VMEM((rows, width), bf16), dma((2,))],
        flops=3 * 10 ** 9, moved=6 << 20, far_outs=(0,))

    output, grad_keys, grad_values, grad_weight = run(
        finish,
        (near_out, last_below, own_grad, grad_before, grad_after, spread),
        [((rows, width), bf16)] * 3 + [((chunk, width), f32)],
        [pltpu.VMEM((rows, width), bf16)] * 3 + [pltpu.VMEM((chunk, width), f32)]
        + [pltpu.VMEM((shards // 2, chunk, width), bf16), dma((PIECES,)), dma((7,))],
        moved=4 << 20, far_args=(5,), far_outs=(0, 1, 2, 3))
    return output, grad_queries, grad_keys, grad_values, grad_weight


def solution(mesh):
    split = P("seq", "head")
    return jax.shard_map(
        local, mesh=mesh, in_specs=(split, split, split, P(None, "head"), split),
        out_specs=(split,) * 5, check_vma=False)
```

```python
import math

import jax
import jax.numpy as jnp
from jax import lax
from jax.experimental import pallas as pl
from jax.experimental.pallas import tpu as pltpu
from jax.sharding import PartitionSpec as P

HEAD_DIM = 128
BLOCK = 128
SCALE = HEAD_DIM ** -0.5
LOG2 = SCALE / math.log(2.0)
NEG = -1e30
VMEM = pl.BlockSpec(memory_space=pltpu.VMEM)
FAR = pl.BlockSpec(memory_space=pl.ANY)
PIECES = 4
NT = (((1,), (1,)), ((), ()))
TN = (((0,), (0,)), ((), ()))
NN = (((1,), (0,)), ((), ()))


def mm(a, b, dims):
    return lax.dot_general(a, b, dims, preferred_element_type=jnp.float32)


def run(body, args, outs, scratch=(), flops=0, moved=0, far_args=(), far_outs=(), room=24):
    return pl.pallas_call(
        body,
        in_specs=[FAR if number in far_args else VMEM for number in range(len(args))],
        out_shape=[jax.ShapeDtypeStruct(shape, kind) for shape, kind in outs],
        out_specs=[FAR if number in far_outs else VMEM for number in range(len(outs))],
        scratch_shapes=list(scratch),
        cost_estimate=pl.CostEstimate(flops=flops, bytes_accessed=moved, transcendentals=0),
        compiler_params=pltpu.CompilerParams(vmem_limit_bytes=room * 1024 * 1024),
    )(*args)


def pool_matrix(rows, factor):
    row = lax.broadcasted_iota(jnp.int32, (rows, rows * factor), 0)
    col = lax.broadcasted_iota(jnp.int32, (rows, rows * factor), 1)
    inside = (col >= row * factor) & (col < row * factor + factor)
    return jnp.where(inside, 1.0 / factor, 0.0).astype(jnp.bfloat16)


def repeat_matrix(rows, factor):
    row = lax.broadcasted_iota(jnp.int32, (rows * factor, rows), 0)
    col = lax.broadcasted_iota(jnp.int32, (rows * factor, rows), 1)
    inside = (row >= col * factor) & (row < col * factor + factor)
    return jnp.where(inside, 1.0, 0.0).astype(jnp.bfloat16)


def repeated(part, factor):
    matrix = repeat_matrix(part.shape[0], factor)
    high = part.astype(jnp.bfloat16)
    low = (part - high.astype(jnp.float32)).astype(jnp.bfloat16)
    return mm(matrix, high, NN) + mm(matrix, low, NN)


def in_pieces(source, target, sems):
    count = sems.shape[0]
    size = source.shape[0] // count
    return [pltpu.make_async_copy(source.at[pl.ds(number * size, size)], target.at[pl.ds(number * size, size)],
                                  sems.at[number]) for number in range(count)]


def on_even():
    return lax.rem(lax.axis_index("seq"), 2) == 0


def prepare(keys, values, mine, to_next, to_prev):
    width = keys.shape[1]
    two = pool_matrix(256, 2)
    four = pool_matrix(64, 4)
    for number, source in enumerate((keys, values)):
        cols = slice(number * width, (number + 1) * width)
        mine[:, cols] = source[...]
        first = mm(two, source[...], NN).astype(jnp.bfloat16)
        to_next[0:128, cols] = source[384:512]
        to_next[128:192, cols] = first[128:192]
        to_next[192:256, cols] = mm(four, source[0:256], NN).astype(jnp.bfloat16)
        to_prev[0:128, cols] = source[0:128]
        to_prev[128:192, cols] = first[64:128]
        to_prev[192:256, cols] = mm(four, source[256:512], NN).astype(jnp.bfloat16)


def fetch(queries, weight, _, queries_here, weight_here):
    queries_here[...] = queries[...]
    weight_here[...] = weight[...]


def widen(before, after, edge):
    half = pool_matrix(64, 2)
    both = pool_matrix(32, 2)
    quarter = pool_matrix(32, 4)
    edge[0:128] = before[0:128]
    edge[128:256] = after[0:128]
    edge[256:320] = before[128:192]
    edge[320:384] = mm(half, before[0:128], NN).astype(jnp.bfloat16)
    edge[384:448] = mm(half, after[0:128], NN).astype(jnp.bfloat16)
    edge[448:512] = after[128:192]
    edge[512:576] = before[192:256]
    edge[576:608] = mm(both, before[128:192], NN).astype(jnp.bfloat16)
    edge[608:640] = mm(quarter, before[0:128], NN).astype(jnp.bfloat16)
    edge[640:672] = mm(quarter, after[0:128], NN).astype(jnp.bfloat16)
    edge[672:704] = mm(both, after[128:192], NN).astype(jnp.bfloat16)
    edge[704:768] = after[192:256]


def own_set(half, mine, pooled):
    both = (0, 256)
    if half == 0:
        return [(mine, 0, 128, 0, both), (mine, 128, 256, 0, both), (mine, 256, 384, 0, (128, 256)), (pooled, 128, 1024, 1, both)]
    return [(mine, 128, 256, 0, (0, 128)), (mine, 256, 384, 0, both), (mine, 384, 512, 0, both), (pooled, 0, 896, 1, both)]


def edge_set(half, edge):
    place = lax.axis_index("seq")
    has_prev = place > 0
    has_next = place < lax.axis_size("seq") - 1
    both = (0, 256)
    far = [(edge, 512, 1280, 2, both, has_prev), (edge, 640, 1408, 2, both, has_next)]
    if half == 0:
        return [(edge, 0, 0, 0, (0, 128), has_prev), (edge, 256, 768, 1, both, has_prev)] + far
    return [(edge, 128, 640, 0, (128, 256), has_next), (edge, 384, 1152, 1, both, has_next)] + far


def logits_of(blocks, mine_q, cols):
    scores = []
    for source, row, _, level, seen, *there in blocks:
        score = mm(source[row:row + 128, cols], mine_q, NT) * LOG2
        if there:
            score = score + jnp.where(there[0], float(level), NEG)
        elif level:
            score = score + float(level)
        empty = jnp.full((128, 128), NEG, jnp.float32)
        if seen == (0, 128):
            score = jnp.concatenate([score[:, :128], empty], axis=1)
        if seen == (128, 256):
            score = jnp.concatenate([empty, score[:, 128:]], axis=1)
        scores.append(score)
    return scores


def gather(blocks, scores, top, value_cols):
    total = jnp.zeros((128, 256), jnp.float32)
    summed = jnp.zeros((128, 256), jnp.float32)
    for (source, row, *_), score in zip(blocks, scores):
        expd = jnp.exp2(score - top)
        total = total + expd
        summed = summed + mm(source[row:row + 128, value_cols], expd.astype(jnp.bfloat16), TN)
    return jnp.sum(total, axis=0, keepdims=True), summed


def top_of(scores):
    top = scores[0]
    for score in scores[1:]:
        top = jnp.maximum(top, score)
    return jnp.max(top, axis=0, keepdims=True)


def forward_own(queries, mine, _, tops, totals, sums, pooled):
    pooled[...] = mm(pool_matrix(256, 2), mine[...], NN).astype(jnp.bfloat16)
    width = queries.shape[1]
    for head in range(2):
        cols = slice(head * 128, head * 128 + 128)
        value_cols = slice(width + head * 128, width + head * 128 + 128)
        for half in range(2):
            span = slice(256 * half, 256 * half + 256)
            blocks = own_set(half, mine, pooled)
            scores = logits_of(blocks, queries[span, cols], cols)
            top = top_of(scores)
            tops[head:head + 1, span] = top
            totals[head:head + 1, span], sums[head * 128:head * 128 + 128, span] = gather(blocks, scores, top, value_cols)


def forward(queries, before, after, weight, tops, totals, sums,
            attention, residue, lse, own, first_up, second_up, first_down, edge):
    widen(before, after, edge)
    width = queries.shape[1]
    for head in range(2):
        cols = slice(head * 128, head * 128 + 128)
        value_cols = slice(width + head * 128, width + head * 128 + 128)
        for half in range(2):
            span = slice(256 * half, 256 * half + 256)
            blocks = edge_set(half, edge)
            scores = logits_of(blocks, queries[span, cols], cols)
            before_top = tops[head:head + 1, span]
            top = jnp.maximum(before_top, top_of(scores))
            total, summed = gather(blocks, scores, top, value_cols)
            scale = jnp.exp2(before_top - top)
            total = total + scale * totals[head:head + 1, span]
            lse[head:head + 1, span] = top + jnp.log2(total)
            result = ((summed + scale * sums[head * 128:head * 128 + 128, span]) / total).T
            rounded = result.astype(jnp.bfloat16)
            attention[span, cols] = rounded
            residue[span, cols] = (result - rounded.astype(jnp.float32)).astype(jnp.bfloat16)
    heads = lax.axis_size("head")
    here = lax.axis_index("head")

    def partial_to(target):
        start = pl.multiple_of(lax.rem(target, heads) * width, width)
        return mm(attention[...], weight[pl.ds(start, width), :], NT)

    own[...] = partial_to(here).astype(jnp.bfloat16)
    first_up[...] = partial_to(here + 2).astype(jnp.bfloat16)
    second_up[...] = partial_to(here + 1).astype(jnp.bfloat16)
    first_down[...] = partial_to(here + 3).astype(jnp.bfloat16)


def product_of(shift, cot, attention, weight, keep, send):
    heads = lax.axis_size("head")
    owner = lax.rem(lax.axis_index("head") + shift, heads)
    even = on_even()
    groups, rows, width = keep.shape
    each = groups // heads
    chunks = mm(cot[...], attention[...], TN).reshape(each, 2, rows, width)
    first, second = chunks[:, 0], chunks[:, 1]
    start = owner * each
    keep[pl.ds(start, each)] = jnp.where(even, first, second)
    send[pl.ds(start, each)] = jnp.where(even, second, first).astype(jnp.bfloat16)
    return mm(cot[...], weight[pl.ds(pl.multiple_of(owner * width, width), width), :], NN)


def near_products(mine, first_cot, second_cot, attention, weight, keep, send, part):
    heads = lax.axis_size("head")
    part[...] = (product_of(0, mine, attention, weight, keep, send)
                 + product_of(1, first_cot, attention, weight, keep, send)
                 + product_of(heads - 1, second_cot, attention, weight, keep, send))


def far_products(opposite, attention, residue, weight, near_keep, near_send, part, keep, send, grad_attention, deltas):
    keep[...] = near_keep[...]
    send[...] = near_send[...]
    rounded = (part[...] + product_of(2, opposite, attention, weight, keep, send)).astype(jnp.bfloat16)
    grad_attention[...] = rounded
    terms = rounded.astype(jnp.float32) * (attention[...].astype(jnp.float32) + residue[...].astype(jnp.float32))
    ones = jnp.ones((16, HEAD_DIM), jnp.bfloat16)
    sums = [jnp.zeros((16, terms.shape[0]), jnp.float32)] * 2
    for _ in range(3):
        part_of = terms.astype(jnp.bfloat16)
        terms = terms - part_of.astype(jnp.float32)
        sums = [sums[head] + mm(ones, part_of[:, head * HEAD_DIM:head * HEAD_DIM + HEAD_DIM], NT) for head in range(2)]
    for head in range(2):
        deltas[head:head + 1] = sums[head][0:1]


def pair_sum(keep, sibling, pairs, pairs_here, sems):
    stores = in_pieces(pairs_here, pairs, sems)
    size = pairs.shape[0] // len(stores)
    for number, store in enumerate(stores):
        span = pl.ds(number * size, size)
        pairs_here[span] = (keep[span] + sibling[span].astype(jnp.float32)).astype(jnp.bfloat16)
        store.start()
    for store in stores:
        store.wait()


def score_grads(blocks, scores, norm, delta, cot, value_cols):
    pairs = []
    for (source, row, *_), score in zip(blocks, scores):
        prob = jnp.exp2(score - norm)
        dprob = mm(source[row:row + 128, value_cols], cot, NT)
        pairs.append((prob.astype(jnp.bfloat16), (prob * (dprob - delta)).astype(jnp.bfloat16)))
    return pairs


def backward(queries, before, after, lse, grad_attention, deltas, second_up, from_below, own, from_above,
             dscores, to_next, to_prev, edge, send_up, near, total):
    send_up[...] = (second_up[...].astype(jnp.float32) + from_below[...].astype(jnp.float32)).astype(jnp.bfloat16)
    near[...] = own[...].astype(jnp.float32) + from_above[...].astype(jnp.float32)
    widen(before, after, edge)
    width = queries.shape[1]
    for half in range(2):
        span = slice(256 * half, 256 * half + 256)
        blocks = edge_set(half, edge)
        for head in range(2):
            cols = slice(head * 128, head * 128 + 128)
            value_cols = slice(width + head * 128, width + head * 128 + 128)
            mine_q = queries[span, cols]
            cot = grad_attention[span, cols]
            pairs = score_grads(blocks, logits_of(blocks, mine_q, cols), lse[head:head + 1, span],
                                deltas[head:head + 1, span], cot, value_cols)
            for number, ((_, _, at, *_), (prob, dscore)) in enumerate(zip(blocks, pairs)):
                dscores[2 * half + head, 128 * number:128 * number + 128] = dscore
                grad_k = mm(dscore, mine_q, NN) * SCALE
                grad_v = mm(prob, cot, NN)
                if half == 1 and at >= 1280:
                    total[at:at + 128, cols] += grad_k
                    total[at:at + 128, value_cols] += grad_v
                else:
                    total[at:at + 128, cols] = grad_k
                    total[at:at + 128, value_cols] = grad_v
    to_prev[0:128] = (total[0:128] + repeated(total[832:896] * 0.5, 2)
                      + repeated(total[1376:1408] * 0.25, 4)).astype(jnp.bfloat16)
    to_prev[128:192] = (total[768:832] * 0.5 + repeated(total[1344:1376] * 0.25, 2)).astype(jnp.bfloat16)
    to_prev[192:256] = (total[1280:1344] * 0.25).astype(jnp.bfloat16)
    to_next[0:128] = (total[640:768] + repeated(total[1152:1216] * 0.5, 2)
                      + repeated(total[1408:1440] * 0.25, 4)).astype(jnp.bfloat16)
    to_next[128:192] = (total[1216:1280] * 0.5 + repeated(total[1440:1472] * 0.25, 2)).astype(jnp.bfloat16)
    to_next[192:256] = (total[1472:1536] * 0.25).astype(jnp.bfloat16)


def own_grads(queries, mine, edge, lse, grad_attention, deltas, dscores,
              grad_queries, own, total, pooled, grad_q_here, sems):
    pooled[...] = mm(pool_matrix(256, 2), mine[...], NN).astype(jnp.bfloat16)
    stores = []
    width = queries.shape[1]
    for half in range(2):
        span = slice(256 * half, 256 * half + 256)
        blocks = own_set(half, mine, pooled)
        for head in range(2):
            cols = slice(head * 128, head * 128 + 128)
            value_cols = slice(width + head * 128, width + head * 128 + 128)
            mine_q = queries[span, cols]
            cot = grad_attention[span, cols]
            pairs = score_grads(blocks, logits_of(blocks, mine_q, cols), lse[head:head + 1, span],
                                deltas[head:head + 1, span], cot, value_cols)
            grad_q = jnp.zeros((128, 256), jnp.float32)
            for number, (source, row, *_) in enumerate(edge_set(half, edge)):
                grad_q = grad_q + mm(source[row:row + 128, cols], dscores[2 * half + head, 128 * number:128 * number + 128], TN)
            for (source, row, at, *_), (prob, dscore) in zip(blocks, pairs):
                grad_q = grad_q + mm(source[row:row + 128, cols], dscore, TN)
                grad_k = mm(dscore, mine_q, NN) * SCALE
                grad_v = mm(prob, cot, NN)
                if half == 1 and 256 <= at < 512:
                    total[at:at + 128, cols] += grad_k
                    total[at:at + 128, value_cols] += grad_v
                else:
                    total[at:at + 128, cols] = grad_k
                    total[at:at + 128, value_cols] = grad_v
            grad_q_here[span, cols] = (grad_q * SCALE).T.astype(jnp.bfloat16)
        store = pltpu.make_async_copy(grad_q_here.at[span], grad_queries.at[span], sems.at[half])
        store.start()
        stores.append(store)
    own[...] = (total[128:640] + repeated(total[896:1152] * 0.5, 2)).astype(jnp.bfloat16)
    for store in stores:
        store.wait()


def finish(near_out, last_below, own, from_prev, from_next, spread,
           output, grad_keys, grad_values, grad_weight,
           output_here, grad_keys_here, grad_values_here, grad_weight_here, spread_here, load_sems, sems):
    loads = in_pieces(spread, spread_here, load_sems)
    for copy in loads:
        copy.start()
    width = grad_keys.shape[1]
    stores = []

    def store(source, target):
        copy = pltpu.make_async_copy(source, target, sems.at[len(stores)])
        copy.start()
        stores.append(copy)

    top, bottom = pl.ds(0, 256), pl.ds(256, 256)
    output_here[top] = (near_out[top] + last_below[top].astype(jnp.float32)).astype(jnp.bfloat16)
    store(output_here.at[top], output.at[top])
    output_here[bottom] = (near_out[bottom] + last_below[bottom].astype(jnp.float32)).astype(jnp.bfloat16)
    store(output_here.at[bottom], output.at[bottom])
    twice = repeat_matrix(64, 2)
    four = repeat_matrix(64, 4)
    coarse = mm(four, from_next[192:256], NN)
    low = mm(four, from_prev[192:256], NN)
    first = own[0:128].astype(jnp.float32) + coarse[0:128] + from_prev[0:128].astype(jnp.float32)
    second = own[128:256].astype(jnp.float32) + coarse[128:256] + mm(twice, from_prev[128:192], NN)
    third = own[256:384].astype(jnp.float32) + low[0:128] + mm(twice, from_next[128:192], NN)
    fourth = own[384:512].astype(jnp.float32) + low[128:256] + from_next[0:128].astype(jnp.float32)
    for number, part in enumerate((first, second, third, fourth)):
        span = pl.ds(128 * number, 128)
        part = part.astype(jnp.bfloat16)
        grad_keys_here[span] = part[:, :width]
        grad_values_here[span] = part[:, width:]
        if number % 2:
            half = pl.ds(128 * (number - 1), 256)
            store(grad_keys_here.at[half], grad_keys.at[half])
            store(grad_values_here.at[half], grad_values.at[half])
    for copy in loads:
        copy.wait()
    grad_weight_here[...] = jnp.sum(spread_here[...].astype(jnp.float32), axis=0)
    store(grad_weight_here, grad_weight)
    for copy in stores:
        copy.wait()


def local(queries, keys, values, out_weight, grad_out):
    bf16, f32 = jnp.bfloat16, jnp.float32
    rows, width = queries.shape
    shards = lax.axis_size("seq")
    heads = lax.axis_size("head")
    features = out_weight.shape[0]
    up = [(i, (i + 1) % heads) for i in range(heads)]
    down = [(target, source) for source, target in up]
    swap = [(i, i ^ 1) for i in range(shards)]
    onward = [(i, (i + 1) % shards) for i in range(shards)]
    back = [(target, source) for source, target in onward]
    dma = pltpu.SemaphoreType.DMA

    first_cot = lax.ppermute(grad_out, "head", down)
    second_cot = lax.ppermute(grad_out, "head", up)

    mine, to_next, to_prev = run(
        prepare, (keys, values),
        [((512, 2 * width), bf16), ((256, 2 * width), bf16), ((256, 2 * width), bf16)],
        flops=2 * 384 * 512 * 512, moved=1 << 20)
    before = lax.ppermute(to_next, "seq", onward)
    after = lax.ppermute(to_prev, "seq", back)
    queries, out_weight = run(
        fetch, (queries, out_weight, to_next), [((rows, width), bf16), ((features, width), bf16)],
        moved=2 << 20, far_args=(2,))
    tops, totals, sums = run(
        forward_own, (queries, mine, to_next),
        [((2, rows), f32), ((2, rows), f32), ((2 * HEAD_DIM, rows), f32)],
        [pltpu.VMEM((256, 2 * width), bf16)], flops=10 ** 9, moved=2 << 20, far_args=(2,))
    opposite = lax.ppermute(first_cot, "head", down)

    attention, residue, lse, own_out, first_up, second_up, first_down = run(
        forward, (queries, before, after, out_weight, tops, totals, sums),
        [((rows, width), bf16), ((rows, width), bf16), ((2, rows), f32), ((rows, width), bf16), ((rows, width), bf16),
         ((rows, width), bf16), ((rows, width), bf16)],
        [pltpu.VMEM((768, 2 * width), bf16)], flops=10 ** 9, moved=3 << 20)
    from_below = lax.ppermute(first_up, "head", up)
    from_above = lax.ppermute(first_down, "head", down)

    chunk = features // shards
    shapes = [((shards // 2, chunk, width), f32), ((shards // 2, chunk, width), bf16)]
    keep, send, part = run(
        near_products, (grad_out, first_cot, second_cot, attention, out_weight), shapes + [((rows, width), f32)],
        flops=4 * 10 ** 8, moved=1 << 20)
    keep, send, grad_attention, deltas = run(
        far_products, (opposite, attention, residue, out_weight, keep, send, part),
        shapes + [((rows, width), bf16), ((2, rows), f32)])
    half_sum = lax.ppermute(send, "seq", swap)
    pairs, = run(pair_sum, (keep, half_sum), [((shards // 2, chunk, width), bf16)],
                 [pltpu.VMEM((shards // 2, chunk, width), bf16), dma((PIECES,))], far_outs=(0,))
    groups = [list(range(core, shards, 2)) for core in range(2)]
    spread = lax.all_to_all(pairs, "seq", 0, 0, axis_index_groups=groups)

    dscores, to_next, to_prev, edge, send_up, near_out = run(
        backward,
        (queries, before, after, lse, grad_attention, deltas, second_up, from_below, own_out, from_above),
        [((4, 512, 256), bf16), ((256, 2 * width), bf16), ((256, 2 * width), bf16), ((768, 2 * width), bf16),
         ((rows, width), bf16), ((rows, width), f32)],
        [pltpu.VMEM((1536, 2 * width), f32)], flops=2 * 10 ** 9, moved=4 << 20)
    last_below = lax.ppermute(send_up, "head", up)
    grad_before = lax.ppermute(to_next, "seq", onward)
    grad_after = lax.ppermute(to_prev, "seq", back)
    grad_queries, own_grad = run(
        own_grads, (queries, mine, edge, lse, grad_attention, deltas, dscores),
        [((rows, width), bf16), ((rows, 2 * width), bf16)],
        [pltpu.VMEM((1536, 2 * width), f32), pltpu.VMEM((256, 2 * width), bf16), pltpu.VMEM((rows, width), bf16), dma((2,))],
        flops=3 * 10 ** 9, moved=6 << 20, far_outs=(0,))

    output, grad_keys, grad_values, grad_weight = run(
        finish,
        (near_out, last_below, own_grad, grad_before, grad_after, spread),
        [((rows, width), bf16)] * 3 + [((chunk, width), f32)],
        [pltpu.VMEM((rows, width), bf16)] * 3 + [pltpu.VMEM((chunk, width), f32)]
        + [pltpu.VMEM((shards // 2, chunk, width), bf16), dma((PIECES,)), dma((7,))],
        moved=4 << 20, far_args=(5,), far_outs=(0, 1, 2, 3))
    return output, grad_queries, grad_keys, grad_values, grad_weight


def solution(mesh):
    split = P("seq", "head")
    return jax.shard_map(
        local, mesh=mesh, in_specs=(split, split, split, P(None, "head"), split),
        out_specs=(split,) * 5, check_vma=False)
```

```python
import math

import jax
import jax.numpy as jnp
from jax import lax
from jax.experimental import pallas as pl
from jax.experimental.pallas import tpu as pltpu
from jax.sharding import PartitionSpec as P

HEAD_DIM = 128
BLOCK = 128
SCALE = HEAD_DIM ** -0.5
LOG2 = SCALE / math.log(2.0)
NEG = -1e30
VMEM = pl.BlockSpec(memory_space=pltpu.VMEM)
FAR = pl.BlockSpec(memory_space=pl.ANY)
PIECES = 4
NT = (((1,), (1,)), ((), ()))
TN = (((0,), (0,)), ((), ()))
NN = (((1,), (0,)), ((), ()))


def mm(a, b, dims):
    return lax.dot_general(a, b, dims, preferred_element_type=jnp.float32)


def run(body, args, outs, scratch=(), flops=0, moved=0, far_args=(), far_outs=(), room=24):
    return pl.pallas_call(
        body,
        in_specs=[FAR if number in far_args else VMEM for number in range(len(args))],
        out_shape=[jax.ShapeDtypeStruct(shape, kind) for shape, kind in outs],
        out_specs=[FAR if number in far_outs else VMEM for number in range(len(outs))],
        scratch_shapes=list(scratch),
        cost_estimate=pl.CostEstimate(flops=flops, bytes_accessed=moved, transcendentals=0),
        compiler_params=pltpu.CompilerParams(vmem_limit_bytes=room * 1024 * 1024),
    )(*args)


def pool_matrix(rows, factor):
    row = lax.broadcasted_iota(jnp.int32, (rows, rows * factor), 0)
    col = lax.broadcasted_iota(jnp.int32, (rows, rows * factor), 1)
    inside = (col >= row * factor) & (col < row * factor + factor)
    return jnp.where(inside, 1.0 / factor, 0.0).astype(jnp.bfloat16)


def repeat_matrix(rows, factor):
    row = lax.broadcasted_iota(jnp.int32, (rows * factor, rows), 0)
    col = lax.broadcasted_iota(jnp.int32, (rows * factor, rows), 1)
    inside = (row >= col * factor) & (row < col * factor + factor)
    return jnp.where(inside, 1.0, 0.0).astype(jnp.bfloat16)


def repeated(part, factor):
    matrix = repeat_matrix(part.shape[0], factor)
    high = part.astype(jnp.bfloat16)
    low = (part - high.astype(jnp.float32)).astype(jnp.bfloat16)
    return mm(matrix, high, NN) + mm(matrix, low, NN)


def in_pieces(source, target, sems):
    count = sems.shape[0]
    size = source.shape[0] // count
    return [pltpu.make_async_copy(source.at[pl.ds(number * size, size)], target.at[pl.ds(number * size, size)],
                                  sems.at[number]) for number in range(count)]


def on_even():
    return lax.rem(lax.axis_index("seq"), 2) == 0


def prepare(keys, values, mine, to_next, to_prev):
    width = keys.shape[1]
    two = pool_matrix(256, 2)
    four = pool_matrix(64, 4)
    for number, source in enumerate((keys, values)):
        cols = slice(number * width, (number + 1) * width)
        mine[:, cols] = source[...]
        first = mm(two, source[...], NN).astype(jnp.bfloat16)
        to_next[0:128, cols] = source[384:512]
        to_next[128:192, cols] = first[128:192]
        to_next[192:256, cols] = mm(four, source[0:256], NN).astype(jnp.bfloat16)
        to_prev[0:128, cols] = source[0:128]
        to_prev[128:192, cols] = first[64:128]
        to_prev[192:256, cols] = mm(four, source[256:512], NN).astype(jnp.bfloat16)


def fetch(queries, weight, _, queries_here, weight_here):
    queries_here[...] = queries[...]
    weight_here[...] = weight[...]


def widen(before, after, edge):
    half = pool_matrix(64, 2)
    both = pool_matrix(32, 2)
    quarter = pool_matrix(32, 4)
    edge[0:128] = before[0:128]
    edge[128:256] = after[0:128]
    edge[256:320] = before[128:192]
    edge[320:384] = mm(half, before[0:128], NN).astype(jnp.bfloat16)
    edge[384:448] = mm(half, after[0:128], NN).astype(jnp.bfloat16)
    edge[448:512] = after[128:192]
    edge[512:576] = before[192:256]
    edge[576:608] = mm(both, before[128:192], NN).astype(jnp.bfloat16)
    edge[608:640] = mm(quarter, before[0:128], NN).astype(jnp.bfloat16)
    edge[640:672] = mm(quarter, after[0:128], NN).astype(jnp.bfloat16)
    edge[672:704] = mm(both, after[128:192], NN).astype(jnp.bfloat16)
    edge[704:768] = after[192:256]


def own_set(half, mine, pooled):
    both = (0, 256)
    if half == 0:
        return [(mine, 0, 128, 0, both), (mine, 128, 256, 0, both), (mine, 256, 384, 0, (128, 256)), (pooled, 128, 1024, 1, both)]
    return [(mine, 128, 256, 0, (0, 128)), (mine, 256, 384, 0, both), (mine, 384, 512, 0, both), (pooled, 0, 896, 1, both)]


def edge_set(half, edge):
    place = lax.axis_index("seq")
    has_prev = place > 0
    has_next = place < lax.axis_size("seq") - 1
    both = (0, 256)
    far = [(edge, 512, 1280, 2, both, has_prev), (edge, 640, 1408, 2, both, has_next)]
    if half == 0:
        return [(edge, 0, 0, 0, (0, 128), has_prev), (edge, 256, 768, 1, both, has_prev)] + far
    return [(edge, 128, 640, 0, (128, 256), has_next), (edge, 384, 1152, 1, both, has_next)] + far


def logits_of(blocks, mine_q, cols):
    scores = []
    for source, row, _, level, seen, *there in blocks:
        score = mm(source[row:row + 128, cols], mine_q, NT) * LOG2
        if there:
            score = score + jnp.where(there[0], float(level), NEG)
        elif level:
            score = score + float(level)
        empty = jnp.full((128, 128), NEG, jnp.float32)
        if seen == (0, 128):
            score = jnp.concatenate([score[:, :128], empty], axis=1)
        if seen == (128, 256):
            score = jnp.concatenate([empty, score[:, 128:]], axis=1)
        scores.append(score)
    return scores


def gather(blocks, scores, top, value_cols):
    total = jnp.zeros((128, 256), jnp.float32)
    summed = jnp.zeros((128, 256), jnp.float32)
    for (source, row, *_), score in zip(blocks, scores):
        expd = jnp.exp2(score - top)
        total = total + expd
        summed = summed + mm(source[row:row + 128, value_cols], expd.astype(jnp.bfloat16), TN)
    return jnp.sum(total, axis=0, keepdims=True), summed


def top_of(scores):
    top = scores[0]
    for score in scores[1:]:
        top = jnp.maximum(top, score)
    return jnp.max(top, axis=0, keepdims=True)


def forward_own(queries, mine, _, tops, totals, sums, pooled):
    pooled[...] = mm(pool_matrix(256, 2), mine[...], NN).astype(jnp.bfloat16)
    width = queries.shape[1]
    for head in range(2):
        cols = slice(head * 128, head * 128 + 128)
        value_cols = slice(width + head * 128, width + head * 128 + 128)
        for half in range(2):
            span = slice(256 * half, 256 * half + 256)
            blocks = own_set(half, mine, pooled)
            scores = logits_of(blocks, queries[span, cols], cols)
            top = top_of(scores)
            tops[head:head + 1, span] = top
            totals[head:head + 1, span], sums[head * 128:head * 128 + 128, span] = gather(blocks, scores, top, value_cols)


def forward(queries, before, after, weight, tops, totals, sums,
            attention, residue, lse, own, first_up, second_up, first_down, edge):
    widen(before, after, edge)
    width = queries.shape[1]
    for head in range(2):
        cols = slice(head * 128, head * 128 + 128)
        value_cols = slice(width + head * 128, width + head * 128 + 128)
        for half in range(2):
            span = slice(256 * half, 256 * half + 256)
            blocks = edge_set(half, edge)
            scores = logits_of(blocks, queries[span, cols], cols)
            before_top = tops[head:head + 1, span]
            top = jnp.maximum(before_top, top_of(scores))
            total, summed = gather(blocks, scores, top, value_cols)
            scale = jnp.exp2(before_top - top)
            total = total + scale * totals[head:head + 1, span]
            lse[head:head + 1, span] = top + jnp.log2(total)
            result = ((summed + scale * sums[head * 128:head * 128 + 128, span]) / total).T
            rounded = result.astype(jnp.bfloat16)
            attention[span, cols] = rounded
            residue[span, cols] = (result - rounded.astype(jnp.float32)).astype(jnp.bfloat16)
    heads = lax.axis_size("head")
    here = lax.axis_index("head")

    def partial_to(target):
        start = pl.multiple_of(lax.rem(target, heads) * width, width)
        return mm(attention[...], weight[pl.ds(start, width), :], NT)

    own[...] = partial_to(here).astype(jnp.bfloat16)
    first_up[...] = partial_to(here + 2).astype(jnp.bfloat16)
    second_up[...] = partial_to(here + 1).astype(jnp.bfloat16)
    first_down[...] = partial_to(here + 3).astype(jnp.bfloat16)


def product_of(shift, cot, attention, weight, keep, send):
    heads = lax.axis_size("head")
    owner = lax.rem(lax.axis_index("head") + shift, heads)
    even = on_even()
    groups, rows, width = keep.shape
    each = groups // heads
    chunks = mm(cot[...], attention[...], TN).reshape(each, 2, rows, width)
    first, second = chunks[:, 0], chunks[:, 1]
    start = owner * each
    keep[pl.ds(start, each)] = jnp.where(even, first, second)
    send[pl.ds(start, each)] = jnp.where(even, second, first).astype(jnp.bfloat16)
    return mm(cot[...], weight[pl.ds(pl.multiple_of(owner * width, width), width), :], NN)


def near_products(mine, first_cot, second_cot, attention, weight, keep, send, part):
    heads = lax.axis_size("head")
    part[...] = (product_of(0, mine, attention, weight, keep, send)
                 + product_of(1, first_cot, attention, weight, keep, send)
                 + product_of(heads - 1, second_cot, attention, weight, keep, send))


def far_products(opposite, attention, residue, weight, near_keep, near_send, part, keep, send, grad_attention, deltas):
    keep[...] = near_keep[...]
    send[...] = near_send[...]
    rounded = (part[...] + product_of(2, opposite, attention, weight, keep, send)).astype(jnp.bfloat16)
    grad_attention[...] = rounded
    terms = rounded.astype(jnp.float32) * (attention[...].astype(jnp.float32) + residue[...].astype(jnp.float32))
    ones = jnp.ones((16, HEAD_DIM), jnp.bfloat16)
    sums = [jnp.zeros((16, terms.shape[0]), jnp.float32)] * 2
    for _ in range(3):
        part_of = terms.astype(jnp.bfloat16)
        terms = terms - part_of.astype(jnp.float32)
        sums = [sums[head] + mm(ones, part_of[:, head * HEAD_DIM:head * HEAD_DIM + HEAD_DIM], NT) for head in range(2)]
    for head in range(2):
        deltas[head:head + 1] = sums[head][0:1]


def pair_sum(keep, sibling, pairs, pairs_here, sems):
    stores = in_pieces(pairs_here, pairs, sems)
    size = pairs.shape[0] // len(stores)
    for number, store in enumerate(stores):
        span = pl.ds(number * size, size)
        pairs_here[span] = (keep[span] + sibling[span].astype(jnp.float32)).astype(jnp.bfloat16)
        store.start()
    for store in stores:
        store.wait()


def score_grads(blocks, scores, norm, delta, cot, value_cols):
    pairs = []
    for (source, row, *_), score in zip(blocks, scores):
        prob = jnp.exp2(score - norm)
        dprob = mm(source[row:row + 128, value_cols], cot, NT)
        pairs.append((prob.astype(jnp.bfloat16), (prob * (dprob - delta)).astype(jnp.bfloat16)))
    return pairs


def backward(queries, before, after, lse, grad_attention, deltas, second_up, from_below,
             dscores, to_next, to_prev, edge, send_up, total):
    send_up[...] = (second_up[...].astype(jnp.float32) + from_below[...].astype(jnp.float32)).astype(jnp.bfloat16)
    widen(before, after, edge)
    width = queries.shape[1]
    for half in range(2):
        span = slice(256 * half, 256 * half + 256)
        blocks = edge_set(half, edge)
        for head in range(2):
            cols = slice(head * 128, head * 128 + 128)
            value_cols = slice(width + head * 128, width + head * 128 + 128)
            mine_q = queries[span, cols]
            cot = grad_attention[span, cols]
            pairs = score_grads(blocks, logits_of(blocks, mine_q, cols), lse[head:head + 1, span],
                                deltas[head:head + 1, span], cot, value_cols)
            for number, ((_, _, at, *_), (prob, dscore)) in enumerate(zip(blocks, pairs)):
                dscores[2 * half + head, 128 * number:128 * number + 128] = dscore
                grad_k = mm(dscore, mine_q, NN) * SCALE
                grad_v = mm(prob, cot, NN)
                if half == 1 and at >= 1280:
                    total[at:at + 128, cols] += grad_k
                    total[at:at + 128, value_cols] += grad_v
                else:
                    total[at:at + 128, cols] = grad_k
                    total[at:at + 128, value_cols] = grad_v
    to_prev[0:128] = (total[0:128] + repeated(total[832:896] * 0.5, 2)
                      + repeated(total[1376:1408] * 0.25, 4)).astype(jnp.bfloat16)
    to_prev[128:192] = (total[768:832] * 0.5 + repeated(total[1344:1376] * 0.25, 2)).astype(jnp.bfloat16)
    to_prev[192:256] = (total[1280:1344] * 0.25).astype(jnp.bfloat16)
    to_next[0:128] = (total[640:768] + repeated(total[1152:1216] * 0.5, 2)
                      + repeated(total[1408:1440] * 0.25, 4)).astype(jnp.bfloat16)
    to_next[128:192] = (total[1216:1280] * 0.5 + repeated(total[1440:1472] * 0.25, 2)).astype(jnp.bfloat16)
    to_next[192:256] = (total[1472:1536] * 0.25).astype(jnp.bfloat16)


def own_grads(queries, mine, edge, lse, grad_attention, deltas, dscores, own_part, from_above,
              grad_queries, own, near, total, pooled, grad_q_here, sems):
    pooled[...] = mm(pool_matrix(256, 2), mine[...], NN).astype(jnp.bfloat16)
    near[...] = own_part[...].astype(jnp.float32) + from_above[...].astype(jnp.float32)
    stores = []
    width = queries.shape[1]
    for half in range(2):
        span = slice(256 * half, 256 * half + 256)
        blocks = own_set(half, mine, pooled)
        for head in range(2):
            cols = slice(head * 128, head * 128 + 128)
            value_cols = slice(width + head * 128, width + head * 128 + 128)
            mine_q = queries[span, cols]
            cot = grad_attention[span, cols]
            pairs = score_grads(blocks, logits_of(blocks, mine_q, cols), lse[head:head + 1, span],
                                deltas[head:head + 1, span], cot, value_cols)
            grad_q = jnp.zeros((128, 256), jnp.float32)
            for number, (source, row, *_) in enumerate(edge_set(half, edge)):
                grad_q = grad_q + mm(source[row:row + 128, cols], dscores[2 * half + head, 128 * number:128 * number + 128], TN)
            for (source, row, at, *_), (prob, dscore) in zip(blocks, pairs):
                grad_q = grad_q + mm(source[row:row + 128, cols], dscore, TN)
                grad_k = mm(dscore, mine_q, NN) * SCALE
                grad_v = mm(prob, cot, NN)
                if half == 1 and 256 <= at < 512:
                    total[at:at + 128, cols] += grad_k
                    total[at:at + 128, value_cols] += grad_v
                else:
                    total[at:at + 128, cols] = grad_k
                    total[at:at + 128, value_cols] = grad_v
            grad_q_here[span, cols] = (grad_q * SCALE).T.astype(jnp.bfloat16)
        store = pltpu.make_async_copy(grad_q_here.at[span], grad_queries.at[span], sems.at[half])
        store.start()
        stores.append(store)
    own[...] = (total[128:640] + repeated(total[896:1152] * 0.5, 2)).astype(jnp.bfloat16)
    for store in stores:
        store.wait()


def finish(near_out, last_below, own, from_prev, from_next, spread,
           output, grad_keys, grad_values, grad_weight,
           output_here, grad_keys_here, grad_values_here, grad_weight_here, spread_here, load_sems, sems):
    loads = in_pieces(spread, spread_here, load_sems)
    for copy in loads:
        copy.start()
    width = grad_keys.shape[1]
    stores = []

    def store(source, target):
        copy = pltpu.make_async_copy(source, target, sems.at[len(stores)])
        copy.start()
        stores.append(copy)

    top, bottom = pl.ds(0, 256), pl.ds(256, 256)
    output_here[top] = (near_out[top] + last_below[top].astype(jnp.float32)).astype(jnp.bfloat16)
    store(output_here.at[top], output.at[top])
    output_here[bottom] = (near_out[bottom] + last_below[bottom].astype(jnp.float32)).astype(jnp.bfloat16)
    store(output_here.at[bottom], output.at[bottom])
    twice = repeat_matrix(64, 2)
    four = repeat_matrix(64, 4)
    coarse = mm(four, from_next[192:256], NN)
    low = mm(four, from_prev[192:256], NN)
    first = own[0:128].astype(jnp.float32) + coarse[0:128] + from_prev[0:128].astype(jnp.float32)
    second = own[128:256].astype(jnp.float32) + coarse[128:256] + mm(twice, from_prev[128:192], NN)
    third = own[256:384].astype(jnp.float32) + low[0:128] + mm(twice, from_next[128:192], NN)
    fourth = own[384:512].astype(jnp.float32) + low[128:256] + from_next[0:128].astype(jnp.float32)
    for number, part in enumerate((first, second, third, fourth)):
        span = pl.ds(128 * number, 128)
        part = part.astype(jnp.bfloat16)
        grad_keys_here[span] = part[:, :width]
        grad_values_here[span] = part[:, width:]
        if number % 2:
            half = pl.ds(128 * (number - 1), 256)
            store(grad_keys_here.at[half], grad_keys.at[half])
            store(grad_values_here.at[half], grad_values.at[half])
    for copy in loads:
        copy.wait()
    grad_weight_here[...] = jnp.sum(spread_here[...].astype(jnp.float32), axis=0)
    store(grad_weight_here, grad_weight)
    for copy in stores:
        copy.wait()


def local(queries, keys, values, out_weight, grad_out):
    bf16, f32 = jnp.bfloat16, jnp.float32
    rows, width = queries.shape
    shards = lax.axis_size("seq")
    heads = lax.axis_size("head")
    features = out_weight.shape[0]
    up = [(i, (i + 1) % heads) for i in range(heads)]
    down = [(target, source) for source, target in up]
    swap = [(i, i ^ 1) for i in range(shards)]
    onward = [(i, (i + 1) % shards) for i in range(shards)]
    back = [(target, source) for source, target in onward]
    dma = pltpu.SemaphoreType.DMA

    first_cot = lax.ppermute(grad_out, "head", down)
    second_cot = lax.ppermute(grad_out, "head", up)

    mine, to_next, to_prev = run(
        prepare, (keys, values),
        [((512, 2 * width), bf16), ((256, 2 * width), bf16), ((256, 2 * width), bf16)],
        flops=2 * 384 * 512 * 512, moved=1 << 20)
    before = lax.ppermute(to_next, "seq", onward)
    after = lax.ppermute(to_prev, "seq", back)
    queries, out_weight = run(
        fetch, (queries, out_weight, to_next), [((rows, width), bf16), ((features, width), bf16)],
        moved=2 << 20, far_args=(2,))
    tops, totals, sums = run(
        forward_own, (queries, mine, to_next),
        [((2, rows), f32), ((2, rows), f32), ((2 * HEAD_DIM, rows), f32)],
        [pltpu.VMEM((256, 2 * width), bf16)], flops=10 ** 9, moved=2 << 20, far_args=(2,))
    opposite = lax.ppermute(first_cot, "head", down)

    attention, residue, lse, own_out, first_up, second_up, first_down = run(
        forward, (queries, before, after, out_weight, tops, totals, sums),
        [((rows, width), bf16), ((rows, width), bf16), ((2, rows), f32), ((rows, width), bf16), ((rows, width), bf16),
         ((rows, width), bf16), ((rows, width), bf16)],
        [pltpu.VMEM((768, 2 * width), bf16)], flops=10 ** 9, moved=3 << 20)
    from_below = lax.ppermute(first_up, "head", up)
    from_above = lax.ppermute(first_down, "head", down)

    chunk = features // shards
    shapes = [((shards // 2, chunk, width), f32), ((shards // 2, chunk, width), bf16)]
    keep, send, part = run(
        near_products, (grad_out, first_cot, second_cot, attention, out_weight), shapes + [((rows, width), f32)],
        flops=4 * 10 ** 8, moved=1 << 20)
    keep, send, grad_attention, deltas = run(
        far_products, (opposite, attention, residue, out_weight, keep, send, part),
        shapes + [((rows, width), bf16), ((2, rows), f32)])
    half_sum = lax.ppermute(send, "seq", swap)
    pairs, = run(pair_sum, (keep, half_sum), [((shards // 2, chunk, width), bf16)],
                 [pltpu.VMEM((shards // 2, chunk, width), bf16), dma((PIECES,))], far_outs=(0,))
    groups = [list(range(core, shards, 2)) for core in range(2)]
    spread = lax.all_to_all(pairs, "seq", 0, 0, axis_index_groups=groups)

    dscores, to_next, to_prev, edge, send_up = run(
        backward,
        (queries, before, after, lse, grad_attention, deltas, second_up, from_below),
        [((4, 512, 256), bf16), ((256, 2 * width), bf16), ((256, 2 * width), bf16), ((768, 2 * width), bf16),
         ((rows, width), bf16)],
        [pltpu.VMEM((1536, 2 * width), f32)], flops=2 * 10 ** 9, moved=4 << 20)
    last_below = lax.ppermute(send_up, "head", up)
    grad_before = lax.ppermute(to_next, "seq", onward)
    grad_after = lax.ppermute(to_prev, "seq", back)
    grad_queries, own_grad, near_out = run(
        own_grads, (queries, mine, edge, lse, grad_attention, deltas, dscores, own_out, from_above),
        [((rows, width), bf16), ((rows, 2 * width), bf16), ((rows, width), f32)],
        [pltpu.VMEM((1536, 2 * width), f32), pltpu.VMEM((256, 2 * width), bf16), pltpu.VMEM((rows, width), bf16), dma((2,))],
        flops=3 * 10 ** 9, moved=6 << 20, far_outs=(0,))

    output, grad_keys, grad_values, grad_weight = run(
        finish,
        (near_out, last_below, own_grad, grad_before, grad_after, spread),
        [((rows, width), bf16)] * 3 + [((chunk, width), f32)],
        [pltpu.VMEM((rows, width), bf16)] * 3 + [pltpu.VMEM((chunk, width), f32)]
        + [pltpu.VMEM((shards // 2, chunk, width), bf16), dma((PIECES,)), dma((7,))],
        moved=4 << 20, far_args=(5,), far_outs=(0, 1, 2, 3))
    return output, grad_queries, grad_keys, grad_values, grad_weight


def solution(mesh):
    split = P("seq", "head")
    return jax.shard_map(
        local, mesh=mesh, in_specs=(split, split, split, P(None, "head"), split),
        out_specs=(split,) * 5, check_vma=False)
```

```python
import math

import jax
import jax.numpy as jnp
from jax import lax
from jax.experimental import pallas as pl
from jax.experimental.pallas import tpu as pltpu
from jax.sharding import PartitionSpec as P

HEAD_DIM = 128
BLOCK = 128
SCALE = HEAD_DIM ** -0.5
LOG2 = SCALE / math.log(2.0)
NEG = -1e30
VMEM = pl.BlockSpec(memory_space=pltpu.VMEM)
FAR = pl.BlockSpec(memory_space=pl.ANY)
PIECES = 8
NT = (((1,), (1,)), ((), ()))
TN = (((0,), (0,)), ((), ()))
NN = (((1,), (0,)), ((), ()))


def mm(a, b, dims):
    return lax.dot_general(a, b, dims, preferred_element_type=jnp.float32)


def run(body, args, outs, scratch=(), flops=0, moved=0, far_args=(), far_outs=(), room=24):
    return pl.pallas_call(
        body,
        in_specs=[FAR if number in far_args else VMEM for number in range(len(args))],
        out_shape=[jax.ShapeDtypeStruct(shape, kind) for shape, kind in outs],
        out_specs=[FAR if number in far_outs else VMEM for number in range(len(outs))],
        scratch_shapes=list(scratch),
        cost_estimate=pl.CostEstimate(flops=flops, bytes_accessed=moved, transcendentals=0),
        compiler_params=pltpu.CompilerParams(vmem_limit_bytes=room * 1024 * 1024),
    )(*args)


def pool_matrix(rows, factor):
    row = lax.broadcasted_iota(jnp.int32, (rows, rows * factor), 0)
    col = lax.broadcasted_iota(jnp.int32, (rows, rows * factor), 1)
    inside = (col >= row * factor) & (col < row * factor + factor)
    return jnp.where(inside, 1.0 / factor, 0.0).astype(jnp.bfloat16)


def repeat_matrix(rows, factor):
    row = lax.broadcasted_iota(jnp.int32, (rows * factor, rows), 0)
    col = lax.broadcasted_iota(jnp.int32, (rows * factor, rows), 1)
    inside = (row >= col * factor) & (row < col * factor + factor)
    return jnp.where(inside, 1.0, 0.0).astype(jnp.bfloat16)


def repeated(part, factor):
    matrix = repeat_matrix(part.shape[0], factor)
    high = part.astype(jnp.bfloat16)
    low = (part - high.astype(jnp.float32)).astype(jnp.bfloat16)
    return mm(matrix, high, NN) + mm(matrix, low, NN)


def in_pieces(source, target, sems):
    count = sems.shape[0]
    size = source.shape[0] // count
    return [pltpu.make_async_copy(source.at[pl.ds(number * size, size)], target.at[pl.ds(number * size, size)],
                                  sems.at[number]) for number in range(count)]


def on_even():
    return lax.rem(lax.axis_index("seq"), 2) == 0


def prepare(keys, values, mine, to_next, to_prev):
    width = keys.shape[1]
    two = pool_matrix(256, 2)
    four = pool_matrix(64, 4)
    for number, source in enumerate((keys, values)):
        cols = slice(number * width, (number + 1) * width)
        mine[:, cols] = source[...]
        first = mm(two, source[...], NN).astype(jnp.bfloat16)
        to_next[0:128, cols] = source[384:512]
        to_next[128:192, cols] = first[128:192]
        to_next[192:256, cols] = mm(four, source[0:256], NN).astype(jnp.bfloat16)
        to_prev[0:128, cols] = source[0:128]
        to_prev[128:192, cols] = first[64:128]
        to_prev[192:256, cols] = mm(four, source[256:512], NN).astype(jnp.bfloat16)


def fetch(queries, weight, _, queries_here, weight_here):
    queries_here[...] = queries[...]
    weight_here[...] = weight[...]


def widen(before, after, edge):
    half = pool_matrix(64, 2)
    both = pool_matrix(32, 2)
    quarter = pool_matrix(32, 4)
    edge[0:128] = before[0:128]
    edge[128:256] = after[0:128]
    edge[256:320] = before[128:192]
    edge[320:384] = mm(half, before[0:128], NN).astype(jnp.bfloat16)
    edge[384:448] = mm(half, after[0:128], NN).astype(jnp.bfloat16)
    edge[448:512] = after[128:192]
    edge[512:576] = before[192:256]
    edge[576:608] = mm(both, before[128:192], NN).astype(jnp.bfloat16)
    edge[608:640] = mm(quarter, before[0:128], NN).astype(jnp.bfloat16)
    edge[640:672] = mm(quarter, after[0:128], NN).astype(jnp.bfloat16)
    edge[672:704] = mm(both, after[128:192], NN).astype(jnp.bfloat16)
    edge[704:768] = after[192:256]


def own_set(half, mine, pooled):
    both = (0, 256)
    if half == 0:
        return [(mine, 0, 128, 0, both), (mine, 128, 256, 0, both), (mine, 256, 384, 0, (128, 256)), (pooled, 128, 1024, 1, both)]
    return [(mine, 128, 256, 0, (0, 128)), (mine, 256, 384, 0, both), (mine, 384, 512, 0, both), (pooled, 0, 896, 1, both)]


def edge_set(half, edge):
    place = lax.axis_index("seq")
    has_prev = place > 0
    has_next = place < lax.axis_size("seq") - 1
    both = (0, 256)
    far = [(edge, 512, 1280, 2, both, has_prev), (edge, 640, 1408, 2, both, has_next)]
    if half == 0:
        return [(edge, 0, 0, 0, (0, 128), has_prev), (edge, 256, 768, 1, both, has_prev)] + far
    return [(edge, 128, 640, 0, (128, 256), has_next), (edge, 384, 1152, 1, both, has_next)] + far


def logits_of(blocks, mine_q, cols):
    scores = []
    for source, row, _, level, seen, *there in blocks:
        score = mm(source[row:row + 128, cols], mine_q, NT) * LOG2
        if there:
            score = score + jnp.where(there[0], float(level), NEG)
        elif level:
            score = score + float(level)
        empty = jnp.full((128, 128), NEG, jnp.float32)
        if seen == (0, 128):
            score = jnp.concatenate([score[:, :128], empty], axis=1)
        if seen == (128, 256):
            score = jnp.concatenate([empty, score[:, 128:]], axis=1)
        scores.append(score)
    return scores


def gather(blocks, scores, top, value_cols):
    total = jnp.zeros((128, 256), jnp.float32)
    summed = jnp.zeros((128, 256), jnp.float32)
    for (source, row, *_), score in zip(blocks, scores):
        expd = jnp.exp2(score - top)
        total = total + expd
        summed = summed + mm(source[row:row + 128, value_cols], expd.astype(jnp.bfloat16), TN)
    return jnp.sum(total, axis=0, keepdims=True), summed


def top_of(scores):
    top = scores[0]
    for score in scores[1:]:
        top = jnp.maximum(top, score)
    return jnp.max(top, axis=0, keepdims=True)


def forward_own(queries, mine, _, tops, totals, sums, pooled):
    pooled[...] = mm(pool_matrix(256, 2), mine[...], NN).astype(jnp.bfloat16)
    width = queries.shape[1]
    for head in range(2):
        cols = slice(head * 128, head * 128 + 128)
        value_cols = slice(width + head * 128, width + head * 128 + 128)
        for half in range(2):
            span = slice(256 * half, 256 * half + 256)
            blocks = own_set(half, mine, pooled)
            scores = logits_of(blocks, queries[span, cols], cols)
            top = top_of(scores)
            tops[head:head + 1, span] = top
            totals[head:head + 1, span], sums[head * 128:head * 128 + 128, span] = gather(blocks, scores, top, value_cols)


def forward(queries, before, after, weight, tops, totals, sums,
            attention, residue, lse, own, first_up, second_up, first_down, edge):
    widen(before, after, edge)
    width = queries.shape[1]
    for head in range(2):
        cols = slice(head * 128, head * 128 + 128)
        value_cols = slice(width + head * 128, width + head * 128 + 128)
        for half in range(2):
            span = slice(256 * half, 256 * half + 256)
            blocks = edge_set(half, edge)
            scores = logits_of(blocks, queries[span, cols], cols)
            before_top = tops[head:head + 1, span]
            top = jnp.maximum(before_top, top_of(scores))
            total, summed = gather(blocks, scores, top, value_cols)
            scale = jnp.exp2(before_top - top)
            total = total + scale * totals[head:head + 1, span]
            lse[head:head + 1, span] = top + jnp.log2(total)
            result = ((summed + scale * sums[head * 128:head * 128 + 128, span]) / total).T
            rounded = result.astype(jnp.bfloat16)
            attention[span, cols] = rounded
            residue[span, cols] = (result - rounded.astype(jnp.float32)).astype(jnp.bfloat16)
    heads = lax.axis_size("head")
    here = lax.axis_index("head")

    def partial_to(target):
        start = pl.multiple_of(lax.rem(target, heads) * width, width)
        return mm(attention[...], weight[pl.ds(start, width), :], NT)

    own[...] = partial_to(here).astype(jnp.bfloat16)
    first_up[...] = partial_to(here + 2).astype(jnp.bfloat16)
    second_up[...] = partial_to(here + 1).astype(jnp.bfloat16)
    first_down[...] = partial_to(here + 3).astype(jnp.bfloat16)


def product_of(shift, cot, attention, weight, keep, send):
    heads = lax.axis_size("head")
    owner = lax.rem(lax.axis_index("head") + shift, heads)
    even = on_even()
    groups, rows, width = keep.shape
    each = groups // heads
    chunks = mm(cot[...], attention[...], TN).reshape(each, 2, rows, width)
    first, second = chunks[:, 0], chunks[:, 1]
    start = owner * each
    keep[pl.ds(start, each)] = jnp.where(even, first, second)
    send[pl.ds(start, each)] = jnp.where(even, second, first).astype(jnp.bfloat16)
    return mm(cot[...], weight[pl.ds(pl.multiple_of(owner * width, width), width), :], NN)


def near_products(mine, first_cot, second_cot, attention, weight, keep, send, part):
    heads = lax.axis_size("head")
    part[...] = (product_of(0, mine, attention, weight, keep, send)
                 + product_of(1, first_cot, attention, weight, keep, send)
                 + product_of(heads - 1, second_cot, attention, weight, keep, send))


def far_products(opposite, attention, residue, weight, near_keep, near_send, part, keep, send, grad_attention, deltas):
    keep[...] = near_keep[...]
    send[...] = near_send[...]
    rounded = (part[...] + product_of(2, opposite, attention, weight, keep, send)).astype(jnp.bfloat16)
    grad_attention[...] = rounded
    terms = rounded.astype(jnp.float32) * (attention[...].astype(jnp.float32) + residue[...].astype(jnp.float32))
    ones = jnp.ones((16, HEAD_DIM), jnp.bfloat16)
    sums = [jnp.zeros((16, terms.shape[0]), jnp.float32)] * 2
    for _ in range(3):
        part_of = terms.astype(jnp.bfloat16)
        terms = terms - part_of.astype(jnp.float32)
        sums = [sums[head] + mm(ones, part_of[:, head * HEAD_DIM:head * HEAD_DIM + HEAD_DIM], NT) for head in range(2)]
    for head in range(2):
        deltas[head:head + 1] = sums[head][0:1]


def pair_sum(keep, sibling, pairs, pairs_here, sems):
    stores = in_pieces(pairs_here, pairs, sems)
    size = pairs.shape[0] // len(stores)
    for number, store in enumerate(stores):
        span = pl.ds(number * size, size)
        pairs_here[span] = (keep[span] + sibling[span].astype(jnp.float32)).astype(jnp.bfloat16)
        store.start()
    for store in stores:
        store.wait()


def score_grads(blocks, scores, norm, delta, cot, value_cols):
    pairs = []
    for (source, row, *_), score in zip(blocks, scores):
        prob = jnp.exp2(score - norm)
        dprob = mm(source[row:row + 128, value_cols], cot, NT)
        pairs.append((prob.astype(jnp.bfloat16), (prob * (dprob - delta)).astype(jnp.bfloat16)))
    return pairs


def backward(queries, before, after, lse, grad_attention, deltas, second_up, from_below,
             dscores, to_next, to_prev, edge, send_up, total):
    send_up[...] = (second_up[...].astype(jnp.float32) + from_below[...].astype(jnp.float32)).astype(jnp.bfloat16)
    widen(before, after, edge)
    width = queries.shape[1]
    for half in range(2):
        span = slice(256 * half, 256 * half + 256)
        blocks = edge_set(half, edge)
        for head in range(2):
            cols = slice(head * 128, head * 128 + 128)
            value_cols = slice(width + head * 128, width + head * 128 + 128)
            mine_q = queries[span, cols]
            cot = grad_attention[span, cols]
            pairs = score_grads(blocks, logits_of(blocks, mine_q, cols), lse[head:head + 1, span],
                                deltas[head:head + 1, span], cot, value_cols)
            for number, ((_, _, at, *_), (prob, dscore)) in enumerate(zip(blocks, pairs)):
                dscores[2 * half + head, 128 * number:128 * number + 128] = dscore
                grad_k = mm(dscore, mine_q, NN) * SCALE
                grad_v = mm(prob, cot, NN)
                if half == 1 and at >= 1280:
                    total[at:at + 128, cols] += grad_k
                    total[at:at + 128, value_cols] += grad_v
                else:
                    total[at:at + 128, cols] = grad_k
                    total[at:at + 128, value_cols] = grad_v
    to_prev[0:128] = (total[0:128] + repeated(total[832:896] * 0.5, 2)
                      + repeated(total[1376:1408] * 0.25, 4)).astype(jnp.bfloat16)
    to_prev[128:192] = (total[768:832] * 0.5 + repeated(total[1344:1376] * 0.25, 2)).astype(jnp.bfloat16)
    to_prev[192:256] = (total[1280:1344] * 0.25).astype(jnp.bfloat16)
    to_next[0:128] = (total[640:768] + repeated(total[1152:1216] * 0.5, 2)
                      + repeated(total[1408:1440] * 0.25, 4)).astype(jnp.bfloat16)
    to_next[128:192] = (total[1216:1280] * 0.5 + repeated(total[1440:1472] * 0.25, 2)).astype(jnp.bfloat16)
    to_next[192:256] = (total[1472:1536] * 0.25).astype(jnp.bfloat16)


def own_grads(queries, mine, edge, lse, grad_attention, deltas, dscores, own_part, from_above,
              grad_queries, own, near, total, pooled, grad_q_here, sems):
    pooled[...] = mm(pool_matrix(256, 2), mine[...], NN).astype(jnp.bfloat16)
    near[...] = own_part[...].astype(jnp.float32) + from_above[...].astype(jnp.float32)
    stores = []
    width = queries.shape[1]
    for half in range(2):
        span = slice(256 * half, 256 * half + 256)
        blocks = own_set(half, mine, pooled)
        for head in range(2):
            cols = slice(head * 128, head * 128 + 128)
            value_cols = slice(width + head * 128, width + head * 128 + 128)
            mine_q = queries[span, cols]
            cot = grad_attention[span, cols]
            pairs = score_grads(blocks, logits_of(blocks, mine_q, cols), lse[head:head + 1, span],
                                deltas[head:head + 1, span], cot, value_cols)
            grad_q = jnp.zeros((128, 256), jnp.float32)
            for number, (source, row, *_) in enumerate(edge_set(half, edge)):
                grad_q = grad_q + mm(source[row:row + 128, cols], dscores[2 * half + head, 128 * number:128 * number + 128], TN)
            for (source, row, at, *_), (prob, dscore) in zip(blocks, pairs):
                grad_q = grad_q + mm(source[row:row + 128, cols], dscore, TN)
                grad_k = mm(dscore, mine_q, NN) * SCALE
                grad_v = mm(prob, cot, NN)
                if half == 1 and 256 <= at < 512:
                    total[at:at + 128, cols] += grad_k
                    total[at:at + 128, value_cols] += grad_v
                else:
                    total[at:at + 128, cols] = grad_k
                    total[at:at + 128, value_cols] = grad_v
            grad_q_here[span, cols] = (grad_q * SCALE).T.astype(jnp.bfloat16)
        store = pltpu.make_async_copy(grad_q_here.at[span], grad_queries.at[span], sems.at[half])
        store.start()
        stores.append(store)
    own[...] = (total[128:640] + repeated(total[896:1152] * 0.5, 2)).astype(jnp.bfloat16)
    for store in stores:
        store.wait()


def finish(near_out, last_below, own, from_prev, from_next, spread,
           output, grad_keys, grad_values, grad_weight,
           output_here, grad_keys_here, grad_values_here, grad_weight_here, spread_here, load_sems, sems):
    loads = in_pieces(spread, spread_here, load_sems)
    for copy in loads:
        copy.start()
    width = grad_keys.shape[1]
    stores = []

    def store(source, target):
        copy = pltpu.make_async_copy(source, target, sems.at[len(stores)])
        copy.start()
        stores.append(copy)

    top, bottom = pl.ds(0, 256), pl.ds(256, 256)
    output_here[top] = (near_out[top] + last_below[top].astype(jnp.float32)).astype(jnp.bfloat16)
    store(output_here.at[top], output.at[top])
    output_here[bottom] = (near_out[bottom] + last_below[bottom].astype(jnp.float32)).astype(jnp.bfloat16)
    store(output_here.at[bottom], output.at[bottom])
    twice = repeat_matrix(64, 2)
    four = repeat_matrix(64, 4)
    coarse = mm(four, from_next[192:256], NN)
    low = mm(four, from_prev[192:256], NN)
    first = own[0:128].astype(jnp.float32) + coarse[0:128] + from_prev[0:128].astype(jnp.float32)
    second = own[128:256].astype(jnp.float32) + coarse[128:256] + mm(twice, from_prev[128:192], NN)
    third = own[256:384].astype(jnp.float32) + low[0:128] + mm(twice, from_next[128:192], NN)
    fourth = own[384:512].astype(jnp.float32) + low[128:256] + from_next[0:128].astype(jnp.float32)
    for number, part in enumerate((first, second, third, fourth)):
        span = pl.ds(128 * number, 128)
        part = part.astype(jnp.bfloat16)
        grad_keys_here[span] = part[:, :width]
        grad_values_here[span] = part[:, width:]
        if number % 2:
            half = pl.ds(128 * (number - 1), 256)
            store(grad_keys_here.at[half], grad_keys.at[half])
            store(grad_values_here.at[half], grad_values.at[half])
    for copy in loads:
        copy.wait()
    grad_weight_here[...] = jnp.sum(spread_here[...].astype(jnp.float32), axis=0)
    store(grad_weight_here, grad_weight)
    for copy in stores:
        copy.wait()


def local(queries, keys, values, out_weight, grad_out):
    bf16, f32 = jnp.bfloat16, jnp.float32
    rows, width = queries.shape
    shards = lax.axis_size("seq")
    heads = lax.axis_size("head")
    features = out_weight.shape[0]
    up = [(i, (i + 1) % heads) for i in range(heads)]
    down = [(target, source) for source, target in up]
    swap = [(i, i ^ 1) for i in range(shards)]
    onward = [(i, (i + 1) % shards) for i in range(shards)]
    back = [(target, source) for source, target in onward]
    dma = pltpu.SemaphoreType.DMA

    first_cot = lax.ppermute(grad_out, "head", down)
    second_cot = lax.ppermute(grad_out, "head", up)

    mine, to_next, to_prev = run(
        prepare, (keys, values),
        [((512, 2 * width), bf16), ((256, 2 * width), bf16), ((256, 2 * width), bf16)],
        flops=2 * 384 * 512 * 512, moved=1 << 20)
    before = lax.ppermute(to_next, "seq", onward)
    after = lax.ppermute(to_prev, "seq", back)
    queries, out_weight = run(
        fetch, (queries, out_weight, to_next), [((rows, width), bf16), ((features, width), bf16)],
        moved=2 << 20, far_args=(2,))
    tops, totals, sums = run(
        forward_own, (queries, mine, to_next),
        [((2, rows), f32), ((2, rows), f32), ((2 * HEAD_DIM, rows), f32)],
        [pltpu.VMEM((256, 2 * width), bf16)], flops=10 ** 9, moved=2 << 20, far_args=(2,))
    opposite = lax.ppermute(first_cot, "head", down)

    attention, residue, lse, own_out, first_up, second_up, first_down = run(
        forward, (queries, before, after, out_weight, tops, totals, sums),
        [((rows, width), bf16), ((rows, width), bf16), ((2, rows), f32), ((rows, width), bf16), ((rows, width), bf16),
         ((rows, width), bf16), ((rows, width), bf16)],
        [pltpu.VMEM((768, 2 * width), bf16)], flops=10 ** 9, moved=3 << 20)
    from_below = lax.ppermute(first_up, "head", up)
    from_above = lax.ppermute(first_down, "head", down)

    chunk = features // shards
    shapes = [((shards // 2, chunk, width), f32), ((shards // 2, chunk, width), bf16)]
    keep, send, part = run(
        near_products, (grad_out, first_cot, second_cot, attention, out_weight), shapes + [((rows, width), f32)],
        flops=4 * 10 ** 8, moved=1 << 20)
    keep, send, grad_attention, deltas = run(
        far_products, (opposite, attention, residue, out_weight, keep, send, part),
        shapes + [((rows, width), bf16), ((2, rows), f32)])
    half_sum = lax.ppermute(send, "seq", swap)
    pairs, = run(pair_sum, (keep, half_sum), [((shards // 2, chunk, width), bf16)],
                 [pltpu.VMEM((shards // 2, chunk, width), bf16), dma((PIECES,))], far_outs=(0,))
    groups = [list(range(core, shards, 2)) for core in range(2)]
    spread = lax.all_to_all(pairs, "seq", 0, 0, axis_index_groups=groups)

    dscores, to_next, to_prev, edge, send_up = run(
        backward,
        (queries, before, after, lse, grad_attention, deltas, second_up, from_below),
        [((4, 512, 256), bf16), ((256, 2 * width), bf16), ((256, 2 * width), bf16), ((768, 2 * width), bf16),
         ((rows, width), bf16)],
        [pltpu.VMEM((1536, 2 * width), f32)], flops=2 * 10 ** 9, moved=4 << 20)
    last_below = lax.ppermute(send_up, "head", up)
    grad_before = lax.ppermute(to_next, "seq", onward)
    grad_after = lax.ppermute(to_prev, "seq", back)
    grad_queries, own_grad, near_out = run(
        own_grads, (queries, mine, edge, lse, grad_attention, deltas, dscores, own_out, from_above),
        [((rows, width), bf16), ((rows, 2 * width), bf16), ((rows, width), f32)],
        [pltpu.VMEM((1536, 2 * width), f32), pltpu.VMEM((256, 2 * width), bf16), pltpu.VMEM((rows, width), bf16), dma((2,))],
        flops=3 * 10 ** 9, moved=6 << 20, far_outs=(0,))

    output, grad_keys, grad_values, grad_weight = run(
        finish,
        (near_out, last_below, own_grad, grad_before, grad_after, spread),
        [((rows, width), bf16)] * 3 + [((chunk, width), f32)],
        [pltpu.VMEM((rows, width), bf16)] * 3 + [pltpu.VMEM((chunk, width), f32)]
        + [pltpu.VMEM((shards // 2, chunk, width), bf16), dma((PIECES,)), dma((7,))],
        moved=4 << 20, far_args=(5,), far_outs=(0, 1, 2, 3))
    return output, grad_queries, grad_keys, grad_values, grad_weight


def solution(mesh):
    split = P("seq", "head")
    return jax.shard_map(
        local, mesh=mesh, in_specs=(split, split, split, P(None, "head"), split),
        out_specs=(split,) * 5, check_vma=False)
```
